32 devices in a mesh: pb: 8 (over y, x, core), ka: 4 (over z).
Axes of the slice: x: 2, y: 2, z: 4, core: 2. Of those that a mesh axis runs over, the one named last changes fastest.
Arguments:
- queries: bfloat16 [4096, 4096], P('pb'), may hold values from -6 to 6
- key_rows: bfloat16 [4096, 512], P(('pb', 'ka')), may hold values from -6 to 6
- values: bfloat16 [4096, 512], P(('pb', 'ka')), may hold values from -6 to 6
- attn_out: bfloat16 [4096, 4096], P(('pb', 'ka')), may hold values from -6 to 6
- grad_out: bfloat16 [4096, 4096], P('pb'), may hold values from -6 to 6
- log_sums: float32 [32, 4096], P(None, ('pb', 'ka')), may hold values from 3 to 7
- key_gain: float32 [512], replicated, may hold values from 0.25 to 1.75
- value_gain: float32 [512], replicated, may hold values from 0.25 to 1.75
- doc_ids: int32 [32], replicated, may hold values from 0 to 3, never falling along the last dimension, each value on 1 to 16 neighbouring positions
- tile_mask: int32 [32, 32], replicated, may hold values 0 or 1
- block_order: int32 [32], replicated, may hold values from 0 to 31, each once
Outputs:
- grad_queries: bfloat16 [4096, 4096], P(('pb', 'ka'))
- grad_keys: bfloat16 [4096, 512], P(('pb', 'ka'))
- grad_values: bfloat16 [4096, 512], P(('pb', 'ka'))
- grad_key_gain: float32 [512], replicated
- grad_value_gain: float32 [512], replicated
The draws below stay inside these ranges and needn't reach their ends.
Inputs may be any that keep to these rules, and one draw needn't show every extreme that they name: `doc_ids`: documents are numbered in sequence order; each spans 1 to 16 tiles, one exactly that many. `block_order`: each sequence tile once.
All inputs are finite; a program needn't handle non-finite values.
Results may differ from the reference program's by a relative error of at most 0.015.
Values may be sent and summed in bfloat16 or wider, within the bound.
No kernel may reach another device: no remote copies, remote signals or barrier semaphores. Data moves between devices by JAX's collectives and lax.ppermute only.
A program may use at most 192 MiB of HBM per device.

```python
import math
import jax
import jax.numpy as jnp
import numpy as np
from jax import lax

HEADS = 32
KV_HEADS = 4
HEAD_DIM = 128
TILE = 128
ROWS_DEV = 128
GROUP = 8
TOKENS = 4096
TILES = 32
N_KA = 4


def set_ends(values, key, smallest, largest):
    index_at = [jax.random.randint(jax.random.fold_in(key, axis), (), 0, length) for axis, length in enumerate(values.shape)]
    main_axis = values.shape.index(max(values.shape))
    neighbour = index_at[:main_axis] + [(index_at[main_axis] + 1) % values.shape[main_axis]] + index_at[main_axis + 1:]
    return values.at[tuple(index_at)].set(smallest).at[tuple(neighbour)].set(largest)


def block_scale(key, extent, split, low, high):
    gain, own = 1.0, jax.random.fold_in(key, 6)
    for axis_at, parts in split:
        heights = jnp.exp(jax.random.uniform(jax.random.fold_in(own, axis_at), (parts,), jnp.float32, low / len(split), high / len(split)))
        gain = gain * jnp.repeat(heights, extent[axis_at] // parts).reshape([-1 if axis == axis_at else 1 for axis in range(len(extent))])
    return gain


def split_up(number_of, total, limit, skew):
    loads = [(1 << 20) // math.isqrt(rank ** skew) + 1 for rank in range(2, number_of + 1)]
    surplus, holding = total - limit - (number_of - 1), [1] * (number_of - 1)
    while surplus > 0:
        movable = [i for i in range(number_of - 1) if holding[i] < limit]
        mass, remaining = sum([loads[i] for i in movable]), surplus
        for i in movable:
            addition = min(limit - holding[i], max(1, remaining * loads[i] // mass), surplus)
            holding[i] = holding[i] + addition
            surplus = surplus - addition
    return np.array([limit] + holding)


def ragged(stream_key, count, total, bound, slope):
    if count == 2:
        one = jax.random.randint(stream_key, (), max(1, total - bound), min(bound, total - 1) + 1)
        return jnp.stack([one, total - one])
    lengths = jnp.asarray(split_up(count, total, bound, slope), jnp.int32)
    pairs = (count - 1) // 2
    source_of, sink = lengths[1:1 + 2 * pairs:2], lengths[2:2 + 2 * pairs:2]
    slack = jnp.minimum(source_of - 1, bound - sink)
    passed = jax.random.randint(jax.random.fold_in(stream_key, 1), (pairs,), 0, 1 << 20) % (slack + 1)
    lengths = lengths.at[1:1 + 2 * pairs:2].set(source_of - passed).at[2:2 + 2 * pairs:2].set(sink + passed)
    return lengths[jax.random.permutation(jax.random.fold_in(stream_key, 2), count)]


def gaussian(own_key, dims, width, bound, shards=(), kind=jnp.bfloat16):
    factor_of = block_scale(own_key, dims, shards, -0.22, 0.18) if shards else 1.0
    values = jax.random.normal(own_key, dims, jnp.float32) * width * factor_of
    return jnp.minimum(jnp.maximum(values, -bound), bound).astype(kind)


def setup_inputs(seed: int = 0) -> dict:
    keys = jax.random.split(jax.random.key(seed), 12)
    queries = gaussian(keys[0], (TOKENS, HEADS * HEAD_DIM), 1.0, 6.0, ((0, 8),))
    key_rows = gaussian(keys[1], (TOKENS, KV_HEADS * HEAD_DIM), 1.0, 6.0, ((0, 32),))
    values = gaussian(keys[2], (TOKENS, KV_HEADS * HEAD_DIM), 1.0, 6.0, ((0, 32),))
    attn_out = gaussian(keys[3], (TOKENS, HEADS * HEAD_DIM), 1.0, 6.0, ((0, 32),))
    grad_out = gaussian(keys[4], (TOKENS, HEADS * HEAD_DIM), 1.0, 6.0, ((0, 8),))
    log_sums = jnp.clip(3.0 + 4.0 * jax.random.uniform(keys[5], (HEADS, TOKENS), jnp.float32) ** block_scale(keys[5], (HEADS, TOKENS), ((1, 32),), -0.2, 0.2), 3.0, 7.0)
    key_gain = jnp.clip(1.0 + 0.15 * jax.random.normal(keys[6], (KV_HEADS * HEAD_DIM,), jnp.float32), 0.25, 1.75)
    value_gain = jnp.clip(1.0 + 0.15 * jax.random.normal(keys[7], (KV_HEADS * HEAD_DIM,), jnp.float32), 0.25, 1.75)
    doc_ids = jnp.searchsorted(jnp.cumsum(ragged(keys[8], TILES // 8, TILES, TILES // 2, 2)), jnp.arange(TILES), side="right").astype(jnp.int32)
    tile_mask = set_ends((jax.random.randint(keys[9], (TILES, TILES), 0, 8) < 7).astype(jnp.int32), jax.random.fold_in(keys[9], 1), 0, 1)
    block_order = jax.random.permutation(keys[10], TILES).astype(jnp.int32)
    return dict(queries=queries, key_rows=key_rows, values=values, attn_out=attn_out, grad_out=grad_out, log_sums=log_sums, key_gain=key_gain, value_gain=value_gain, doc_ids=doc_ids, tile_mask=tile_mask, block_order=block_order)


def settle(value):
    return lax.optimization_barrier(value).astype(jnp.float32)


def add_rows(total, start, term):
    current = lax.dynamic_slice_in_dim(total, start, term.shape[0], 0)
    return lax.dynamic_update_slice_in_dim(total, current + term, start, 0)


def reference(queries, key_rows, values, attn_out, grad_out, log_sums, key_gain, value_gain, doc_ids, tile_mask, block_order):
    score_scale = HEAD_DIM ** -0.5
    feat_width = HEADS * HEAD_DIM
    kv_width = KV_HEADS * HEAD_DIM
    key_scaled = (key_rows.astype(jnp.float32) * key_gain).astype(jnp.bfloat16)
    value_scaled = (values.astype(jnp.float32) * value_gain).astype(jnp.bfloat16)
    products = grad_out.astype(jnp.float32) * attn_out.astype(jnp.float32)
    delta_rows = jnp.sum(products.reshape(TOKENS, HEADS, HEAD_DIM), axis=2).T
    tiles_block = ROWS_DEV // TILE
    offsets = jnp.arange(TILE, dtype=jnp.int32)
    loop_start = jnp.int32(0)
    loop_end = jnp.int32(TILES)

    def query_tile(query_at, totals):
        key_total, value_total, query_grads = totals
        seq_query = block_order[query_at]
        start_query = query_at * TILE
        query_tile_f = lax.dynamic_slice_in_dim(queries, start_query, TILE, 0).astype(jnp.float32).reshape(TILE, KV_HEADS, GROUP, HEAD_DIM)
        grad_tile = lax.dynamic_slice_in_dim(grad_out, start_query, TILE, 0).astype(jnp.float32).reshape(TILE, KV_HEADS, GROUP, HEAD_DIM)
        lse_tile = lax.dynamic_slice_in_dim(log_sums, start_query, TILE, 1).reshape(KV_HEADS, GROUP, TILE)
        delta_tile = lax.dynamic_slice_in_dim(delta_rows, start_query, TILE, 1).reshape(KV_HEADS, GROUP, TILE)
        query_pos = seq_query * TILE + offsets

        def key_tile(key_at, partial_value):
            seq_key = block_order[key_at]
            is_live = (tile_mask[seq_query, seq_key] == 1) & (doc_ids[seq_query] == doc_ids[seq_key]) & (seq_query >= seq_key)

            def accumulate(kept):
                key_parts, key_sum, value_sum = kept
                start_key = key_at * TILE
                key_tile_f = lax.dynamic_slice_in_dim(key_scaled, start_key, TILE, 0).astype(jnp.float32).reshape(TILE, KV_HEADS, HEAD_DIM)
                value_tile_f = lax.dynamic_slice_in_dim(value_scaled, start_key, TILE, 0).astype(jnp.float32).reshape(TILE, KV_HEADS, HEAD_DIM)
                key_pos = seq_key * TILE + offsets
                allowed = query_pos[:, None] >= key_pos[None, :]
                scores = jnp.einsum("ihgd,jhd->hgij", query_tile_f, key_tile_f) * score_scale
                weights = jnp.where(allowed, jnp.exp(scores - lse_tile[..., None]), 0.0)
                dweights = jnp.einsum("ihgd,jhd->hgij", grad_tile, value_tile_f)
                dscores = weights * (dweights - delta_tile[..., None])
                weights_low = settle(weights.astype(jnp.bfloat16))
                dscores_low = settle(dscores.astype(jnp.bfloat16))
                value_term = jnp.einsum("hgij,ihgd->jhd", weights_low, grad_tile).reshape(TILE, kv_width)
                key_term = (jnp.einsum("hgij,ihgd->jhd", dscores_low, query_tile_f) * score_scale).reshape(TILE, kv_width)
                query_term = (jnp.einsum("hgij,jhd->ihgd", dscores_low, key_tile_f) * score_scale).reshape(TILE, feat_width)
                key_set = (key_at // tiles_block) % N_KA
                key_parts = key_parts.at[key_set].add(query_term)
                key_sum = add_rows(key_sum, start_key, key_term)
                value_sum = add_rows(value_sum, start_key, value_term)
                return key_parts, key_sum, value_sum

            return lax.cond(is_live, accumulate, lambda kept: kept, partial_value)

        empty_parts = jnp.zeros((N_KA, TILE, feat_width), jnp.float32)
        key_parts, key_total, value_total = lax.fori_loop(loop_start, loop_end, key_tile, (empty_parts, key_total, value_total))
        rounded = jnp.sum(settle(key_parts.astype(jnp.bfloat16)), axis=0)
        query_grads = lax.dynamic_update_slice_in_dim(query_grads, rounded.astype(jnp.bfloat16), start_query, 0)
        return key_total, value_total, query_grads

    start_totals = (jnp.zeros((TOKENS, kv_width), jnp.float32), jnp.zeros((TOKENS, kv_width), jnp.float32), jnp.zeros((TOKENS, feat_width), jnp.bfloat16))
    key_total, value_total, grad_queries = lax.fori_loop(loop_start, loop_end, query_tile, start_totals)
    grad_keys = (key_total * key_gain).astype(jnp.bfloat16)
    grad_values = (value_total * value_gain).astype(jnp.bfloat16)
    grad_key_gain = jnp.sum(key_total * key_rows.astype(jnp.float32), axis=0)
    grad_value_gain = jnp.sum(value_total * values.astype(jnp.float32), axis=0)
    return grad_queries, grad_keys, grad_values, grad_key_gain, grad_value_gain
```

```python
import functools

import jax
import jax.numpy as jnp
from jax import lax
from jax.experimental import pallas as pl
from jax.experimental.pallas import tpu as pltpu
from jax.sharding import PartitionSpec as P

HEAD_DIM = 128
TILE = 128
SPARE = 16
LOG2E = 1.4426950408889634
VMEM = pltpu.VMEM
SMEM = pltpu.SMEM
F32 = jnp.float32
BF16 = jnp.bfloat16


def split_three(x):
    high = x.astype(BF16).astype(F32)
    rest = x - high
    middle = rest.astype(BF16).astype(F32)
    low = (rest - middle).astype(BF16).astype(F32)
    return high, middle, low


def head_rows(heads_dev):
    return -(-heads_dev // 8) * 8


def extra_rows(heads_dev):
    return -(-3 * head_rows(heads_dev) // 16) * 16


def prepare_kernel(dims, place_ref, key_ref, value_ref, attn_ref, grad_ref, lse_ref, *rest):
    count_ka, heads, heads_dev, share = dims
    outs, (lse_pad, delta_pad) = rest[:count_ka], rest[count_ka:]
    place_ka = place_ref[1]
    rows8 = head_rows(heads_dev)
    lanes = lax.broadcasted_iota(jnp.int32, (TILE, TILE), 1)
    columns = jnp.zeros((TILE, TILE), F32)
    for head in range(heads):
        part = pl.ds(head * HEAD_DIM, HEAD_DIM)
        products = grad_ref[:, part].astype(F32) * attn_ref[:, part].astype(F32)
        total = jnp.sum(products, axis=1, keepdims=True)
        columns = jnp.where(lanes == head, total, columns)
    delta_pad[...] = jnp.zeros_like(delta_pad)
    lse_pad[...] = jnp.zeros_like(lse_pad)
    delta_pad[:heads, :] = columns.T[:heads, :]
    lse_pad[:heads, :] = lse_ref[...]
    filler = extra_rows(heads_dev) - 3 * rows8
    for step in range(count_ka):
        target = lax.rem(place_ka + step, count_ka)
        kv_at = pl.ds(pl.multiple_of(target // share * HEAD_DIM, HEAD_DIM), HEAD_DIM)
        outs[step][:TILE, :HEAD_DIM] = key_ref[:, kv_at]
        outs[step][:TILE, HEAD_DIM:] = value_ref[:, kv_at]
        head_at = pl.ds(target * heads_dev, rows8)
        both = jnp.concatenate([lse_pad[head_at, :], delta_pad[head_at, :]], axis=1)
        terms = list(split_three(both))
        if filler:
            terms.append(jnp.zeros((filler, 2 * HEAD_DIM), F32))
        outs[step][TILE:, :] = jnp.concatenate(terms, axis=0).astype(BF16)


def own_heads_kernel(place_ref, queries_ref, grads_ref, out_ref):
    for number, ref in enumerate((queries_ref, grads_ref)):
        for head in range(ref.shape[1] // HEAD_DIM):
            part = pl.ds(head * HEAD_DIM, HEAD_DIM)
            tile = ref[:, part]
            out_ref[number, 0, part, :] = tile
            out_ref[2 + number, 0, part, :] = tile.T


def attention_kernel(dims, place_ref, order_ref, doc_ref, mask_ref, *rest):
    count_chip, count_ka, heads_dev, share, stage, steps = dims
    key_tiles = count_chip * count_ka
    if stage == 0:
        (key_gain_ref, value_gain_ref), rest = rest[:2], rest[2:]
    (heads_ref, stats_ref), rest = rest[:2], rest[2:]
    if stage != 1:
        blocks, rest = rest[:count_chip], rest[count_chip:]
    if stage == 0:
        (dq_out, keys, values, keys_t, key_sum, value_sum), rest = rest[:6], rest[6:]
    else:
        (keys, values, keys_t, key_start, value_start), rest = rest[:5], rest[5:]
    if stage == 1:
        dq_outs, rest = rest[:len(steps)], rest[len(steps):]
        (key_sum, value_sum), rest = rest[:2], rest[2:]
    if stage == 2:
        dq_back, rest = rest[0], rest[1:]
        dq_outs, rest = rest[:len(steps)], rest[len(steps):]
        kv_outs, rest = rest[:count_chip], rest[count_chip:]
        (key_sum, value_sum), rest = rest[:2], rest[2:]
    (lse_delta, weights_low, dscores_low, dq_turn, live_list, limit_list) = rest
    place_pb, place_ka = place_ref[0], place_ref[1]
    query_pb = place_pb if stage else place_pb ^ 1
    rows8 = head_rows(heads_dev)
    spare = extra_rows(heads_dev)
    score_scale = HEAD_DIM ** -0.5

    if stage == 0:
        kv_at = pl.ds(pl.multiple_of(place_ka // share * HEAD_DIM, HEAD_DIM), HEAD_DIM)
        key_gain = key_gain_ref[:, kv_at]
        value_gain = value_gain_ref[:, kv_at]
        for number in range(count_chip):
            for step in range(count_ka):
                part = pl.ds(step * TILE, TILE)
                local = number * count_ka + step
                key_tile = (blocks[number][part, :HEAD_DIM].astype(F32) * key_gain).astype(BF16)
                value_tile = (blocks[number][part, HEAD_DIM:].astype(F32) * value_gain).astype(BF16)
                keys[local] = key_tile
                values[local] = value_tile
                keys_t[local] = key_tile.T
        key_sum[...] = jnp.zeros_like(key_sum)
        value_sum[...] = jnp.zeros_like(value_sum)
    else:
        key_sum[...] = key_start[...]
        value_sum[...] = value_start[...]

    reach = (lax.broadcasted_iota(jnp.int32, (TILE, TILE), 1)
             - lax.broadcasted_iota(jnp.int32, (TILE, TILE), 0))
    reach = jnp.concatenate([reach, reach], axis=0)
    reach = jnp.concatenate([reach, reach], axis=1)
    lower = lax.broadcasted_iota(jnp.int32, (2 * TILE, 2 * TILE), 0) < TILE

    def query_step(turn_q, carry):
        step_q = jnp.int32(steps[0])
        for number, step in enumerate(steps):
            step_q = jnp.where(turn_q == number, step, step_q)
        tile_at = lax.rem(place_ka + step_q, count_ka)
        seq_q = order_ref[query_pb * count_ka + tile_at]
        doc_q = doc_ref[seq_q]

        def collect(local, count):
            number = local // count_ka
            step = lax.rem(local, count_ka)
            stored = ((place_pb ^ (2 * number)) * count_ka
                      + lax.rem(place_ka - step + count_ka, count_ka))
            seq_k = order_ref[stored]
            live = (mask_ref[seq_q, seq_k] == 1) & (doc_ref[seq_k] == doc_q) & (seq_q >= seq_k)
            live_list[count] = local
            limit_list[count] = jnp.where(seq_q == seq_k, 0, -TILE)
            return count + live.astype(jnp.int32)

        live_count = lax.fori_loop(0, key_tiles, collect, jnp.int32(0))
        live_list[live_count] = 0
        limit_list[live_count] = TILE

        slot = lax.rem(place_ka - tile_at + count_ka, count_ka)
        packed = stats_ref[pl.ds(pl.multiple_of(slot * spare, spare), spare), :].astype(F32)
        lse_delta[...] = (packed[:rows8] + packed[rows8:2 * rows8]) + packed[2 * rows8:3 * rows8]
        dq_turn[...] = jnp.zeros_like(dq_turn)

        def pair_step(at, carry):
            first, second = live_list[2 * at], live_list[2 * at + 1]
            limits = jnp.where(lower, limit_list[2 * at], limit_list[2 * at + 1])
            allowed = reach >= limits
            key_pair = jnp.concatenate([keys[first], keys[second]], axis=0)
            value_pair = jnp.concatenate([values[first], values[second]], axis=0)
            key_turn = jnp.concatenate([keys_t[first], keys_t[second]], axis=1)
            for head in range(0, heads_dev, 2):
                part = pl.ds(head * HEAD_DIM, 2 * HEAD_DIM)
                q_turn, o_turn = [
                    jnp.concatenate(
                        [heads_ref[kind, tile_at, pl.ds(at * HEAD_DIM, HEAD_DIM), :] for at in (head, head + 1)],
                        axis=1,
                    )
                    for kind in (2, 3)
                ]
                scores = jnp.dot(key_pair, q_turn, preferred_element_type=F32)
                dweights = jnp.dot(value_pair, o_turn, preferred_element_type=F32)
                lse_row = jnp.concatenate([lse_delta[at:at + 1, :TILE] for at in (head, head + 1)], axis=1)
                delta_row = jnp.concatenate([lse_delta[at:at + 1, TILE:] for at in (head, head + 1)], axis=1)
                weights = jnp.exp2(scores * (score_scale * LOG2E) - lse_row * LOG2E)
                weights = jnp.where(allowed, weights, 0.0)
                weights_low[:, part] = weights.astype(BF16)
                dscores_low[:, part] = (weights * (dweights - delta_row)).astype(BF16)
            value_term = jnp.dot(weights_low[...], heads_ref[1, tile_at], preferred_element_type=F32)
            key_term = jnp.dot(dscores_low[...], heads_ref[0, tile_at], preferred_element_type=F32)
            dq_turn[...] += jnp.dot(key_turn, dscores_low[...], preferred_element_type=F32)
            key_sum[first] += key_term[:TILE]
            value_sum[first] += value_term[:TILE]
            key_sum[second] += key_term[TILE:]
            value_sum[second] += value_term[TILE:]
            return carry

        lax.fori_loop(0, (live_count + 1) // 2, pair_step, 0)
        tile_grad = dq_turn[...] * score_scale
        if stage == 0:
            dq_out[tile_at] = tile_grad.astype(BF16)
            return carry
        if stage == 2:
            tile_grad = tile_grad + dq_back[tile_at].astype(F32)
        for number in range(len(steps)):
            @pl.when(turn_q == number)
            def _():
                dq_outs[number][...] = tile_grad.astype(dq_outs[number].dtype)
        return carry

    lax.fori_loop(0, len(steps), query_step, 0)
    if stage != 2:
        return

    key_gains = jnp.zeros((8, HEAD_DIM), F32)
    value_gains = jnp.zeros((8, HEAD_DIM), F32)
    for number in range(count_chip):
        for step in range(count_ka):
            part = pl.ds(step * TILE, TILE)
            local = number * count_ka + step
            key_total = key_sum[local] * score_scale
            value_total = value_sum[local]
            kv_outs[number][part, :HEAD_DIM] = key_total.astype(kv_outs[number].dtype)
            kv_outs[number][part, HEAD_DIM:] = value_total.astype(kv_outs[number].dtype)
            key_raw = blocks[number][part, :HEAD_DIM].astype(F32)
            value_raw = blocks[number][part, HEAD_DIM:].astype(F32)
            key_gains += jnp.sum((key_total * key_raw).reshape(TILE // 8, 8, HEAD_DIM), axis=0)
            value_gains += jnp.sum((value_total * value_raw).reshape(TILE // 8, 8, HEAD_DIM), axis=0)
    gains = jnp.concatenate([jnp.sum(key_gains, axis=0, keepdims=True),
                             jnp.sum(value_gains, axis=0, keepdims=True)], axis=1)
    packed = pack_gains(gains)
    for number in range(count_chip):
        kv_outs[number][count_ka * TILE:, :] = packed.astype(kv_outs[number].dtype)


def pack_gains(gains):
    rows = lax.broadcasted_iota(jnp.int32, (SPARE, gains.shape[1]), 0)
    high, middle, low = split_three(gains)
    packed = jnp.where(rows == 0, high, jnp.where(rows == 1, middle, low))
    return jnp.where(rows < 3, packed, 0.0)


def add_kernel(dims, place_ref, other_ref, *rest):
    count_ka, steps = dims
    parts, outs = rest[:len(steps)], rest[len(steps):]
    for number, step in enumerate(steps):
        tile_at = lax.rem(place_ref[1] + step, count_ka)
        outs[number][...] = (parts[number][...] + other_ref[tile_at].astype(F32)).astype(BF16)


def collect_kernel(dims, place_ref, key_gain_ref, value_gain_ref, *rest):
    count_chip, count_ka, share = dims
    parts, outs = rest[:count_chip], rest[count_chip:]
    kv_at = pl.ds(pl.multiple_of(place_ref[1] // share * HEAD_DIM, HEAD_DIM), HEAD_DIM)
    gain = jnp.concatenate([key_gain_ref[:, kv_at], value_gain_ref[:, kv_at]], axis=1)
    for step in range(count_ka):
        rows = pl.ds(step * TILE, TILE)
        total = parts[0][rows, :]
        for number in range(1, count_chip):
            total = total + parts[number][rows, :].astype(F32)
        if share == 1:
            total = total * gain
        outs[step][:TILE, :] = total.astype(outs[step].dtype)
    spare = pl.ds(count_ka * TILE, SPARE)
    total = parts[0][spare, :]
    for number in range(1, count_chip):
        total = total + parts[number][spare, :].astype(F32)
    packed = pack_gains(jnp.sum(total, axis=0, keepdims=True))
    for step in range(count_ka):
        outs[step][TILE:, :] = packed.astype(outs[step].dtype)


def turn_kernel(*refs):
    half = len(refs) // 2
    for source, target in zip(refs[:half], refs[half:]):
        for head in range(source.shape[1] // HEAD_DIM):
            part = pl.ds(head * HEAD_DIM, HEAD_DIM)
            target[:, part] = source[:, part].T


def place_kernel(dims, place_ref, *rest):
    count_ka, heads_dev, late = dims
    dq_parts, rest = rest[:count_ka], rest[count_ka:]
    dq_out, rest = rest[0], rest[1:]
    turned, sems = rest[:-1], rest[-1]
    width = heads_dev * HEAD_DIM
    copies = []
    for step in tuple(at for at in range(count_ka) if at not in late) + late:
        source = lax.rem(place_ref[1] - step + count_ka, count_ka)
        columns = pl.ds(pl.multiple_of(source * width, HEAD_DIM), width)
        piece = dq_parts[step]
        if step in late:
            turn_kernel(piece, turned[late.index(step)])
            piece = turned[late.index(step)]
        copies.append(pltpu.make_async_copy(piece, dq_out.at[:, columns], sems.at[step]))
        copies[-1].start()
    for copy in copies:
        copy.wait()


def finish_kernel(dims, place_ref, key_gain_ref, value_gain_ref, *rest):
    count_ka, share = dims
    pieces, rest = rest[:count_ka], rest[count_ka:]
    dk_out, dv_out, gains_out, sums = rest
    place_ka = place_ref[1]
    sums[...] = jnp.zeros_like(sums)
    for step in range(count_ka):
        source = lax.rem(place_ka + step, count_ka)
        sums[source // share] += pieces[step][...].astype(F32)
    for head in range(count_ka // share):
        part = pl.ds(head * HEAD_DIM, HEAD_DIM)
        key_total = sums[head, :TILE, :HEAD_DIM]
        value_total = sums[head, :TILE, HEAD_DIM:]
        if share > 1:
            key_total = key_total * key_gain_ref[:, part]
            value_total = value_total * value_gain_ref[:, part]
        dk_out[:, part] = key_total.astype(BF16)
        dv_out[:, part] = value_total.astype(BF16)
        gains = jnp.sum(sums[head, TILE:, :], axis=0, keepdims=True)
        gains_out[0:1, part] = gains[:, :HEAD_DIM]
        gains_out[1:2, part] = gains[:, HEAD_DIM:]


def in_vmem(count):
    return [pl.BlockSpec(memory_space=VMEM)] * count


def in_smem(count):
    return [pl.BlockSpec(memory_space=SMEM)] * count


def anywhere(count):
    return [pl.BlockSpec(memory_space=pl.ANY)] * count


def params(mib):
    return pltpu.CompilerParams(vmem_limit_bytes=mib * 1024 * 1024)


def shards(
    queries,
    key_rows,
    values,
    attn_out,
    grad_out,
    log_sums,
    key_gain,
    value_gain,
    doc_ids,
    tile_mask,
    block_order,
):
    count_pb = lax.axis_size("pb")
    count_ka = lax.axis_size("ka")
    place_pb = lax.axis_index("pb")
    place_ka = lax.axis_index("ka")
    rows_dev = key_rows.shape[0]
    query_rows = queries.shape[0]
    heads = log_sums.shape[0]
    feat_width = queries.shape[1]
    kv_heads = key_rows.shape[1] // HEAD_DIM
    heads_dev = heads // count_ka
    share = count_ka // kv_heads
    assert rows_dev == TILE and share * kv_heads == count_ka and count_pb & (count_pb - 1) == 0
    width = heads_dev * HEAD_DIM
    place = jnp.stack([place_pb, place_ka]).astype(jnp.int32)
    key_gain = key_gain.reshape(1, -1)
    value_gain = value_gain.reshape(1, -1)

    spare = extra_rows(heads_dev)
    count_chip = count_pb // 2

    def swap(array, number):
        return lax.ppermute(array, "pb", [(at, at ^ number) for at in range(count_pb)])

    def turn(array, step):
        return lax.ppermute(array, "ka", [(at, (at + step) % count_ka) for at in range(count_ka)])

    sends = pl.pallas_call(
        functools.partial(prepare_kernel, (count_ka, heads, heads_dev, share)),
        grid_spec=pltpu.PrefetchScalarGridSpec(
            num_scalar_prefetch=1,
            grid=(1,),
            in_specs=[
                pl.BlockSpec((rows_dev, key_rows.shape[1]), lambda i, s: (0, 0)),
                pl.BlockSpec((rows_dev, key_rows.shape[1]), lambda i, s: (0, 0)),
                pl.BlockSpec((rows_dev, feat_width), lambda i, s: (0, 0)),
                pl.BlockSpec((rows_dev, feat_width), lambda i, s: (s[1], 0)),
                pl.BlockSpec((heads, rows_dev), lambda i, s: (0, 0)),
            ],
            out_specs=[pl.BlockSpec((TILE + spare, 2 * HEAD_DIM), lambda i, s: (0, 0))] * count_ka,
            scratch_shapes=[VMEM((heads + 8, TILE), F32)] * 2,
        ),
        out_shape=[jax.ShapeDtypeStruct((TILE + spare, 2 * HEAD_DIM), BF16)] * count_ka,
        compiler_params=params(57),
        name="prepare",
    )(place, key_rows, values, attn_out, grad_out, log_sums)
    messages = [sends[0]] + [turn(sends[step], step) for step in range(1, count_ka)]

    later_place, _ = lax.optimization_barrier((place, sends[0]))
    own_queries = pl.pallas_call(
        own_heads_kernel,
        grid_spec=pltpu.PrefetchScalarGridSpec(
            num_scalar_prefetch=1,
            grid=(count_ka,),
            in_specs=[pl.BlockSpec((TILE, width), lambda i, s: (i, s[1]))] * 2,
            out_specs=pl.BlockSpec((4, 1, width, HEAD_DIM), lambda i, s: (0, i, 0, 0)),
        ),
        out_shape=jax.ShapeDtypeStruct((4, count_ka, width, HEAD_DIM), BF16),
        compiler_params=params(60),
        cost_estimate=pl.CostEstimate(flops=0, bytes_accessed=12 * query_rows * width, transcendentals=0),
        name="own_heads",
    )(later_place, queries, grad_out)
    messages, own_queries = lax.optimization_barrier((messages, own_queries))
    own_block = jnp.concatenate([message[:TILE] for message in messages], axis=0)
    own_stats = jnp.concatenate([message[TILE:] for message in messages], axis=0)
    blocks = [own_block] + [swap(own_block, 2 * number) for number in range(1, count_chip)]
    other_stats = swap(own_stats, 1)
    other_queries = swap(own_queries, 1)

    key_tiles = count_chip * count_ka
    sum_shape = jax.ShapeDtypeStruct((key_tiles, TILE, HEAD_DIM), F32)
    key_shape = jax.ShapeDtypeStruct((key_tiles, TILE, HEAD_DIM), BF16)
    kv_shape = (query_rows + SPARE, 2 * HEAD_DIM)
    work = [
        VMEM((head_rows(heads_dev), 2 * TILE), F32),
        VMEM((2 * TILE, width), BF16),
        VMEM((2 * TILE, width), BF16),
        VMEM((HEAD_DIM, width), F32),
        SMEM((key_tiles + 2,), jnp.int32),
        SMEM((key_tiles + 2,), jnp.int32),
    ]
    half = count_ka // 2
    early = (half, 0)
    late = tuple(step for step in range(1, count_ka) if step != half)
    scalars = (place, block_order, doc_ids, tile_mask)

    def attend(stage, steps, outs, scratch, *operands):
        dims = (count_chip, count_ka, heads_dev, share, stage, steps)
        pairs = len(steps) * key_tiles
        return pl.pallas_call(
            functools.partial(attention_kernel, dims),
            in_specs=in_smem(4) + in_vmem(len(operands)),
            out_specs=in_vmem(len(outs)),
            out_shape=outs,
            scratch_shapes=scratch + work,
            compiler_params=params(14 + key_tiles // 2),
            cost_estimate=pl.CostEstimate(
                flops=10 * pairs * TILE * TILE * width, bytes_accessed=1 << 22, transcendentals=0
            ),
            name=("attention_other", "attention_early", "attention_late")[stage],
        )(*scalars, *operands)

    part_shape = jax.ShapeDtypeStruct((HEAD_DIM, width), F32)
    full_shape = jax.ShapeDtypeStruct((HEAD_DIM, width), BF16)
    dq_other, *state = attend(
        0, tuple(range(count_ka)),
        [jax.ShapeDtypeStruct((count_ka, HEAD_DIM, width), BF16)] + [key_shape] * 3 + [sum_shape] * 2,
        [], key_gain, value_gain, other_queries, other_stats, *blocks,
    )
    dq_back = swap(dq_other, 1)
    keys, sums = state[:3], state[3:]
    *dq_early, key_sum, value_sum = attend(
        1, early, [part_shape] * len(early) + [sum_shape] * 2, [],
        own_queries, own_stats, *keys, *sums,
    )
    added = pl.pallas_call(
        functools.partial(add_kernel, (count_ka, early)),
        in_specs=in_smem(1) + in_vmem(1 + len(early)),
        out_specs=in_vmem(len(early)),
        out_shape=[full_shape] * len(early),
        compiler_params=params(16),
        name="add_queries",
    )(place, dq_back, *dq_early)
    dq_parts = [None] * count_ka
    added = list(added)
    late_stats, added[-1] = lax.optimization_barrier((own_stats, added[-1]))
    dq_parts[half], dq_parts[0] = turn(added[0], half), added[1]
    results = attend(
        2, late,
        [full_shape] * len(late) + [jax.ShapeDtypeStruct(kv_shape, F32)]
        + [jax.ShapeDtypeStruct(kv_shape, BF16)] * (count_chip - 1),
        [VMEM(sum_shape.shape, F32)] * 2,
        own_queries, late_stats, *blocks, *keys, key_sum, value_sum, dq_back,
    )
    dq_late, kv_own = results[:len(late)], results[len(late):]
    kv_own = list(kv_own)
    kv_own[-1], dq_parts[half] = lax.optimization_barrier((kv_own[-1], dq_parts[half]))
    kv_parts = [kv_own[0]] + [swap(kv_own[number], 2 * number) for number in range(1, count_chip)]
    for number, step in enumerate(late):
        dq_parts[step] = turn(dq_late[number], step)

    piece_type = BF16 if share == 1 else F32
    piece_shape = (TILE + SPARE, 2 * HEAD_DIM)
    totals = pl.pallas_call(
        functools.partial(collect_kernel, (count_chip, count_ka, share)),
        in_specs=in_smem(1) + in_vmem(2 + count_chip),
        out_specs=in_vmem(count_ka),
        out_shape=[jax.ShapeDtypeStruct(piece_shape, piece_type)] * count_ka,
        compiler_params=params(24),
        name="collect",
    )(place, key_gain, value_gain, *kv_parts)
    pieces = [totals[0]] + [turn(totals[step], -step) for step in range(1, count_ka)]

    grad_keys, grad_values, gains = pl.pallas_call(
        functools.partial(finish_kernel, (count_ka, share)),
        in_specs=in_smem(1) + in_vmem(2 + count_ka),
        out_specs=in_vmem(3),
        out_shape=[
            jax.ShapeDtypeStruct(key_rows.shape, BF16),
            jax.ShapeDtypeStruct(key_rows.shape, BF16),
            jax.ShapeDtypeStruct((2, key_rows.shape[1]), F32),
        ],
        scratch_shapes=[VMEM((kv_heads, TILE + SPARE, 2 * HEAD_DIM), F32)],
        compiler_params=params(16),
        name="finish",
    )(place, key_gain, value_gain, *pieces)
    gains = gains + swap(gains, 1)
    first = (0, half)
    turned = pl.pallas_call(
        turn_kernel,
        in_specs=in_vmem(len(first)),
        out_specs=in_vmem(len(first)),
        out_shape=[full_shape] * len(first),
        compiler_params=params(8),
        cost_estimate=pl.CostEstimate(flops=0, bytes_accessed=1 << 22, transcendentals=0),
        name="turn_queries",
    )(*[dq_parts[step] for step in first])
    for number, step in enumerate(first):
        dq_parts[step] = turned[number]
    grad_queries = pl.pallas_call(
        functools.partial(place_kernel, (count_ka, heads_dev, late)),
        in_specs=in_smem(1) + in_vmem(count_ka),
        out_specs=pl.BlockSpec(memory_space=pl.ANY),
        out_shape=jax.ShapeDtypeStruct((rows_dev, feat_width), BF16),
        scratch_shapes=[VMEM((TILE, width), BF16)] * len(late) + [pltpu.SemaphoreType.DMA((count_ka,))],
        compiler_params=params(16),
        cost_estimate=pl.CostEstimate(flops=0, bytes_accessed=4 * rows_dev * feat_width, transcendentals=0),
        name="place_queries",
    )(place, *dq_parts)
    return grad_queries, grad_keys, grad_values, gains[0], gains[1]


def solution(mesh):
    placed = (
        P("pb", None),
        P(("pb", "ka"), None),
        P(("pb", "ka"), None),
        P(("pb", "ka"), None),
        P("pb", None),
        P(None, ("pb", "ka")),
        P(),
        P(),
        P(),
        P(),
        P(),
    )
    return jax.shard_map(
        shards,
        mesh=mesh,
        in_specs=placed,
        out_specs=(P(("pb", "ka"), None), P(("pb", "ka"), None), P(("pb", "ka"), None), P(), P()),
        check_vma=False,
    )
```

```python
import functools

import jax
import jax.numpy as jnp
from jax import lax
from jax.experimental import pallas as pl
from jax.experimental.pallas import tpu as pltpu
from jax.sharding import PartitionSpec as P

HEAD_DIM = 128
TILE = 128
SPARE = 16
LOG2E = 1.4426950408889634
ENTRY = 8
LAST_DIMS = (((1,), (1,)), ((), ()))
VMEM = pltpu.VMEM
SMEM = pltpu.SMEM
F32 = jnp.float32
BF16 = jnp.bfloat16


def split_three(x):
    high = x.astype(BF16).astype(F32)
    rest = x - high
    middle = rest.astype(BF16).astype(F32)
    low = (rest - middle).astype(BF16).astype(F32)
    return high, middle, low


def head_rows(heads_dev):
    return -(-heads_dev // 8) * 8


def extra_rows(heads_dev):
    return -(-3 * head_rows(heads_dev) // 16) * 16


def prepare_kernel(dims, place_ref, key_ref, value_ref, attn_ref, grad_ref, lse_ref, *rest):
    count_ka, heads, heads_dev, share = dims
    outs, (lse_pad, delta_pad) = rest[:count_ka], rest[count_ka:]
    place_ka = place_ref[1]
    rows8 = head_rows(heads_dev)
    lanes = lax.broadcasted_iota(jnp.int32, (TILE, TILE), 1)
    columns = jnp.zeros((TILE, TILE), F32)
    for head in range(heads):
        part = pl.ds(head * HEAD_DIM, HEAD_DIM)
        products = grad_ref[:, part].astype(F32) * attn_ref[:, part].astype(F32)
        total = jnp.sum(products, axis=1, keepdims=True)
        columns = jnp.where(lanes == head, total, columns)
    delta_pad[...] = jnp.zeros_like(delta_pad)
    lse_pad[...] = jnp.zeros_like(lse_pad)
    delta_pad[:heads, :] = columns.T[:heads, :]
    lse_pad[:heads, :] = lse_ref[...]
    filler = extra_rows(heads_dev) - 3 * rows8
    for step in range(count_ka):
        target = lax.rem(place_ka + step, count_ka)
        kv_at = pl.ds(pl.multiple_of(target // share * HEAD_DIM, HEAD_DIM), HEAD_DIM)
        outs[step][:TILE, :HEAD_DIM] = key_ref[:, kv_at]
        outs[step][:TILE, HEAD_DIM:] = value_ref[:, kv_at]
        head_at = pl.ds(target * heads_dev, rows8)
        both = jnp.concatenate([lse_pad[head_at, :], delta_pad[head_at, :]], axis=1)
        terms = list(split_three(both))
        if filler:
            terms.append(jnp.zeros((filler, 2 * HEAD_DIM), F32))
        outs[step][TILE:, :] = jnp.concatenate(terms, axis=0).astype(BF16)


def own_heads_kernel(place_ref, queries_ref, grads_ref, out_ref):
    for number, ref in enumerate((queries_ref, grads_ref)):
        for head in range(ref.shape[1] // HEAD_DIM):
            part = pl.ds(head * HEAD_DIM, HEAD_DIM)
            out_ref[number, 0, part, :] = ref[:, part]


def places():
    return lax.axis_index("pb"), lax.axis_index("ka")


def plan_kernel(dims, order_ref, doc_ref, mask_ref, *rest):
    count_chip, count_ka, stages = dims
    tables, (live_list, limit_list) = rest[:len(stages)], rest[len(stages):]
    key_tiles = count_chip * count_ka
    place_pb, place_ka = places()
    for table, (other, steps) in zip(tables, stages):
        query_pb = place_pb ^ other

        def query_step(turn_q, chunks, table=table, query_pb=query_pb, steps=steps):
            step_q = jnp.int32(steps[0])
            for number, step in enumerate(steps):
                step_q = jnp.where(turn_q == number, step, step_q)
            tile_at = lax.rem(place_ka + step_q, count_ka)
            seq_q = order_ref[query_pb * count_ka + tile_at]
            doc_q = doc_ref[seq_q]

            def collect(number, count):
                for step in range(count_ka):
                    stored = (place_pb ^ (2 * number)) * count_ka + lax.rem(
                        place_ka - step + count_ka, count_ka
                    )
                    seq_k = order_ref[stored]
                    live = (mask_ref[seq_q, seq_k] == 1) & (doc_ref[seq_k] == doc_q) & (seq_q >= seq_k)
                    live_list[count] = number * count_ka + step
                    limit_list[count] = jnp.where(seq_q == seq_k, 0, -TILE)
                    count = count + live.astype(jnp.int32)
                return count

            count = lax.fori_loop(0, count_chip, collect, jnp.int32(0))
            live_list[count] = 0
            limit_list[count] = TILE
            pairs = (count + 1) // 2

            def write(at, carry):
                base = ENTRY * (chunks + at + 1)
                table[base] = turn_q
                table[base + 1] = tile_at
                table[base + 2] = live_list[2 * at]
                table[base + 3] = live_list[2 * at + 1]
                table[base + 4] = limit_list[2 * at]
                table[base + 5] = limit_list[2 * at + 1]
                return carry

            lax.fori_loop(0, pairs, write, 0)
            return chunks + pairs

        table[0] = lax.fori_loop(0, len(steps), query_step, jnp.int32(0))


def attention_kernel(dims, table_ref, *rest):
    count_chip, count_ka, heads_dev, share, stage, steps = dims
    if stage == 0:
        (key_gain_ref, value_gain_ref), rest = rest[:2], rest[2:]
    (heads_ref, stats_ref), rest = rest[:2], rest[2:]
    if stage != 1:
        blocks, rest = rest[:count_chip], rest[count_chip:]
    if stage == 0:
        (dq_out, keys, values, keys_t, key_sum, value_sum), rest = rest[:6], rest[6:]
    else:
        (keys, values, keys_t, key_start, value_start), rest = rest[:5], rest[5:]
    if stage == 1:
        dq_outs, rest = rest[:len(steps)], rest[len(steps):]
        (key_sum, value_sum), rest = rest[:2], rest[2:]
    if stage == 2:
        dq_back, rest = rest[0], rest[1:]
        dq_outs, rest = rest[:len(steps)], rest[len(steps):]
        kv_outs, rest = rest[:count_chip], rest[count_chip:]
        (key_sum, value_sum), rest = rest[:2], rest[2:]
    lse_delta, weights_low, dscores_low, dq_sum = rest
    _, place_ka = places()
    rows8 = head_rows(heads_dev)
    spare = extra_rows(heads_dev)
    score_scale = HEAD_DIM ** -0.5

    if stage == 0:
        kv_at = pl.ds(pl.multiple_of(place_ka // share * HEAD_DIM, HEAD_DIM), HEAD_DIM)
        key_gain = key_gain_ref[:, kv_at]
        value_gain = value_gain_ref[:, kv_at]
        for number in range(count_chip):
            for step in range(count_ka):
                part = pl.ds(step * TILE, TILE)
                local = number * count_ka + step
                key_tile = (blocks[number][part, :HEAD_DIM].astype(F32) * key_gain).astype(BF16)
                value_tile = (blocks[number][part, HEAD_DIM:].astype(F32) * value_gain).astype(BF16)
                keys[local] = key_tile
                values[local] = value_tile
                keys_t[local] = key_tile.T
        key_sum[...] = jnp.zeros_like(key_sum)
        value_sum[...] = jnp.zeros_like(value_sum)
    else:
        key_sum[...] = key_start[...]
        value_sum[...] = value_start[...]

    reach = (lax.broadcasted_iota(jnp.int32, (TILE, TILE), 1)
             - lax.broadcasted_iota(jnp.int32, (TILE, TILE), 0))
    reach = jnp.concatenate([reach, reach], axis=0)
    reach = jnp.concatenate([reach, reach], axis=1)
    lower = lax.broadcasted_iota(jnp.int32, (2 * TILE, 2 * TILE), 0) < TILE

    tiles = [lax.rem(place_ka + step, count_ka) for step in steps]
    for number, step in enumerate(steps):
        slot = count_ka - step if step else 0
        packed = stats_ref[pl.ds(slot * spare, spare), :].astype(F32)
        lse_delta[number] = (packed[:rows8] + packed[rows8:2 * rows8]) + packed[2 * rows8:3 * rows8]
    dq_sum[...] = jnp.zeros_like(dq_sum)

    def chunk_step(at, carry):
        base = ENTRY * (at + 1)
        turn_q, tile_at = table_ref[base], table_ref[base + 1]
        first, second = table_ref[base + 2], table_ref[base + 3]
        limits = jnp.where(lower, table_ref[base + 4], table_ref[base + 5])
        allowed = reach >= limits
        key_pair = jnp.concatenate([keys[first], keys[second]], axis=0)
        value_pair = jnp.concatenate([values[first], values[second]], axis=0)
        key_turn = jnp.concatenate([keys_t[first], keys_t[second]], axis=1)
        for head in range(0, heads_dev, 2):
            part = pl.ds(head * HEAD_DIM, 2 * HEAD_DIM)
            scores = lax.dot_general(
                key_pair, heads_ref[0, tile_at, part, :], LAST_DIMS, preferred_element_type=F32
            )
            dweights = lax.dot_general(
                value_pair, heads_ref[1, tile_at, part, :], LAST_DIMS, preferred_element_type=F32
            )
            lse_row, delta_row = [
                jnp.concatenate(
                    [lse_delta[turn_q, at_head:at_head + 1, lanes] for at_head in (head, head + 1)], axis=1
                )
                for lanes in (slice(0, TILE), slice(TILE, 2 * TILE))
            ]
            weights = jnp.exp2(scores * (score_scale * LOG2E) - lse_row * LOG2E)
            weights = jnp.where(allowed, weights, 0.0)
            weights_low[:, part] = weights.astype(BF16)
            dscores_low[:, part] = (weights * (dweights - delta_row)).astype(BF16)
        value_term = jnp.dot(weights_low[...], heads_ref[1, tile_at], preferred_element_type=F32)
        key_term = jnp.dot(dscores_low[...], heads_ref[0, tile_at], preferred_element_type=F32)
        dq_sum[turn_q] += jnp.dot(key_turn, dscores_low[...], preferred_element_type=F32)
        key_sum[first] += key_term[:TILE]
        value_sum[first] += value_term[:TILE]
        key_sum[second] += key_term[TILE:]
        value_sum[second] += value_term[TILE:]
        return carry

    lax.fori_loop(0, table_ref[0], chunk_step, 0)
    for number, tile_at in enumerate(tiles):
        tile_grad = dq_sum[number] * score_scale
        if stage == 0:
            dq_out[tile_at] = tile_grad.astype(BF16)
        else:
            if stage == 2:
                tile_grad = tile_grad + dq_back[tile_at].astype(F32)
            dq_outs[number][...] = tile_grad.astype(dq_outs[number].dtype)
    if stage != 2:
        return

    key_gains = jnp.zeros((8, HEAD_DIM), F32)
    value_gains = jnp.zeros((8, HEAD_DIM), F32)
    for number in range(count_chip):
        for step in range(count_ka):
            part = pl.ds(step * TILE, TILE)
            local = number * count_ka + step
            key_total = key_sum[local] * score_scale
            value_total = value_sum[local]
            kv_outs[number][part, :HEAD_DIM] = key_total.astype(kv_outs[number].dtype)
            kv_outs[number][part, HEAD_DIM:] = value_total.astype(kv_outs[number].dtype)
            key_raw = blocks[number][part, :HEAD_DIM].astype(F32)
            value_raw = blocks[number][part, HEAD_DIM:].astype(F32)
            key_gains += jnp.sum((key_total * key_raw).reshape(TILE // 8, 8, HEAD_DIM), axis=0)
            value_gains += jnp.sum((value_total * value_raw).reshape(TILE // 8, 8, HEAD_DIM), axis=0)
    gains = jnp.concatenate([jnp.sum(key_gains, axis=0, keepdims=True),
                             jnp.sum(value_gains, axis=0, keepdims=True)], axis=1)
    packed = pack_gains(gains)
    for number in range(count_chip):
        kv_outs[number][count_ka * TILE:, :] = packed.astype(kv_outs[number].dtype)


def pack_gains(gains):
    rows = lax.broadcasted_iota(jnp.int32, (SPARE, gains.shape[1]), 0)
    high, middle, low = split_three(gains)
    packed = jnp.where(rows == 0, high, jnp.where(rows == 1, middle, low))
    return jnp.where(rows < 3, packed, 0.0)


def add_kernel(dims, other_ref, *rest):
    count_ka, steps = dims
    parts, outs = rest[:len(steps)], rest[len(steps):]
    for number, step in enumerate(steps):
        tile_at = lax.rem(places()[1] + step, count_ka)
        outs[number][...] = (parts[number][...] + other_ref[tile_at].astype(F32)).astype(BF16)


def collect_kernel(dims, key_gain_ref, value_gain_ref, *rest):
    count_chip, count_ka, share = dims
    parts, outs = rest[:count_chip], rest[count_chip:]
    kv_at = pl.ds(pl.multiple_of(places()[1] // share * HEAD_DIM, HEAD_DIM), HEAD_DIM)
    gain = jnp.concatenate([key_gain_ref[:, kv_at], value_gain_ref[:, kv_at]], axis=1)
    for step in range(count_ka):
        rows = pl.ds(step * TILE, TILE)
        total = parts[0][rows, :]
        for number in range(1, count_chip):
            total = total + parts[number][rows, :].astype(F32)
        if share == 1:
            total = total * gain
        outs[step][:TILE, :] = total.astype(outs[step].dtype)
    spare = pl.ds(count_ka * TILE, SPARE)
    total = parts[0][spare, :]
    for number in range(1, count_chip):
        total = total + parts[number][spare, :].astype(F32)
    packed = pack_gains(jnp.sum(total, axis=0, keepdims=True))
    for step in range(count_ka):
        outs[step][TILE:, :] = packed.astype(outs[step].dtype)


def turn_kernel(*refs):
    half = len(refs) // 2
    for source, target in zip(refs[:half], refs[half:]):
        for head in range(source.shape[1] // HEAD_DIM):
            part = pl.ds(head * HEAD_DIM, HEAD_DIM)
            target[:, part] = source[:, part].T


def place_kernel(dims, *rest):
    count_ka, heads_dev, late = dims
    dq_parts, rest = rest[:count_ka], rest[count_ka:]
    dq_out, rest = rest[0], rest[1:]
    turned, sems = rest[:-1], rest[-1]
    width = heads_dev * HEAD_DIM
    copies = []
    for step in tuple(at for at in range(count_ka) if at not in late) + late:
        source = lax.rem(places()[1] - step + count_ka, count_ka)
        columns = pl.ds(pl.multiple_of(source * width, HEAD_DIM), width)
        piece = dq_parts[step]
        if step in late:
            turn_kernel(piece, turned[late.index(step)])
            piece = turned[late.index(step)]
        copies.append(pltpu.make_async_copy(piece, dq_out.at[:, columns], sems.at[step]))
        copies[-1].start()
    for copy in copies:
        copy.wait()


def finish_kernel(dims, key_gain_ref, value_gain_ref, *rest):
    count_ka, share = dims
    pieces, rest = rest[:count_ka], rest[count_ka:]
    dk_out, dv_out, gains_out, sums = rest
    _, place_ka = places()
    sums[...] = jnp.zeros_like(sums)
    for step in range(count_ka):
        source = lax.rem(place_ka + step, count_ka)
        sums[source // share] += pieces[step][...].astype(F32)
    for head in range(count_ka // share):
        part = pl.ds(head * HEAD_DIM, HEAD_DIM)
        key_total = sums[head, :TILE, :HEAD_DIM]
        value_total = sums[head, :TILE, HEAD_DIM:]
        if share > 1:
            key_total = key_total * key_gain_ref[:, part]
            value_total = value_total * value_gain_ref[:, part]
        dk_out[:, part] = key_total.astype(BF16)
        dv_out[:, part] = value_total.astype(BF16)
        gains = jnp.sum(sums[head, TILE:, :], axis=0, keepdims=True)
        gains_out[0:1, part] = gains[:, :HEAD_DIM]
        gains_out[1:2, part] = gains[:, HEAD_DIM:]


def in_vmem(count):
    return [pl.BlockSpec(memory_space=VMEM)] * count


def in_smem(count):
    return [pl.BlockSpec(memory_space=SMEM)] * count


def anywhere(count):
    return [pl.BlockSpec(memory_space=pl.ANY)] * count


def params(mib):
    return pltpu.CompilerParams(vmem_limit_bytes=mib * 1024 * 1024)


def shards(
    queries,
    key_rows,
    values,
    attn_out,
    grad_out,
    log_sums,
    key_gain,
    value_gain,
    doc_ids,
    tile_mask,
    block_order,
):
    count_pb = lax.axis_size("pb")
    count_ka = lax.axis_size("ka")
    place_pb = lax.axis_index("pb")
    place_ka = lax.axis_index("ka")
    rows_dev = key_rows.shape[0]
    query_rows = queries.shape[0]
    heads = log_sums.shape[0]
    feat_width = queries.shape[1]
    kv_heads = key_rows.shape[1] // HEAD_DIM
    heads_dev = heads // count_ka
    share = count_ka // kv_heads
    assert rows_dev == TILE and share * kv_heads == count_ka and count_pb & (count_pb - 1) == 0
    width = heads_dev * HEAD_DIM
    place = jnp.stack([place_pb, place_ka]).astype(jnp.int32)
    key_gain = key_gain.reshape(1, -1)
    value_gain = value_gain.reshape(1, -1)

    spare = extra_rows(heads_dev)
    count_chip = count_pb // 2

    def swap(array, number):
        return lax.ppermute(array, "pb", [(at, at ^ number) for at in range(count_pb)])

    def turn(array, step):
        return lax.ppermute(array, "ka", [(at, (at + step) % count_ka) for at in range(count_ka)])

    sends = pl.pallas_call(
        functools.partial(prepare_kernel, (count_ka, heads, heads_dev, share)),
        grid_spec=pltpu.PrefetchScalarGridSpec(
            num_scalar_prefetch=1,
            grid=(1,),
            in_specs=[
                pl.BlockSpec((rows_dev, key_rows.shape[1]), lambda i, s: (0, 0)),
                pl.BlockSpec((rows_dev, key_rows.shape[1]), lambda i, s: (0, 0)),
                pl.BlockSpec((rows_dev, feat_width), lambda i, s: (0, 0)),
                pl.BlockSpec((rows_dev, feat_width), lambda i, s: (s[1], 0)),
                pl.BlockSpec((heads, rows_dev), lambda i, s: (0, 0)),
            ],
            out_specs=[pl.BlockSpec((TILE + spare, 2 * HEAD_DIM), lambda i, s: (0, 0))] * count_ka,
            scratch_shapes=[VMEM((heads + 8, TILE), F32)] * 2,
        ),
        out_shape=[jax.ShapeDtypeStruct((TILE + spare, 2 * HEAD_DIM), BF16)] * count_ka,
        compiler_params=params(57),
        name="prepare",
    )(place, key_rows, values, attn_out, grad_out, log_sums)
    messages = [sends[0]] + [turn(sends[step], step) for step in range(1, count_ka)]

    later_place, _ = lax.optimization_barrier((place, sends[0]))
    own_queries = pl.pallas_call(
        own_heads_kernel,
        grid_spec=pltpu.PrefetchScalarGridSpec(
            num_scalar_prefetch=1,
            grid=(count_ka,),
            in_specs=[pl.BlockSpec((TILE, width), lambda i, s: (i, s[1]))] * 2,
            out_specs=pl.BlockSpec((2, 1, width, HEAD_DIM), lambda i, s: (0, i, 0, 0)),
        ),
        out_shape=jax.ShapeDtypeStruct((2, count_ka, width, HEAD_DIM), BF16),
        compiler_params=params(60),
        cost_estimate=pl.CostEstimate(flops=0, bytes_accessed=8 * query_rows * width, transcendentals=0),
        name="own_heads",
    )(later_place, queries, grad_out)
    messages, own_queries = lax.optimization_barrier((messages, own_queries))
    own_block = jnp.concatenate([message[:TILE] for message in messages], axis=0)
    own_stats = jnp.concatenate([message[TILE:] for message in messages], axis=0)
    blocks = [own_block] + [swap(own_block, 2 * number) for number in range(1, count_chip)]
    other_stats = swap(own_stats, 1)
    later_order, _ = lax.optimization_barrier((block_order, own_block))
    other_queries = swap(own_queries, 1)

    key_tiles = count_chip * count_ka
    sum_shape = jax.ShapeDtypeStruct((key_tiles, TILE, HEAD_DIM), F32)
    key_shape = jax.ShapeDtypeStruct((key_tiles, TILE, HEAD_DIM), BF16)
    kv_shape = (query_rows + SPARE, 2 * HEAD_DIM)
    half = count_ka // 2
    early = (half, 0)
    late = tuple(step for step in range(1, count_ka) if step != half)
    stages = ((1, tuple(range(count_ka))), (0, early), (0, late))
    tables = pl.pallas_call(
        functools.partial(plan_kernel, (count_chip, count_ka, stages)),
        in_specs=in_smem(3),
        out_specs=in_smem(len(stages)),
        out_shape=[
            jax.ShapeDtypeStruct((ENTRY * (1 + len(steps) * (key_tiles + 1) // 2),), jnp.int32)
            for _, steps in stages
        ],
        scratch_shapes=[SMEM((key_tiles + 2,), jnp.int32)] * 2,
        cost_estimate=pl.CostEstimate(flops=0, bytes_accessed=1 << 22, transcendentals=0),
        name="plan",
    )(later_order, doc_ids, tile_mask)

    def attend(stage, outs, scratch, *operands):
        steps = stages[stage][1]
        dims = (count_chip, count_ka, heads_dev, share, stage, steps)
        pairs = len(steps) * key_tiles
        return pl.pallas_call(
            functools.partial(attention_kernel, dims),
            in_specs=in_smem(1) + in_vmem(len(operands)),
            out_specs=in_vmem(len(outs)),
            out_shape=outs,
            scratch_shapes=scratch + [
                VMEM((len(steps), head_rows(heads_dev), 2 * TILE), F32),
                VMEM((2 * TILE, width), BF16),
                VMEM((2 * TILE, width), BF16),
                VMEM((len(steps), HEAD_DIM, width), F32),
            ],
            compiler_params=params(14 + key_tiles // 2),
            cost_estimate=pl.CostEstimate(
                flops=10 * pairs * TILE * TILE * width, bytes_accessed=1 << 22, transcendentals=0
            ),
            name=("attention_other", "attention_early", "attention_late")[stage],
        )(tables[stage], *operands)

    part_shape = jax.ShapeDtypeStruct((HEAD_DIM, width), F32)
    full_shape = jax.ShapeDtypeStruct((HEAD_DIM, width), BF16)
    dq_other, *state = attend(
        0,
        [jax.ShapeDtypeStruct((count_ka, HEAD_DIM, width), BF16)] + [key_shape] * 3 + [sum_shape] * 2,
        [], key_gain, value_gain, other_queries, other_stats, *blocks,
    )
    dq_back = swap(dq_other, 1)
    keys, sums = state[:3], state[3:]
    *dq_early, key_sum, value_sum = attend(
        1, [part_shape] * len(early) + [sum_shape] * 2, [],
        own_queries, own_stats, *keys, *sums,
    )
    added = pl.pallas_call(
        functools.partial(add_kernel, (count_ka, early)),
        in_specs=in_vmem(1 + len(early)),
        out_specs=in_vmem(len(early)),
        out_shape=[full_shape] * len(early),
        compiler_params=params(16),
        name="add_queries",
    )(dq_back, *dq_early)
    dq_parts = [None] * count_ka
    added = list(added)
    late_stats, added[-1] = lax.optimization_barrier((own_stats, added[-1]))
    dq_parts[half], dq_parts[0] = turn(added[0], half), added[1]
    results = attend(
        2,
        [full_shape] * len(late) + [jax.ShapeDtypeStruct(kv_shape, F32)]
        + [jax.ShapeDtypeStruct(kv_shape, BF16)] * (count_chip - 1),
        [VMEM(sum_shape.shape, F32)] * 2,
        own_queries, late_stats, *blocks, *keys, key_sum, value_sum, dq_back,
    )
    dq_late, kv_own = results[:len(late)], results[len(late):]
    kv_own = list(kv_own)
    kv_own[2], dq_parts[half] = lax.optimization_barrier((kv_own[2], dq_parts[half]))
    kv_parts = [kv_own[0]] + [swap(kv_own[number], 2 * number) for number in range(1, count_chip)]
    for number, step in enumerate(late):
        dq_parts[step] = turn(dq_late[number], step)

    piece_type = BF16 if share == 1 else F32
    piece_shape = (TILE + SPARE, 2 * HEAD_DIM)
    totals = pl.pallas_call(
        functools.partial(collect_kernel, (count_chip, count_ka, share)),
        in_specs=in_vmem(2 + count_chip),
        out_specs=in_vmem(count_ka),
        out_shape=[jax.ShapeDtypeStruct(piece_shape, piece_type)] * count_ka,
        compiler_params=params(24),
        name="collect",
    )(key_gain, value_gain, *kv_parts)
    pieces = [totals[0]] + [turn(totals[step], -step) for step in range(1, count_ka)]

    grad_keys, grad_values, gains = pl.pallas_call(
        functools.partial(finish_kernel, (count_ka, share)),
        in_specs=in_vmem(2 + count_ka),
        out_specs=in_vmem(3),
        out_shape=[
            jax.ShapeDtypeStruct(key_rows.shape, BF16),
            jax.ShapeDtypeStruct(key_rows.shape, BF16),
            jax.ShapeDtypeStruct((2, key_rows.shape[1]), F32),
        ],
        scratch_shapes=[VMEM((kv_heads, TILE + SPARE, 2 * HEAD_DIM), F32)],
        compiler_params=params(16),
        name="finish",
    )(key_gain, value_gain, *pieces)
    gains = gains + swap(gains, 1)
    first = (0, half)
    turned = pl.pallas_call(
        turn_kernel,
        in_specs=in_vmem(len(first)),
        out_specs=in_vmem(len(first)),
        out_shape=[full_shape] * len(first),
        compiler_params=params(8),
        cost_estimate=pl.CostEstimate(flops=0, bytes_accessed=1 << 22, transcendentals=0),
        name="turn_queries",
    )(*[dq_parts[step] for step in first])
    for number, step in enumerate(first):
        dq_parts[step] = turned[number]
    grad_queries = pl.pallas_call(
        functools.partial(place_kernel, (count_ka, heads_dev, late)),
        in_specs=in_vmem(count_ka),
        out_specs=pl.BlockSpec(memory_space=pl.ANY),
        out_shape=jax.ShapeDtypeStruct((rows_dev, feat_width), BF16),
        scratch_shapes=[VMEM((TILE, width), BF16)] * len(late) + [pltpu.SemaphoreType.DMA((count_ka,))],
        compiler_params=params(16),
        cost_estimate=pl.CostEstimate(flops=0, bytes_accessed=4 * rows_dev * feat_width, transcendentals=0),
        name="place_queries",
    )(*dq_parts)
    return grad_queries, grad_keys, grad_values, gains[0], gains[1]


def solution(mesh):
    placed = (
        P("pb", None),
        P(("pb", "ka"), None),
        P(("pb", "ka"), None),
        P(("pb", "ka"), None),
        P("pb", None),
        P(None, ("pb", "ka")),
        P(),
        P(),
        P(),
        P(),
        P(),
    )
    return jax.shard_map(
        shards,
        mesh=mesh,
        in_specs=placed,
        out_specs=(P(("pb", "ka"), None), P(("pb", "ka"), None), P(("pb", "ka"), None), P(), P()),
        check_vma=False,
    )
```

```python
import functools

import jax
import jax.numpy as jnp
from jax import lax
from jax.experimental import pallas as pl
from jax.experimental.pallas import tpu as pltpu
from jax.sharding import PartitionSpec as P

HEAD_DIM = 128
TILE = 128
SPARE = 16
LOG2E = 1.4426950408889634
ENTRY = 4
PARTS = 4
LAST_DIMS = (((1,), (1,)), ((), ()))
VMEM = pltpu.VMEM
SMEM = pltpu.SMEM
F32 = jnp.float32
BF16 = jnp.bfloat16


def split_three(x):
    high = x.astype(BF16).astype(F32)
    rest = x - high
    middle = rest.astype(BF16).astype(F32)
    low = (rest - middle).astype(BF16).astype(F32)
    return high, middle, low


def head_rows(heads_dev):
    return -(-heads_dev // 8) * 8


def extra_rows(heads_dev):
    return -(-3 * head_rows(heads_dev) // 16) * 16


def prepare_kernel(dims, key_ref, value_ref, attn_ref, grads_ref, lse_ref, *rest):
    count_ka, heads, heads_dev, share = dims
    outs, (attn, grad, lse_pad, delta_pad, sems) = rest[:count_ka], rest[count_ka:]
    _, place_ka = places()
    rows8 = head_rows(heads_dev)
    part_heads = heads // PARTS
    rows = pl.ds(pl.multiple_of(place_ka * TILE, TILE), TILE)
    copies = []
    for part in range(PARTS):
        columns = pl.ds(part * part_heads * HEAD_DIM, part_heads * HEAD_DIM)
        copies.append((
            pltpu.make_async_copy(attn_ref.at[:, columns], attn.at[part], sems.at[0, part]),
            pltpu.make_async_copy(grads_ref.at[rows, columns], grad.at[part], sems.at[1, part]),
        ))
        for copy in copies[-1]:
            copy.start()
    for step in range(count_ka):
        target = lax.rem(place_ka + step, count_ka)
        kv_at = pl.ds(pl.multiple_of(target // share * HEAD_DIM, HEAD_DIM), HEAD_DIM)
        outs[step][:TILE, :HEAD_DIM] = key_ref[:, kv_at]
        outs[step][:TILE, HEAD_DIM:] = value_ref[:, kv_at]
    lanes = lax.broadcasted_iota(jnp.int32, (TILE, TILE), 1)
    columns = jnp.zeros((TILE, TILE), F32)
    for part in range(PARTS):
        for copy in copies[part]:
            copy.wait()
        for head in range(part_heads):
            at = pl.ds(head * HEAD_DIM, HEAD_DIM)
            products = grad[part, :, at].astype(F32) * attn[part, :, at].astype(F32)
            total = jnp.sum(products, axis=1, keepdims=True)
            columns = jnp.where(lanes == part * part_heads + head, total, columns)
    delta_pad[...] = jnp.zeros_like(delta_pad)
    lse_pad[...] = jnp.zeros_like(lse_pad)
    delta_pad[:heads, :] = columns.T[:heads, :]
    lse_pad[:heads, :] = lse_ref[...]
    filler = extra_rows(heads_dev) - 3 * rows8
    for step in range(count_ka):
        target = lax.rem(place_ka + step, count_ka)
        head_at = pl.ds(target * heads_dev, rows8)
        both = jnp.concatenate([lse_pad[head_at, :], delta_pad[head_at, :]], axis=1)
        terms = list(split_three(both))
        if filler:
            terms.append(jnp.zeros((filler, 2 * HEAD_DIM), F32))
        outs[step][TILE:, :] = jnp.concatenate(terms, axis=0).astype(BF16)


def own_heads_kernel(dims, queries_ref, grads_ref, out_ref, sems):
    count_ka, heads_dev = dims
    _, place_ka = places()
    copies = []
    for number, ref in enumerate((queries_ref, grads_ref)):
        for head in range(heads_dev):
            columns = pl.ds(pl.multiple_of((place_ka * heads_dev + head) * HEAD_DIM, HEAD_DIM), HEAD_DIM)
            for tile in range(count_ka):
                copies.append(pltpu.make_async_copy(
                    ref.at[pl.ds(tile * TILE, TILE), columns],
                    out_ref.at[number, tile, pl.ds(head * HEAD_DIM, HEAD_DIM), :],
                    sems.at[number, head, tile],
                ))
                copies[-1].start()
    for copy in copies:
        copy.wait()


def places():
    return lax.axis_index("pb"), lax.axis_index("ka")


def plan_kernel(dims, order_ref, doc_ref, mask_ref, *tables):
    count_chip, count_ka, stages = dims
    place_pb, place_ka = places()
    for table, (other, steps) in zip(tables, stages):
        query_pb = place_pb ^ other

        def query_step(turn_q, units, table=table, query_pb=query_pb, steps=steps):
            step_q = jnp.int32(steps[0])
            for number, step in enumerate(steps):
                step_q = jnp.where(turn_q == number, step, step_q)
            tile_at = lax.rem(place_ka + step_q, count_ka)
            seq_q = order_ref[query_pb * count_ka + tile_at]
            doc_q = doc_ref[seq_q]

            def collect(number, units):
                for step in range(count_ka):
                    stored = (place_pb ^ (2 * number)) * count_ka + lax.rem(
                        place_ka - step + count_ka, count_ka
                    )
                    seq_k = order_ref[stored]
                    live = (mask_ref[seq_q, seq_k] == 1) & (doc_ref[seq_k] == doc_q) & (seq_q >= seq_k)
                    base = ENTRY * (units + 1)
                    table[base] = turn_q
                    table[base + 1] = tile_at
                    table[base + 2] = number * count_ka + step
                    table[base + 3] = jnp.where(seq_q == seq_k, 0, -TILE)
                    units = units + live.astype(jnp.int32)
                return units

            return lax.fori_loop(0, count_chip, collect, units)

        units = lax.fori_loop(0, len(steps), query_step, jnp.int32(0))
        table[0] = (units + 1) // 2
        base = ENTRY * (units + 1)
        table[base] = 0
        table[base + 1] = 0
        table[base + 2] = 0
        table[base + 3] = TILE


def attention_kernel(dims, table_ref, *rest):
    count_chip, count_ka, heads_dev, share, stage, steps = dims
    if stage == 0:
        (key_gain_ref, value_gain_ref), rest = rest[:2], rest[2:]
    (heads_ref, stats_ref), rest = rest[:2], rest[2:]
    if stage in (0, 3):
        blocks, rest = rest[:count_chip], rest[count_chip:]
    if stage == 0:
        (dq_out, keys, values, keys_t, key_sum, value_sum), rest = rest[:6], rest[6:]
    else:
        (keys, values, keys_t, key_start, value_start), rest = rest[:5], rest[5:]
        dq_out, rest = rest[0], rest[1:]
        if stage == 3:
            kv_outs, rest = rest[:count_chip], rest[count_chip:]
        (key_sum, value_sum), rest = rest[:2], rest[2:]
    lse_delta, weights_low, dscores_low, dq_sum = rest
    _, place_ka = places()
    rows8 = head_rows(heads_dev)
    spare = extra_rows(heads_dev)
    score_scale = HEAD_DIM ** -0.5

    if stage == 0:
        kv_at = pl.ds(pl.multiple_of(place_ka // share * HEAD_DIM, HEAD_DIM), HEAD_DIM)
        key_gain = key_gain_ref[:, kv_at]
        value_gain = value_gain_ref[:, kv_at]
        for number in range(count_chip):
            for step in range(count_ka):
                part = pl.ds(step * TILE, TILE)
                local = number * count_ka + step
                key_tile = (blocks[number][part, :HEAD_DIM].astype(F32) * key_gain).astype(BF16)
                value_tile = (blocks[number][part, HEAD_DIM:].astype(F32) * value_gain).astype(BF16)
                keys[local] = key_tile
                values[local] = value_tile
                keys_t[local] = key_tile.T
        key_sum[...] = jnp.zeros_like(key_sum)
        value_sum[...] = jnp.zeros_like(value_sum)
    else:
        key_sum[...] = key_start[...]
        value_sum[...] = value_start[...]

    reach = (lax.broadcasted_iota(jnp.int32, (TILE, TILE), 1)
             - lax.broadcasted_iota(jnp.int32, (TILE, TILE), 0))
    reach = jnp.concatenate([reach, reach], axis=1)

    for number, step in enumerate(steps):
        slot = count_ka - step if step else 0
        packed = stats_ref[pl.ds(slot * spare, spare), :].astype(F32)
        lse_delta[number] = (packed[:rows8] + packed[rows8:2 * rows8]) + packed[2 * rows8:3 * rows8]
    dq_sum[...] = jnp.zeros_like(dq_sum)

    def unit_step(at, carry):
        terms = []
        for lane in range(2):
            base = ENTRY * (2 * at + lane + 1)
            turn_q, tile_at, key_at = table_ref[base], table_ref[base + 1], table_ref[base + 2]
            allowed = reach >= table_ref[base + 3]
            for head in range(0, heads_dev, 2):
                part = pl.ds(head * HEAD_DIM, 2 * HEAD_DIM)
                scores = lax.dot_general(
                    keys[key_at], heads_ref[0, tile_at, part, :], LAST_DIMS, preferred_element_type=F32
                )
                dweights = lax.dot_general(
                    values[key_at], heads_ref[1, tile_at, part, :], LAST_DIMS, preferred_element_type=F32
                )
                lse_row, delta_row = [
                    jnp.concatenate(
                        [lse_delta[turn_q, number:number + 1, lanes] for number in (head, head + 1)], axis=1
                    )
                    for lanes in (slice(0, TILE), slice(TILE, 2 * TILE))
                ]
                weights = jnp.exp2(scores * (score_scale * LOG2E) - lse_row * LOG2E)
                weights = jnp.where(allowed, weights, 0.0)
                weights_low[lane, :, part] = weights.astype(BF16)
                dscores_low[lane, :, part] = (weights * (dweights - delta_row)).astype(BF16)
            terms.append((
                turn_q,
                key_at,
                jnp.dot(weights_low[lane], heads_ref[1, tile_at], preferred_element_type=F32),
                jnp.dot(dscores_low[lane], heads_ref[0, tile_at], preferred_element_type=F32),
                jnp.dot(keys_t[key_at], dscores_low[lane], preferred_element_type=F32),
            ))
        for turn_q, key_at, value_term, key_term, dq_term in terms:
            value_sum[key_at] += value_term
            key_sum[key_at] += key_term
            dq_sum[turn_q] += dq_term
        return carry

    lax.fori_loop(0, table_ref[0], unit_step, 0)
    for number in range(len(steps)):
        dq_out[number] = (dq_sum[number] * score_scale).astype(dq_out.dtype)
    if stage != 3:
        return

    key_gains = jnp.zeros((8, HEAD_DIM), F32)
    value_gains = jnp.zeros((8, HEAD_DIM), F32)
    for number in range(count_chip):
        for step in range(count_ka):
            part = pl.ds(step * TILE, TILE)
            local = number * count_ka + step
            key_total = key_sum[local] * score_scale
            value_total = value_sum[local]
            kv_outs[number][part, :HEAD_DIM] = key_total.astype(kv_outs[number].dtype)
            kv_outs[number][part, HEAD_DIM:] = value_total.astype(kv_outs[number].dtype)
            key_raw = blocks[number][part, :HEAD_DIM].astype(F32)
            value_raw = blocks[number][part, HEAD_DIM:].astype(F32)
            key_gains += jnp.sum((key_total * key_raw).reshape(TILE // 8, 8, HEAD_DIM), axis=0)
            value_gains += jnp.sum((value_total * value_raw).reshape(TILE // 8, 8, HEAD_DIM), axis=0)
    gains = jnp.concatenate([jnp.sum(key_gains, axis=0, keepdims=True),
                             jnp.sum(value_gains, axis=0, keepdims=True)], axis=1)
    packed = pack_gains(gains)
    for number in range(count_chip):
        kv_outs[number][count_ka * TILE:, :] = packed.astype(kv_outs[number].dtype)


def pack_gains(gains):
    rows = lax.broadcasted_iota(jnp.int32, (SPARE, gains.shape[1]), 0)
    high, middle, low = split_three(gains)
    packed = jnp.where(rows == 0, high, jnp.where(rows == 1, middle, low))
    return jnp.where(rows < 3, packed, 0.0)


def add_kernel(part_ref, other_ref, *outs):
    width = part_ref.shape[2]
    tile, column = 0, 0
    for out_ref in outs:
        part = pl.ds(column, out_ref.shape[1])
        out_ref[...] = (part_ref[tile, :, part] + other_ref[tile, :, part].astype(F32)).astype(BF16)
        column += out_ref.shape[1]
        if column == width:
            tile, column = tile + 1, 0


def collect_kernel(dims, key_gain_ref, value_gain_ref, *rest):
    count_chip, count_ka, share = dims
    parts, outs = rest[:count_chip], rest[count_chip:]
    kv_at = pl.ds(pl.multiple_of(places()[1] // share * HEAD_DIM, HEAD_DIM), HEAD_DIM)
    gain = jnp.concatenate([key_gain_ref[:, kv_at], value_gain_ref[:, kv_at]], axis=1)
    for step in range(count_ka):
        rows = pl.ds(step * TILE, TILE)
        total = parts[0][rows, :]
        for number in range(1, count_chip):
            total = total + parts[number][rows, :].astype(F32)
        if share == 1:
            total = total * gain
        outs[step][:TILE, :] = total.astype(outs[step].dtype)
    spare = pl.ds(count_ka * TILE, SPARE)
    total = parts[0][spare, :]
    for number in range(1, count_chip):
        total = total + parts[number][spare, :].astype(F32)
    packed = pack_gains(jnp.sum(total, axis=0, keepdims=True))
    for step in range(count_ka):
        outs[step][TILE:, :] = packed.astype(outs[step].dtype)


def turn_kernel(*refs):
    half = len(refs) // 2
    for source, target in zip(refs[:half], refs[half:]):
        for head in range(source.shape[1] // HEAD_DIM):
            part = pl.ds(head * HEAD_DIM, HEAD_DIM)
            target[:, part] = source[:, part].T


def place_kernel(dims, *rest):
    count_ka, heads_dev, pieces = dims
    dq_parts, rest = rest[:len(pieces)], rest[len(pieces):]
    dq_out, rest = rest[0], rest[1:]
    turned, sems = rest[:-1], rest[-1]
    copies, used = [], 0
    for number, ((step, offset, late), piece) in enumerate(zip(pieces, dq_parts)):
        source = lax.rem(places()[1] - step + count_ka, count_ka)
        column = (source * heads_dev + offset) * HEAD_DIM
        columns = pl.ds(pl.multiple_of(column, HEAD_DIM), piece.shape[1])
        if late:
            turn_kernel(piece, turned[used])
            piece, used = turned[used], used + 1
        copies.append(pltpu.make_async_copy(piece, dq_out.at[:, columns], sems.at[number]))
        copies[-1].start()
    for copy in copies:
        copy.wait()


def finish_kernel(dims, key_gain_ref, value_gain_ref, *rest):
    count_ka, share = dims
    pieces, rest = rest[:count_ka], rest[count_ka:]
    dk_out, dv_out, gains_out, sums = rest
    _, place_ka = places()
    sums[...] = jnp.zeros_like(sums)
    for step in range(count_ka):
        source = lax.rem(place_ka + step, count_ka)
        sums[source // share] += pieces[step][...].astype(F32)
    for head in range(count_ka // share):
        part = pl.ds(head * HEAD_DIM, HEAD_DIM)
        key_total = sums[head, :TILE, :HEAD_DIM]
        value_total = sums[head, :TILE, HEAD_DIM:]
        if share > 1:
            key_total = key_total * key_gain_ref[:, part]
            value_total = value_total * value_gain_ref[:, part]
        dk_out[:, part] = key_total.astype(BF16)
        dv_out[:, part] = value_total.astype(BF16)
        gains = jnp.sum(sums[head, TILE:, :], axis=0, keepdims=True)
        gains_out[0:1, part] = gains[:, :HEAD_DIM]
        gains_out[1:2, part] = gains[:, HEAD_DIM:]


def in_vmem(count):
    return [pl.BlockSpec(memory_space=VMEM)] * count


def in_smem(count):
    return [pl.BlockSpec(memory_space=SMEM)] * count


def anywhere(count):
    return [pl.BlockSpec(memory_space=pl.ANY)] * count


def params(mib):
    return pltpu.CompilerParams(vmem_limit_bytes=mib * 1024 * 1024)


def shards(
    queries,
    key_rows,
    values,
    attn_out,
    grad_out,
    log_sums,
    key_gain,
    value_gain,
    doc_ids,
    tile_mask,
    block_order,
):
    count_pb = lax.axis_size("pb")
    count_ka = lax.axis_size("ka")
    rows_dev = key_rows.shape[0]
    query_rows = queries.shape[0]
    heads = log_sums.shape[0]
    feat_width = queries.shape[1]
    kv_heads = key_rows.shape[1] // HEAD_DIM
    heads_dev = heads // count_ka
    share = count_ka // kv_heads
    assert rows_dev == TILE and share * kv_heads == count_ka and count_pb & (count_pb - 1) == 0
    width = heads_dev * HEAD_DIM
    key_gain = key_gain.reshape(1, -1)
    value_gain = value_gain.reshape(1, -1)

    spare = extra_rows(heads_dev)
    count_chip = count_pb // 2

    def swap(array, number):
        return lax.ppermute(array, "pb", [(at, at ^ number) for at in range(count_pb)])

    def turn(array, step):
        return lax.ppermute(array, "ka", [(at, (at + step) % count_ka) for at in range(count_ka)])

    sends = pl.pallas_call(
        functools.partial(prepare_kernel, (count_ka, heads, heads_dev, share)),
        in_specs=in_vmem(2) + anywhere(2) + in_vmem(1),
        out_specs=in_vmem(count_ka),
        out_shape=[jax.ShapeDtypeStruct((TILE + spare, 2 * HEAD_DIM), BF16)] * count_ka,
        scratch_shapes=[VMEM((PARTS, TILE, feat_width // PARTS), BF16)] * 2
        + [VMEM((heads + 8, TILE), F32)] * 2
        + [pltpu.SemaphoreType.DMA((2, PARTS))],
        compiler_params=params(57),
        name="prepare",
    )(key_rows, values, attn_out, grad_out, log_sums)
    messages = [sends[0]] + [turn(sends[step], step) for step in range(1, count_ka)]

    later_queries, _ = lax.optimization_barrier((queries, sends[0]))
    own_queries = pl.pallas_call(
        functools.partial(own_heads_kernel, (count_ka, heads_dev)),
        in_specs=anywhere(2),
        out_specs=in_vmem(1)[0],
        out_shape=jax.ShapeDtypeStruct((2, count_ka, width, HEAD_DIM), BF16),
        scratch_shapes=[pltpu.SemaphoreType.DMA((2, heads_dev, count_ka))],
        compiler_params=params(57),
        cost_estimate=pl.CostEstimate(flops=0, bytes_accessed=8 * query_rows * width, transcendentals=0),
        name="own_heads",
    )(later_queries, grad_out)
    messages, own_queries = lax.optimization_barrier((messages, own_queries))
    own_block = jnp.concatenate([message[:TILE] for message in messages], axis=0)
    own_stats = jnp.concatenate([message[TILE:] for message in messages], axis=0)
    blocks = [own_block] + [swap(own_block, 2 * number) for number in range(1, count_chip)]
    other_stats = swap(own_stats, 1)
    later_order, _ = lax.optimization_barrier((block_order, own_block))
    other_queries = swap(own_queries, 1)

    key_tiles = count_chip * count_ka
    sum_shape = jax.ShapeDtypeStruct((key_tiles, TILE, HEAD_DIM), F32)
    key_shape = jax.ShapeDtypeStruct((key_tiles, TILE, HEAD_DIM), BF16)
    kv_shape = (query_rows + SPARE, 2 * HEAD_DIM)
    half = count_ka // 2
    rest_steps = tuple(step for step in range(1, count_ka) if step != half) + (0,)
    stages = ((1, (half,)), (0, (half,)), (1, rest_steps), (0, rest_steps))
    tables = pl.pallas_call(
        functools.partial(plan_kernel, (count_chip, count_ka, stages)),
        in_specs=in_smem(3),
        out_specs=in_smem(len(stages)),
        out_shape=[
            jax.ShapeDtypeStruct((ENTRY * (2 + len(steps) * key_tiles),), jnp.int32)
            for _, steps in stages
        ],
        cost_estimate=pl.CostEstimate(flops=0, bytes_accessed=1 << 22, transcendentals=0),
        name="plan",
    )(later_order, doc_ids, tile_mask)

    def attend(stage, outs, scratch, *operands):
        steps = stages[stage][1]
        dims = (count_chip, count_ka, heads_dev, share, stage, steps)
        pairs = len(steps) * key_tiles
        return pl.pallas_call(
            functools.partial(attention_kernel, dims),
            in_specs=in_smem(1) + in_vmem(len(operands)),
            out_specs=in_vmem(len(outs)),
            out_shape=outs,
            scratch_shapes=scratch + [
                VMEM((len(steps), head_rows(heads_dev), 2 * TILE), F32),
                VMEM((2, TILE, width), BF16),
                VMEM((2, TILE, width), BF16),
                VMEM((len(steps), HEAD_DIM, width), F32),
            ],
            compiler_params=params(14 + key_tiles // 2),
            cost_estimate=pl.CostEstimate(
                flops=10 * pairs * TILE * TILE * width if stage < 3 else 0,
                bytes_accessed=1 << 20 if stage < 3 else 0,
                transcendentals=0,
            ),
            name=("attention_other_first", "attention_own_first", "attention_other", "attention_own")[stage],
        )(tables[stage], *operands)

    def part_shape(stage, dtype):
        return jax.ShapeDtypeStruct((len(stages[stage][1]), HEAD_DIM, width), dtype)

    def add(part, other, cuts):
        return pl.pallas_call(
            add_kernel,
            in_specs=in_vmem(2),
            out_specs=in_vmem(part.shape[0] * cuts),
            out_shape=[jax.ShapeDtypeStruct((HEAD_DIM, width // cuts), BF16)] * (part.shape[0] * cuts),
            compiler_params=params(4 * part.shape[0]),
            name="add_queries",
        )(part, other)

    dq_other, *state = attend(
        0, [part_shape(0, BF16)] + [key_shape] * 3 + [sum_shape] * 2,
        [], key_gain, value_gain, other_queries, other_stats, *blocks,
    )
    keys, sums = state[:3], state[3:]
    dq_back = swap(dq_other, 1)
    dq_own, *sums = attend(
        1, [part_shape(1, F32)] + [sum_shape] * 2, [], own_queries, own_stats, *keys, *sums
    )
    dq_parts = [None] * count_ka
    dq_first = add(dq_own, dq_back, 2)
    dq_halves = [turn(part, half) for part in dq_first]
    rest_stats, _ = lax.optimization_barrier((other_stats, dq_first[0]))
    dq_other, *sums = attend(
        2, [part_shape(2, BF16)] + [sum_shape] * 2, [], other_queries, rest_stats, *keys, *sums
    )
    dq_other, dq_halves[0] = lax.optimization_barrier((dq_other, dq_halves[0]))
    dq_back = swap(dq_other, 1)
    dq_own, *kv_own = attend(
        3,
        [part_shape(3, F32), jax.ShapeDtypeStruct(kv_shape, F32)]
        + [jax.ShapeDtypeStruct(kv_shape, BF16)] * (count_chip - 1),
        [VMEM(sum_shape.shape, F32)] * 2,
        own_queries, own_stats, *blocks, *keys, *sums,
    )
    for step, tile in zip(rest_steps, add(dq_own, dq_back, 1)):
        dq_parts[step] = turn(tile, step) if step else tile
    kv_own[2], dq_halves[1] = lax.optimization_barrier((kv_own[2], dq_halves[1]))
    kv_parts = [kv_own[0]] + [swap(kv_own[number], 2 * number) for number in range(1, count_chip)]
    piece_type = BF16 if share == 1 else F32
    piece_shape = (TILE + SPARE, 2 * HEAD_DIM)
    totals = pl.pallas_call(
        functools.partial(collect_kernel, (count_chip, count_ka, share)),
        in_specs=in_vmem(2 + count_chip),
        out_specs=in_vmem(count_ka),
        out_shape=[jax.ShapeDtypeStruct(piece_shape, piece_type)] * count_ka,
        compiler_params=params(24),
        name="collect",
    )(key_gain, value_gain, *kv_parts)
    first_turns = [dq_parts[step] for step in rest_steps if step]
    totals, first_turns = lax.optimization_barrier((totals, first_turns))
    for step, tile in zip([step for step in rest_steps if step], first_turns):
        dq_parts[step] = tile
    pieces = [totals[0]] + [turn(totals[step], -step) for step in range(1, count_ka)]

    grad_keys, grad_values, gains = pl.pallas_call(
        functools.partial(finish_kernel, (count_ka, share)),
        in_specs=in_vmem(2 + count_ka),
        out_specs=in_vmem(3),
        out_shape=[
            jax.ShapeDtypeStruct(key_rows.shape, BF16),
            jax.ShapeDtypeStruct(key_rows.shape, BF16),
            jax.ShapeDtypeStruct((2, key_rows.shape[1]), F32),
        ],
        scratch_shapes=[VMEM((kv_heads, TILE + SPARE, 2 * HEAD_DIM), F32)],
        compiler_params=params(16),
        name="finish",
    )(key_gain, value_gain, *pieces)
    gains = gains + swap(gains, 1)
    first = [dq_parts[0], *dq_halves]
    turned = pl.pallas_call(
        turn_kernel,
        in_specs=in_vmem(len(first)),
        out_specs=in_vmem(len(first)),
        out_shape=[jax.ShapeDtypeStruct(part.shape, BF16) for part in first],
        compiler_params=params(8),
        cost_estimate=pl.CostEstimate(flops=0, bytes_accessed=1 << 22, transcendentals=0),
        name="turn_queries",
    )(*first)
    late = [step for step in rest_steps if step]
    where = ((0, 0, False), (half, 0, False), (half, heads_dev // 2, False))
    where += tuple((step, 0, True) for step in late)
    grad_queries = pl.pallas_call(
        functools.partial(place_kernel, (count_ka, heads_dev, where)),
        in_specs=in_vmem(len(where)),
        out_specs=pl.BlockSpec(memory_space=pl.ANY),
        out_shape=jax.ShapeDtypeStruct((rows_dev, feat_width), BF16),
        scratch_shapes=[VMEM((TILE, width), BF16)] * len(late) + [pltpu.SemaphoreType.DMA((len(where),))],
        compiler_params=params(16),
        cost_estimate=pl.CostEstimate(flops=0, bytes_accessed=4 * rows_dev * feat_width, transcendentals=0),
        name="place_queries",
    )(*turned, *[dq_parts[step] for step in late])
    return grad_queries, grad_keys, grad_values, gains[0], gains[1]


def solution(mesh):
    placed = (
        P("pb", None),
        P(("pb", "ka"), None),
        P(("pb", "ka"), None),
        P(("pb", "ka"), None),
        P("pb", None),
        P(None, ("pb", "ka")),
        P(),
        P(),
        P(),
        P(),
        P(),
    )
    return jax.shard_map(
        shards,
        mesh=mesh,
        in_specs=placed,
        out_specs=(P(("pb", "ka"), None), P(("pb", "ka"), None), P(("pb", "ka"), None), P(), P()),
        check_vma=False,
    )
```

```python
import functools

import jax
import jax.numpy as jnp
from jax import lax
from jax.experimental import pallas as pl
from jax.experimental.pallas import tpu as pltpu
from jax.sharding import PartitionSpec as P

HEAD_DIM = 128
TILE = 128
SPARE = 16
LOG2E = 1.4426950408889634
ENTRY = 4
PARTS = 4
LAST_DIMS = (((1,), (1,)), ((), ()))
VMEM = pltpu.VMEM
SMEM = pltpu.SMEM
F32 = jnp.float32
BF16 = jnp.bfloat16


def split_three(x):
    high = x.astype(BF16).astype(F32)
    rest = x - high
    middle = rest.astype(BF16).astype(F32)
    low = (rest - middle).astype(BF16).astype(F32)
    return high, middle, low


def head_rows(heads_dev):
    return -(-heads_dev // 8) * 8


def extra_rows(heads_dev):
    return -(-3 * head_rows(heads_dev) // 16) * 16


def prepare_kernel(dims, key_ref, value_ref, attn_ref, grads_ref, lse_ref, *rest):
    count_ka, heads, heads_dev, share = dims
    outs, (attn, grad, lse_pad, delta_pad, sems) = rest[:count_ka], rest[count_ka:]
    _, place_ka = places()
    rows8 = head_rows(heads_dev)
    part_heads = heads // PARTS
    rows = pl.ds(pl.multiple_of(place_ka * TILE, TILE), TILE)
    copies = []
    for part in range(PARTS):
        columns = pl.ds(part * part_heads * HEAD_DIM, part_heads * HEAD_DIM)
        copies.append((
            pltpu.make_async_copy(attn_ref.at[:, columns], attn.at[part], sems.at[0, part]),
            pltpu.make_async_copy(grads_ref.at[rows, columns], grad.at[part], sems.at[1, part]),
        ))
        for copy in copies[-1]:
            copy.start()
    for step in range(count_ka):
        target = lax.rem(place_ka + step, count_ka)
        kv_at = pl.ds(pl.multiple_of(target // share * HEAD_DIM, HEAD_DIM), HEAD_DIM)
        outs[step][:TILE, :HEAD_DIM] = key_ref[:, kv_at]
        outs[step][:TILE, HEAD_DIM:] = value_ref[:, kv_at]
    lanes = lax.broadcasted_iota(jnp.int32, (TILE, TILE), 1)
    columns = jnp.zeros((TILE, TILE), F32)
    for part in range(PARTS):
        for copy in copies[part]:
            copy.wait()
        for head in range(part_heads):
            at = pl.ds(head * HEAD_DIM, HEAD_DIM)
            products = grad[part, :, at].astype(F32) * attn[part, :, at].astype(F32)
            total = jnp.sum(products, axis=1, keepdims=True)
            columns = jnp.where(lanes == part * part_heads + head, total, columns)
    delta_pad[...] = jnp.zeros_like(delta_pad)
    lse_pad[...] = jnp.zeros_like(lse_pad)
    delta_pad[:heads, :] = columns.T[:heads, :]
    lse_pad[:heads, :] = lse_ref[...]
    filler = extra_rows(heads_dev) - 3 * rows8
    for step in range(count_ka):
        target = lax.rem(place_ka + step, count_ka)
        head_at = pl.ds(target * heads_dev, rows8)
        both = jnp.concatenate([lse_pad[head_at, :], delta_pad[head_at, :]], axis=1)
        terms = list(split_three(both))
        if filler:
            terms.append(jnp.zeros((filler, 2 * HEAD_DIM), F32))
        outs[step][TILE:, :] = jnp.concatenate(terms, axis=0).astype(BF16)


def own_heads_kernel(dims, queries_ref, grads_ref, out_ref, sems):
    count_ka, heads_dev = dims
    _, place_ka = places()
    copies = []
    for number, ref in enumerate((queries_ref, grads_ref)):
        for head in range(heads_dev):
            columns = pl.ds(pl.multiple_of((place_ka * heads_dev + head) * HEAD_DIM, HEAD_DIM), HEAD_DIM)
            for tile in range(count_ka):
                copies.append(pltpu.make_async_copy(
                    ref.at[pl.ds(tile * TILE, TILE), columns],
                    out_ref.at[number, tile, pl.ds(head * HEAD_DIM, HEAD_DIM), :],
                    sems.at[number, head, tile],
                ))
                copies[-1].start()
    for copy in copies:
        copy.wait()


def places():
    return lax.axis_index("pb"), lax.axis_index("ka")


def plan_kernel(dims, order_ref, doc_ref, mask_ref, *tables):
    count_chip, count_ka, stages = dims
    place_pb, place_ka = places()
    for table, (other, steps) in zip(tables, stages):
        query_pb = place_pb ^ other

        def query_step(turn_q, units, table=table, query_pb=query_pb, steps=steps):
            step_q = jnp.int32(steps[0])
            for number, step in enumerate(steps):
                step_q = jnp.where(turn_q == number, step, step_q)
            tile_at = lax.rem(place_ka + step_q, count_ka)
            seq_q = order_ref[query_pb * count_ka + tile_at]
            doc_q = doc_ref[seq_q]

            def collect(number, units):
                for step in range(count_ka):
                    stored = (place_pb ^ (2 * number)) * count_ka + lax.rem(
                        place_ka - step + count_ka, count_ka
                    )
                    seq_k = order_ref[stored]
                    live = (mask_ref[seq_q, seq_k] == 1) & (doc_ref[seq_k] == doc_q) & (seq_q >= seq_k)
                    base = ENTRY * (units + 1)
                    table[base] = turn_q
                    table[base + 1] = tile_at
                    table[base + 2] = number * count_ka + step
                    table[base + 3] = jnp.where(seq_q == seq_k, 0, -TILE)
                    units = units + live.astype(jnp.int32)
                return units

            return lax.fori_loop(0, count_chip, collect, units)

        units = lax.fori_loop(0, len(steps), query_step, jnp.int32(0))
        table[0] = (units + 1) // 2
        base = ENTRY * (units + 1)
        table[base] = 0
        table[base + 1] = 0
        table[base + 2] = 0
        table[base + 3] = TILE


def attention_kernel(dims, table_ref, *rest):
    count_chip, count_ka, heads_dev, share, stage, steps = dims
    if stage == 0:
        (key_gain_ref, value_gain_ref), rest = rest[:2], rest[2:]
    (heads_ref, stats_ref), rest = rest[:2], rest[2:]
    if stage in (0, 2):
        blocks, rest = rest[:count_chip], rest[count_chip:]
    if stage == 0:
        (dq_out, keys, values, keys_t, key_sum, value_sum), rest = rest[:6], rest[6:]
    else:
        (keys, values, keys_t, key_start, value_start), rest = rest[:5], rest[5:]
        dq_out, rest = rest[0], rest[1:]
        if stage == 2:
            (kv_own, kv_all), rest = rest[:2], rest[2:]
        (key_sum, value_sum), rest = rest[:2], rest[2:]
    lse_delta, weights_low, dscores_low, dq_sum = rest
    _, place_ka = places()
    rows8 = head_rows(heads_dev)
    spare = extra_rows(heads_dev)
    score_scale = HEAD_DIM ** -0.5

    if stage == 0:
        kv_at = pl.ds(pl.multiple_of(place_ka // share * HEAD_DIM, HEAD_DIM), HEAD_DIM)
        key_gain = key_gain_ref[:, kv_at]
        value_gain = value_gain_ref[:, kv_at]
        for number in range(count_chip):
            for step in range(count_ka):
                part = pl.ds(step * TILE, TILE)
                local = number * count_ka + step
                key_tile = (blocks[number][part, :HEAD_DIM].astype(F32) * key_gain).astype(BF16)
                value_tile = (blocks[number][part, HEAD_DIM:].astype(F32) * value_gain).astype(BF16)
                keys[local] = key_tile
                values[local] = value_tile
                keys_t[local] = key_tile.T
        key_sum[...] = jnp.zeros_like(key_sum)
        value_sum[...] = jnp.zeros_like(value_sum)
    else:
        key_sum[...] = key_start[...]
        value_sum[...] = value_start[...]

    reach = (lax.broadcasted_iota(jnp.int32, (TILE, TILE), 1)
             - lax.broadcasted_iota(jnp.int32, (TILE, TILE), 0))
    reach = jnp.concatenate([reach, reach], axis=1)

    for number, step in enumerate(steps):
        slot = count_ka - step if step else 0
        packed = stats_ref[pl.ds(slot * spare, spare), :].astype(F32)
        lse_delta[number] = (packed[:rows8] + packed[rows8:2 * rows8]) + packed[2 * rows8:3 * rows8]
    dq_sum[...] = jnp.zeros_like(dq_sum)

    def unit_step(at, carry):
        terms = []
        for lane in range(2):
            base = ENTRY * (2 * at + lane + 1)
            turn_q, tile_at, key_at = table_ref[base], table_ref[base + 1], table_ref[base + 2]
            allowed = reach >= table_ref[base + 3]
            for head in range(0, heads_dev, 2):
                part = pl.ds(head * HEAD_DIM, 2 * HEAD_DIM)
                scores = lax.dot_general(
                    keys[key_at], heads_ref[0, tile_at, part, :], LAST_DIMS, preferred_element_type=F32
                )
                dweights = lax.dot_general(
                    values[key_at], heads_ref[1, tile_at, part, :], LAST_DIMS, preferred_element_type=F32
                )
                lse_row, delta_row = [
                    jnp.concatenate(
                        [lse_delta[turn_q, number:number + 1, lanes] for number in (head, head + 1)], axis=1
                    )
                    for lanes in (slice(0, TILE), slice(TILE, 2 * TILE))
                ]
                weights = jnp.exp2(scores * (score_scale * LOG2E) - lse_row * LOG2E)
                weights = jnp.where(allowed, weights, 0.0)
                weights_low[lane, :, part] = weights.astype(BF16)
                dscores_low[lane, :, part] = (weights * (dweights - delta_row)).astype(BF16)
            terms.append((
                turn_q,
                key_at,
                jnp.dot(weights_low[lane], heads_ref[1, tile_at], preferred_element_type=F32),
                jnp.dot(dscores_low[lane], heads_ref[0, tile_at], preferred_element_type=F32),
                jnp.dot(keys_t[key_at], dscores_low[lane], preferred_element_type=F32),
            ))
        for turn_q, key_at, value_term, key_term, dq_term in terms:
            value_sum[key_at] += value_term
            key_sum[key_at] += key_term
            dq_sum[turn_q] += dq_term
        return carry

    lax.fori_loop(0, table_ref[0], unit_step, 0)
    for number in range(len(steps)):
        dq_out[number] = (dq_sum[number] * score_scale).astype(dq_out.dtype)
    if stage != 2:
        return

    place_chip = places()[0] // 2
    key_gains = jnp.zeros((8, HEAD_DIM), F32)
    value_gains = jnp.zeros((8, HEAD_DIM), F32)
    for number in range(count_chip):
        for step in range(count_ka):
            part = pl.ds(step * TILE, TILE)
            local = number * count_ka + step
            key_total = key_sum[local] * score_scale
            value_total = value_sum[local]
            both = jnp.concatenate([key_total, value_total], axis=1)
            kv_all[place_chip ^ number, part, :] = both.astype(BF16)
            if number == 0:
                kv_own[part, :] = both
            key_raw = blocks[number][part, :HEAD_DIM].astype(F32)
            value_raw = blocks[number][part, HEAD_DIM:].astype(F32)
            key_gains += jnp.sum((key_total * key_raw).reshape(TILE // 8, 8, HEAD_DIM), axis=0)
            value_gains += jnp.sum((value_total * value_raw).reshape(TILE // 8, 8, HEAD_DIM), axis=0)
    gains = jnp.concatenate([jnp.sum(key_gains, axis=0, keepdims=True),
                             jnp.sum(value_gains, axis=0, keepdims=True)], axis=1)
    packed = pack_gains(gains)
    kv_own[count_ka * TILE:, :] = packed
    for number in range(count_chip):
        kv_all[number, count_ka * TILE:, :] = packed.astype(BF16)


def pack_gains(gains):
    rows = lax.broadcasted_iota(jnp.int32, (SPARE, gains.shape[1]), 0)
    high, middle, low = split_three(gains)
    packed = jnp.where(rows == 0, high, jnp.where(rows == 1, middle, low))
    return jnp.where(rows < 3, packed, 0.0)


def add_kernel(steps, part_ref, other_ref, *outs):
    width = part_ref.shape[2]
    tile, column = 0, 0
    for out_ref in outs:
        part = pl.ds(column, out_ref.shape[1])
        other = other_ref[steps[tile], :, part].astype(F32)
        out_ref[...] = (part_ref[tile, :, part] + other).astype(BF16)
        column += out_ref.shape[1]
        if column == width:
            tile, column = tile + 1, 0


def collect_kernel(dims, key_gain_ref, value_gain_ref, *rest):
    count_chip, count_ka, share = dims
    own_ref, parts_ref, out_ref = rest
    place_pb, place_ka = places()
    others = [(place_pb // 2) ^ number for number in range(1, count_chip)]
    kv_at = pl.ds(pl.multiple_of(place_ka // share * HEAD_DIM, HEAD_DIM), HEAD_DIM)
    gain = jnp.concatenate([key_gain_ref[:, kv_at], value_gain_ref[:, kv_at]], axis=1)
    for step in range(count_ka):
        rows = pl.ds(step * TILE, TILE)
        total = own_ref[rows, :]
        for other in others:
            total = total + parts_ref[other, rows, :].astype(F32)
        if share == 1:
            total = total * gain
        out_ref[lax.rem(place_ka - step + count_ka, count_ka), :TILE, :] = total.astype(out_ref.dtype)
    spare = pl.ds(count_ka * TILE, SPARE)
    total = own_ref[spare, :]
    for other in others:
        total = total + parts_ref[other, spare, :].astype(F32)
    packed = pack_gains(jnp.sum(total, axis=0, keepdims=True))
    for step in range(count_ka):
        out_ref[step, TILE:, :] = packed.astype(out_ref.dtype)


def turn_kernel(*refs):
    half = len(refs) // 2
    for source, target in zip(refs[:half], refs[half:]):
        for head in range(source.shape[1] // HEAD_DIM):
            part = pl.ds(head * HEAD_DIM, HEAD_DIM)
            target[:, part] = source[:, part].T


def place_kernel(dims, *rest):
    count_ka, heads_dev, pieces = dims
    dq_parts, rest = rest[:len(pieces)], rest[len(pieces):]
    dq_out, rest = rest[0], rest[1:]
    turned, sems = rest[:-1], rest[-1]
    copies, used = [], 0
    for number, ((step, offset, late), piece) in enumerate(zip(pieces, dq_parts)):
        source = lax.rem(places()[1] - step + count_ka, count_ka)
        column = (source * heads_dev + offset) * HEAD_DIM
        columns = pl.ds(pl.multiple_of(column, HEAD_DIM), piece.shape[1])
        if late:
            turn_kernel(piece, turned[used])
            piece, used = turned[used], used + 1
        copies.append(pltpu.make_async_copy(piece, dq_out.at[:, columns], sems.at[number]))
        copies[-1].start()
    for copy in copies:
        copy.wait()


def finish_kernel(dims, key_gain_ref, value_gain_ref, *rest):
    count_ka, share = dims
    pieces, dk_out, dv_out, gains_out, sums = rest
    for source in range(count_ka):
        if source % share:
            sums[source // share] += pieces[source].astype(F32)
        else:
            sums[source // share] = pieces[source].astype(F32)
    for head in range(count_ka // share):
        part = pl.ds(head * HEAD_DIM, HEAD_DIM)
        key_total = sums[head, :TILE, :HEAD_DIM]
        value_total = sums[head, :TILE, HEAD_DIM:]
        if share > 1:
            key_total = key_total * key_gain_ref[:, part]
            value_total = value_total * value_gain_ref[:, part]
        dk_out[:, part] = key_total.astype(BF16)
        dv_out[:, part] = value_total.astype(BF16)
        gains = jnp.sum(sums[head, TILE:, :], axis=0, keepdims=True)
        gains_out[0:1, part] = gains[:, :HEAD_DIM]
        gains_out[1:2, part] = gains[:, HEAD_DIM:]


def in_vmem(count):
    return [pl.BlockSpec(memory_space=VMEM)] * count


def in_smem(count):
    return [pl.BlockSpec(memory_space=SMEM)] * count


def anywhere(count):
    return [pl.BlockSpec(memory_space=pl.ANY)] * count


def params(mib):
    return pltpu.CompilerParams(vmem_limit_bytes=mib * 1024 * 1024)


def shards(
    queries,
    key_rows,
    values,
    attn_out,
    grad_out,
    log_sums,
    key_gain,
    value_gain,
    doc_ids,
    tile_mask,
    block_order,
):
    count_pb = lax.axis_size("pb")
    count_ka = lax.axis_size("ka")
    rows_dev = key_rows.shape[0]
    query_rows = queries.shape[0]
    heads = log_sums.shape[0]
    feat_width = queries.shape[1]
    kv_heads = key_rows.shape[1] // HEAD_DIM
    heads_dev = heads // count_ka
    share = count_ka // kv_heads
    assert rows_dev == TILE and share * kv_heads == count_ka and count_pb & (count_pb - 1) == 0
    width = heads_dev * HEAD_DIM
    key_gain = key_gain.reshape(1, -1)
    value_gain = value_gain.reshape(1, -1)

    spare = extra_rows(heads_dev)
    count_chip = count_pb // 2

    def swap(array, number):
        return lax.ppermute(array, "pb", [(at, at ^ number) for at in range(count_pb)])

    def turn(array, step):
        return lax.ppermute(array, "ka", [(at, (at + step) % count_ka) for at in range(count_ka)])

    sends = pl.pallas_call(
        functools.partial(prepare_kernel, (count_ka, heads, heads_dev, share)),
        in_specs=in_vmem(2) + anywhere(2) + in_vmem(1),
        out_specs=in_vmem(count_ka),
        out_shape=[jax.ShapeDtypeStruct((TILE + spare, 2 * HEAD_DIM), BF16)] * count_ka,
        scratch_shapes=[VMEM((PARTS, TILE, feat_width // PARTS), BF16)] * 2
        + [VMEM((heads + 8, TILE), F32)] * 2
        + [pltpu.SemaphoreType.DMA((2, PARTS))],
        compiler_params=params(57),
        name="prepare",
    )(key_rows, values, attn_out, grad_out, log_sums)
    messages = [sends[0]] + [turn(sends[step], step) for step in range(1, count_ka)]

    later_queries, _ = lax.optimization_barrier((queries, sends[0]))
    own_queries = pl.pallas_call(
        functools.partial(own_heads_kernel, (count_ka, heads_dev)),
        in_specs=anywhere(2),
        out_specs=in_vmem(1)[0],
        out_shape=jax.ShapeDtypeStruct((2, count_ka, width, HEAD_DIM), BF16),
        scratch_shapes=[pltpu.SemaphoreType.DMA((2, heads_dev, count_ka))],
        compiler_params=params(57),
        cost_estimate=pl.CostEstimate(flops=0, bytes_accessed=8 * query_rows * width, transcendentals=0),
        name="own_heads",
    )(later_queries, grad_out)
    messages, own_queries = lax.optimization_barrier((messages, own_queries))
    other_queries = swap(own_queries, 1)
    own_block = jnp.concatenate([message[:TILE] for message in messages], axis=0)
    own_stats = jnp.concatenate([message[TILE:] for message in messages], axis=0)
    blocks = [own_block] + [swap(own_block, 2 * number) for number in range(1, count_chip)]
    other_stats = swap(own_stats, 1)
    later_order, _ = lax.optimization_barrier((block_order, own_block))

    key_tiles = count_chip * count_ka
    sum_shape = jax.ShapeDtypeStruct((key_tiles, TILE, HEAD_DIM), F32)
    key_shape = jax.ShapeDtypeStruct((key_tiles, TILE, HEAD_DIM), BF16)
    kv_shape = (query_rows + SPARE, 2 * HEAD_DIM)
    half = count_ka // 2
    early = (half, 0)
    late = tuple(step for step in range(1, count_ka) if step != half)
    stages = ((1, tuple(range(count_ka))), (0, early), (0, late))
    tables = pl.pallas_call(
        functools.partial(plan_kernel, (count_chip, count_ka, stages)),
        in_specs=in_smem(3),
        out_specs=in_smem(len(stages)),
        out_shape=[
            jax.ShapeDtypeStruct((ENTRY * (2 + len(steps) * key_tiles),), jnp.int32)
            for _, steps in stages
        ],
        cost_estimate=pl.CostEstimate(flops=0, bytes_accessed=1 << 22, transcendentals=0),
        name="plan",
    )(later_order, doc_ids, tile_mask)

    def attend(stage, outs, scratch, *operands):
        steps = stages[stage][1]
        dims = (count_chip, count_ka, heads_dev, share, stage, steps)
        pairs = len(steps) * key_tiles
        return pl.pallas_call(
            functools.partial(attention_kernel, dims),
            in_specs=in_smem(1) + in_vmem(len(operands)),
            out_specs=in_vmem(len(outs)),
            out_shape=outs,
            scratch_shapes=scratch + [
                VMEM((len(steps), head_rows(heads_dev), 2 * TILE), F32),
                VMEM((2, TILE, width), BF16),
                VMEM((2, TILE, width), BF16),
                VMEM((len(steps), HEAD_DIM, width), F32),
            ],
            compiler_params=params(14 + key_tiles // 2),
            cost_estimate=pl.CostEstimate(
                flops=10 * pairs * TILE * TILE * width if stage < 2 else 0,
                bytes_accessed=1 << 20 if stage < 2 else 0,
                transcendentals=0,
            ),
            name=("attention_other", "attention_own_first", "attention_own")[stage],
        )(tables[stage], *operands)

    def part_shape(stage, dtype):
        return jax.ShapeDtypeStruct((len(stages[stage][1]), HEAD_DIM, width), dtype)

    def add(part, other, steps, cuts):
        widths = [width // cut for cut in cuts for _ in range(cut)]
        return pl.pallas_call(
            functools.partial(add_kernel, steps),
            in_specs=in_vmem(2),
            out_specs=in_vmem(len(widths)),
            out_shape=[jax.ShapeDtypeStruct((HEAD_DIM, each), BF16) for each in widths],
            compiler_params=params(4 * part.shape[0]),
            name="add_queries",
        )(part, other)

    dq_other, *state = attend(
        0, [part_shape(0, BF16)] + [key_shape] * 3 + [sum_shape] * 2,
        [], key_gain, value_gain, other_queries, other_stats, *blocks,
    )
    keys, sums = state[:3], state[3:]
    dq_back = swap(dq_other, 1)
    dq_own, *sums = attend(
        1, [part_shape(1, F32)] + [sum_shape] * 2, [], own_queries, own_stats, *keys, *sums
    )
    dq_parts = [None] * count_ka
    *dq_first, dq_parts[0] = add(dq_own, dq_back, early, (2, 1))
    dq_halves = [turn(part, half) for part in dq_first]
    late_stats, _ = lax.optimization_barrier((own_stats, dq_first[0]))
    dq_own, kv_own, kv_all = attend(
        2,
        [
            part_shape(2, F32),
            jax.ShapeDtypeStruct(kv_shape, F32),
            jax.ShapeDtypeStruct((count_chip, *kv_shape), BF16),
        ],
        [VMEM(sum_shape.shape, F32)] * 2,
        own_queries, late_stats, *blocks, *keys, *sums,
    )
    for step, tile in zip(late, add(dq_own, dq_back, late, (1,) * len(late))):
        dq_parts[step] = turn(tile, step)
    kv_all, dq_halves[0] = lax.optimization_barrier((kv_all, dq_halves[0]))
    cores = [list(range(core, count_pb, 2)) for core in range(2)]
    kv_parts = lax.all_to_all(kv_all, "pb", 0, 0, axis_index_groups=cores)

    piece_type = BF16 if share == 1 else F32
    piece_shape = (count_ka, TILE + SPARE, 2 * HEAD_DIM)
    totals = pl.pallas_call(
        functools.partial(collect_kernel, (count_chip, count_ka, share)),
        in_specs=in_vmem(4),
        out_specs=in_vmem(1)[0],
        out_shape=jax.ShapeDtypeStruct(piece_shape, piece_type),
        compiler_params=params(24),
        name="collect",
    )(key_gain, value_gain, kv_own, kv_parts)
    first_turns = [dq_parts[step] for step in late]
    totals, first_turns = lax.optimization_barrier((totals, first_turns))
    for step, tile in zip(late, first_turns):
        dq_parts[step] = tile
    pieces = lax.all_to_all(totals, "ka", 0, 0)

    grad_keys, grad_values, gains = pl.pallas_call(
        functools.partial(finish_kernel, (count_ka, share)),
        in_specs=in_vmem(3),
        out_specs=in_vmem(3),
        out_shape=[
            jax.ShapeDtypeStruct(key_rows.shape, BF16),
            jax.ShapeDtypeStruct(key_rows.shape, BF16),
            jax.ShapeDtypeStruct((2, key_rows.shape[1]), F32),
        ],
        scratch_shapes=[VMEM((kv_heads, TILE + SPARE, 2 * HEAD_DIM), F32)],
        compiler_params=params(16),
        name="finish",
    )(key_gain, value_gain, pieces)
    gains = gains + swap(gains, 1)
    first = [dq_parts[0], *dq_halves]
    turned = pl.pallas_call(
        turn_kernel,
        in_specs=in_vmem(len(first)),
        out_specs=in_vmem(len(first)),
        out_shape=[jax.ShapeDtypeStruct(part.shape, BF16) for part in first],
        compiler_params=params(8),
        cost_estimate=pl.CostEstimate(flops=0, bytes_accessed=1 << 22, transcendentals=0),
        name="turn_queries",
    )(*first)
    where = ((0, 0, False), (half, 0, False), (half, heads_dev // 2, False))
    where += tuple((step, 0, True) for step in late)
    grad_queries = pl.pallas_call(
        functools.partial(place_kernel, (count_ka, heads_dev, where)),
        in_specs=in_vmem(len(where)),
        out_specs=pl.BlockSpec(memory_space=pl.ANY),
        out_shape=jax.ShapeDtypeStruct((rows_dev, feat_width), BF16),
        scratch_shapes=[VMEM((TILE, width), BF16)] * len(late) + [pltpu.SemaphoreType.DMA((len(where),))],
        compiler_params=params(16),
        cost_estimate=pl.CostEstimate(flops=0, bytes_accessed=4 * rows_dev * feat_width, transcendentals=0),
        name="place_queries",
    )(*turned, *[dq_parts[step] for step in late])
    return grad_queries, grad_keys, grad_values, gains[0], gains[1]


def solution(mesh):
    placed = (
        P("pb", None),
        P(("pb", "ka"), None),
        P(("pb", "ka"), None),
        P(("pb", "ka"), None),
        P("pb", None),
        P(None, ("pb", "ka")),
        P(),
        P(),
        P(),
        P(),
        P(),
    )
    return jax.shard_map(
        shards,
        mesh=mesh,
        in_specs=placed,
        out_specs=(P(("pb", "ka"), None), P(("pb", "ka"), None), P(("pb", "ka"), None), P(), P()),
        check_vma=False,
    )
```

```python
import functools

import jax
import jax.numpy as jnp
from jax import lax
from jax.experimental import pallas as pl
from jax.experimental.pallas import tpu as pltpu
from jax.sharding import PartitionSpec as P

HEAD_DIM = 128
TILE = 128
SPARE = 16
LOG2E = 1.4426950408889634
ENTRY = 4
PARTS = 4
STAT_TERMS = 2
EARLY = 1
HIDING = 3
LAST_DIMS = (((1,), (1,)), ((), ()))
VMEM = pltpu.VMEM
SMEM = pltpu.SMEM
F32 = jnp.float32
BF16 = jnp.bfloat16


def split_float(x, count):
    terms = []
    for _ in range(count):
        terms.append(x.astype(BF16).astype(F32))
        x = x - terms[-1]
    return terms


def head_rows(heads_dev):
    return -(-heads_dev // 8) * 8


def extra_rows(heads_dev):
    return STAT_TERMS * head_rows(heads_dev)


def prepare_kernel(dims, key_ref, value_ref, attn_ref, grads_ref, lse_ref, *rest):
    count_ka, heads, heads_dev, share = dims
    outs, (attn, grad, lse_pad, delta_pad, sems) = rest[:count_ka], rest[count_ka:]
    _, place_ka = places()
    rows8 = head_rows(heads_dev)
    part_heads = heads // PARTS
    rows = pl.ds(pl.multiple_of(place_ka * TILE, TILE), TILE)
    copies = []
    for part in range(PARTS):
        columns = pl.ds(part * part_heads * HEAD_DIM, part_heads * HEAD_DIM)
        copies.append((
            pltpu.make_async_copy(attn_ref.at[:, columns], attn.at[part], sems.at[0, part]),
            pltpu.make_async_copy(grads_ref.at[rows, columns], grad.at[part], sems.at[1, part]),
        ))
        for copy in copies[-1]:
            copy.start()
    for step in range(count_ka):
        target = lax.rem(place_ka + step, count_ka)
        kv_at = pl.ds(pl.multiple_of(target // share * HEAD_DIM, HEAD_DIM), HEAD_DIM)
        outs[step][:TILE, :HEAD_DIM] = key_ref[:, kv_at]
        outs[step][:TILE, HEAD_DIM:] = value_ref[:, kv_at]
    lanes = lax.broadcasted_iota(jnp.int32, (TILE, TILE), 1)
    columns = jnp.zeros((TILE, TILE), F32)
    for part in range(PARTS):
        for copy in copies[part]:
            copy.wait()
        for head in range(part_heads):
            at = pl.ds(head * HEAD_DIM, HEAD_DIM)
            products = grad[part, :, at].astype(F32) * attn[part, :, at].astype(F32)
            total = jnp.sum(products, axis=1, keepdims=True)
            columns = jnp.where(lanes == part * part_heads + head, total, columns)
    delta_pad[...] = jnp.zeros_like(delta_pad)
    lse_pad[...] = jnp.zeros_like(lse_pad)
    delta_pad[:heads, :] = columns.T[:heads, :]
    lse_pad[:heads, :] = lse_ref[...]
    for step in range(count_ka):
        target = lax.rem(place_ka + step, count_ka)
        head_at = pl.ds(target * heads_dev, rows8)
        both = jnp.concatenate([lse_pad[head_at, :], delta_pad[head_at, :]], axis=1)
        outs[step][TILE:, :] = jnp.concatenate(split_float(both, STAT_TERMS), axis=0).astype(BF16)


def own_heads_kernel(queries_ref, grads_ref, out_ref, sems):
    _, place_ka = places()
    width = out_ref.shape[2]
    columns = pl.ds(pl.multiple_of(place_ka * width, HEAD_DIM), width)
    copies = [
        pltpu.make_async_copy(ref.at[:, columns], out_ref.at[number], sems.at[number])
        for number, ref in enumerate((queries_ref, grads_ref))
    ]
    for copy in copies:
        copy.start()
    for copy in copies:
        copy.wait()


def places():
    return lax.axis_index("pb"), lax.axis_index("ka")


def plan_kernel(dims, order_ref, doc_ref, mask_ref, other_ref, own_ref):
    count_chip, count_ka, order = dims
    place_pb, place_ka = places()

    def walk(table, query_pb, key_pb, steps, units):
        def query_step(turn_q, units):
            step_q = jnp.int32(order[0])
            for number, step in enumerate(order):
                step_q = jnp.where(turn_q == number, step, step_q)
            tile_at = lax.rem(place_ka + step_q, count_ka)
            seq_q = order_ref[query_pb * count_ka + tile_at]
            doc_q = doc_ref[seq_q]

            def collect(number, units):
                for step in range(count_ka):
                    stored = (key_pb ^ (2 * number)) * count_ka + lax.rem(
                        place_ka - step + count_ka, count_ka
                    )
                    seq_k = order_ref[stored]
                    live = (mask_ref[seq_q, seq_k] == 1) & (doc_ref[seq_k] == doc_q) & (seq_q >= seq_k)
                    if table is not None:
                        base = ENTRY * (units + 1)
                        table[base] = turn_q
                        table[base + 1] = tile_at
                        table[base + 2] = number * count_ka + step
                        table[base + 3] = jnp.where(seq_q == seq_k, 0, -TILE)
                    units = units + live.astype(jnp.int32)
                return units

            return lax.fori_loop(0, count_chip, collect, units)

        return lax.fori_loop(*steps, query_step, units)

    def close(table, units):
        base = ENTRY * (units + 1)
        table[base] = 0
        table[base + 1] = 0
        table[base + 2] = 0
        table[base + 3] = TILE
        return (units + 1) // 2

    none = jnp.int32(0)
    other = close(other_ref, walk(other_ref, place_pb ^ 1, place_pb, (0, count_ka), none))
    early = walk(own_ref, place_pb, place_pb, (0, EARLY), none)
    total = close(own_ref, walk(own_ref, place_pb, place_pb, (EARLY, count_ka), early))
    partner = (walk(None, place_pb, place_pb ^ 1, (0, count_ka), none) + 1) // 2
    first = jnp.minimum(jnp.maximum(partner - other, (early + 1) // 2), total)
    other_ref[0] = other
    own_ref[0] = first
    own_ref[1] = jnp.minimum(first + HIDING, total)
    own_ref[2] = total


def attention_kernel(dims, *rest):
    count_chip, count_ka, heads_dev, share, stage = dims
    if stage == 0:
        (other_table, own_table, key_gain_ref, value_gain_ref), rest = rest[:4], rest[4:]
        (other_heads, other_stats), rest = rest[:2], rest[2:]
    else:
        own_table, rest = rest[0], rest[1:]
    (own_heads, own_stats), rest = rest[:2], rest[2:]
    if stage != 1:
        blocks, rest = rest[:count_chip], rest[count_chip:]
    if stage == 0:
        (dq_out, dq_sum, keys, values, keys_t, key_sum, value_sum), rest = rest[:7], rest[7:]
    else:
        (keys, values, keys_t, dq_start, key_start, value_start), rest = rest[:6], rest[6:]
        dq_sum, rest = rest[0], rest[1:]
        if stage == 2:
            kv_outs, rest = rest[:count_chip], rest[count_chip:]
        (key_sum, value_sum), rest = rest[:2], rest[2:]
    own_lse, weights_low, dscores_low = rest[:3]
    _, place_ka = places()
    rows8 = head_rows(heads_dev)
    spare = extra_rows(heads_dev)
    score_scale = HEAD_DIM ** -0.5

    if stage == 0:
        kv_at = pl.ds(pl.multiple_of(place_ka // share * HEAD_DIM, HEAD_DIM), HEAD_DIM)
        key_gain = key_gain_ref[:, kv_at]
        value_gain = value_gain_ref[:, kv_at]
        for number in range(count_chip):
            for step in range(count_ka):
                part = pl.ds(step * TILE, TILE)
                local = number * count_ka + step
                key_tile = (blocks[number][part, :HEAD_DIM].astype(F32) * key_gain).astype(BF16)
                value_tile = (blocks[number][part, HEAD_DIM:].astype(F32) * value_gain).astype(BF16)
                keys[local] = key_tile
                values[local] = value_tile
                keys_t[local] = key_tile.T
        key_sum[...] = jnp.zeros_like(key_sum)
        value_sum[...] = jnp.zeros_like(value_sum)
        dq_sum[...] = jnp.zeros_like(dq_sum)
    else:
        key_sum[...] = key_start[...]
        value_sum[...] = value_start[...]
        dq_sum[...] = dq_start[...]

    reach = (lax.broadcasted_iota(jnp.int32, (TILE, TILE), 1)
             - lax.broadcasted_iota(jnp.int32, (TILE, TILE), 0))
    reach = jnp.concatenate([reach, reach], axis=1)

    def run(table, heads_ref, stats_ref, lse_delta, dq_to, first, last):
        for slot in range(count_ka):
            packed = stats_ref[pl.ds(slot * spare, spare), :].astype(F32)
            terms = [packed[term * rows8:(term + 1) * rows8] for term in range(STAT_TERMS)]
            lse_delta[slot] = sum(terms[1:], terms[0])

        def heads_of(kind, tile_at, heads):
            rows = pl.ds(pl.multiple_of(tile_at * TILE, TILE), TILE)
            return jnp.concatenate(
                [heads_ref[kind, rows, pl.ds(head * HEAD_DIM, HEAD_DIM)] for head in heads], axis=0
            )

        def unit_step(at, carry):
            terms = []
            for lane in range(2):
                base = ENTRY * (2 * at + lane + 1)
                turn_q, tile_at, key_at = table[base], table[base + 1], table[base + 2]
                slot = lax.rem(place_ka - tile_at + count_ka, count_ka)
                allowed = reach >= table[base + 3]
                for head in range(0, heads_dev, 2):
                    part = pl.ds(head * HEAD_DIM, 2 * HEAD_DIM)
                    both = (head, head + 1)
                    scores = lax.dot_general(
                        keys[key_at], heads_of(0, tile_at, both), LAST_DIMS, preferred_element_type=F32
                    )
                    dweights = lax.dot_general(
                        values[key_at], heads_of(1, tile_at, both), LAST_DIMS, preferred_element_type=F32
                    )
                    lse_row, delta_row = [
                        jnp.concatenate(
                            [lse_delta[slot, number:number + 1, lanes] for number in both], axis=1
                        )
                        for lanes in (slice(0, TILE), slice(TILE, 2 * TILE))
                    ]
                    weights = jnp.exp2(scores * (score_scale * LOG2E) - lse_row * LOG2E)
                    weights = jnp.where(allowed, weights, 0.0)
                    weights_low[lane, :, part] = weights.astype(BF16)
                    dscores_low[lane, :, part] = (weights * (dweights - delta_row)).astype(BF16)
                every = range(heads_dev)
                terms.append((
                    turn_q,
                    key_at,
                    jnp.dot(weights_low[lane], heads_of(1, tile_at, every), preferred_element_type=F32),
                    jnp.dot(dscores_low[lane], heads_of(0, tile_at, every), preferred_element_type=F32),
                    jnp.dot(keys_t[key_at], dscores_low[lane], preferred_element_type=F32),
                ))
            for turn_q, key_at, value_term, key_term, dq_term in terms:
                value_sum[key_at] += value_term
                key_sum[key_at] += key_term
                dq_to[turn_q] += dq_term
            return carry

        lax.fori_loop(first, last, unit_step, 0)

    if stage == 0:
        other_lse, dq_other = rest[3:]
        dq_other[...] = jnp.zeros_like(dq_other)
        run(other_table, other_heads, other_stats, other_lse, dq_other, 0, other_table[0])
        for turn_q in range(count_ka):
            dq_out[turn_q] = (dq_other[turn_q] * score_scale).astype(BF16)
    first = own_table[stage - 1] if stage else 0
    run(own_table, own_heads, own_stats, own_lse, dq_sum, first, own_table[stage])
    if stage != 2:
        return

    key_gains = jnp.zeros((8, HEAD_DIM), F32)
    value_gains = jnp.zeros((8, HEAD_DIM), F32)
    for number in range(count_chip):
        for step in range(count_ka):
            part = pl.ds(step * TILE, TILE)
            local = number * count_ka + step
            key_total = key_sum[local] * score_scale
            value_total = value_sum[local]
            kv_outs[number][part, :HEAD_DIM] = key_total.astype(kv_outs[number].dtype)
            kv_outs[number][part, HEAD_DIM:] = value_total.astype(kv_outs[number].dtype)
            key_raw = blocks[number][part, :HEAD_DIM].astype(F32)
            value_raw = blocks[number][part, HEAD_DIM:].astype(F32)
            key_gains += jnp.sum((key_total * key_raw).reshape(TILE // 8, 8, HEAD_DIM), axis=0)
            value_gains += jnp.sum((value_total * value_raw).reshape(TILE // 8, 8, HEAD_DIM), axis=0)
    gains = jnp.concatenate([jnp.sum(key_gains, axis=0, keepdims=True),
                             jnp.sum(value_gains, axis=0, keepdims=True)], axis=1)
    packed = pack_gains(gains)
    for number in range(count_chip):
        kv_outs[number][count_ka * TILE:, :] = packed.astype(kv_outs[number].dtype)


def pack_gains(gains):
    rows = lax.broadcasted_iota(jnp.int32, (SPARE, gains.shape[1]), 0)
    high, middle, low = split_float(gains, 3)
    packed = jnp.where(rows == 0, high, jnp.where(rows == 1, middle, low))
    return jnp.where(rows < 3, packed, 0.0)


def add_kernel(first, part_ref, other_ref, *outs):
    for tile, out_ref in enumerate(outs, first):
        own = part_ref[tile] * HEAD_DIM ** -0.5
        out_ref[...] = (own + other_ref[tile].astype(F32)).astype(BF16)


def collect_kernel(dims, key_gain_ref, value_gain_ref, *rest):
    count_chip, count_ka, share = dims
    parts, outs = rest[:count_chip], rest[count_chip:]
    kv_at = pl.ds(pl.multiple_of(places()[1] // share * HEAD_DIM, HEAD_DIM), HEAD_DIM)
    gain = jnp.concatenate([key_gain_ref[:, kv_at], value_gain_ref[:, kv_at]], axis=1)
    for step in range(count_ka):
        rows = pl.ds(step * TILE, TILE)
        total = parts[0][rows, :]
        for number in range(1, count_chip):
            total = total + parts[number][rows, :].astype(F32)
        if share == 1:
            total = total * gain
        outs[step][:TILE, :] = total.astype(outs[step].dtype)
    spare = pl.ds(count_ka * TILE, SPARE)
    total = parts[0][spare, :]
    for number in range(1, count_chip):
        total = total + parts[number][spare, :].astype(F32)
    packed = pack_gains(jnp.sum(total, axis=0, keepdims=True))
    for step in range(count_ka):
        outs[step][TILE:, :] = packed.astype(outs[step].dtype)


def turn_kernel(*refs):
    half = len(refs) // 2
    for source, target in zip(refs[:half], refs[half:]):
        for head in range(source.shape[1] // HEAD_DIM):
            part = pl.ds(head * HEAD_DIM, HEAD_DIM)
            target[:, part] = source[:, part].T


def place_kernel(dims, gains_ref, other_ref, *rest):
    count_ka, heads_dev, pieces = dims
    dq_parts, rest = rest[:len(pieces)], rest[len(pieces):]
    dq_out, key_gain_out, value_gain_out, *turned, sems = rest
    width = heads_dev * HEAD_DIM
    copies, used = [], 0
    for number, ((step, late), piece) in enumerate(zip(pieces, dq_parts)):
        source = lax.rem(places()[1] - step + count_ka, count_ka)
        columns = pl.ds(pl.multiple_of(source * width, HEAD_DIM), width)
        if late:
            turn_kernel(piece, turned[used])
            piece, used = turned[used], used + 1
        copies.append(pltpu.make_async_copy(piece, dq_out.at[:, columns], sems.at[number]))
        copies[-1].start()
    key_gain_out[...] = gains_ref[0:1, :] + other_ref[0:1, :]
    value_gain_out[...] = gains_ref[1:2, :] + other_ref[1:2, :]
    for copy in copies:
        copy.wait()


def finish_kernel(dims, key_gain_ref, value_gain_ref, *rest):
    count_ka, share = dims
    pieces, rest = rest[:count_ka], rest[count_ka:]
    dk_out, dv_out, gains_out, sums = rest
    _, place_ka = places()
    sums[...] = jnp.zeros_like(sums)
    for step in range(count_ka):
        source = lax.rem(place_ka + step, count_ka)
        sums[source // share] += pieces[step][...].astype(F32)
    for head in range(count_ka // share):
        part = pl.ds(head * HEAD_DIM, HEAD_DIM)
        key_total = sums[head, :TILE, :HEAD_DIM]
        value_total = sums[head, :TILE, HEAD_DIM:]
        if share > 1:
            key_total = key_total * key_gain_ref[:, part]
            value_total = value_total * value_gain_ref[:, part]
        dk_out[:, part] = key_total.astype(BF16)
        dv_out[:, part] = value_total.astype(BF16)
        gains = jnp.sum(sums[head, TILE:, :], axis=0, keepdims=True)
        gains_out[0:1, part] = gains[:, :HEAD_DIM]
        gains_out[1:2, part] = gains[:, HEAD_DIM:]


def in_vmem(count):
    return [pl.BlockSpec(memory_space=VMEM)] * count


def in_smem(count):
    return [pl.BlockSpec(memory_space=SMEM)] * count


def anywhere(count):
    return [pl.BlockSpec(memory_space=pl.ANY)] * count


def params(mib):
    return pltpu.CompilerParams(vmem_limit_bytes=mib * 1024 * 1024)


def shards(
    queries,
    key_rows,
    values,
    attn_out,
    grad_out,
    log_sums,
    key_gain,
    value_gain,
    doc_ids,
    tile_mask,
    block_order,
):
    count_pb = lax.axis_size("pb")
    count_ka = lax.axis_size("ka")
    rows_dev = key_rows.shape[0]
    query_rows = queries.shape[0]
    heads = log_sums.shape[0]
    feat_width = queries.shape[1]
    kv_heads = key_rows.shape[1] // HEAD_DIM
    heads_dev = heads // count_ka
    share = count_ka // kv_heads
    assert rows_dev == TILE and share * kv_heads == count_ka and count_pb & (count_pb - 1) == 0
    width = heads_dev * HEAD_DIM
    key_gain = key_gain.reshape(1, -1)
    value_gain = value_gain.reshape(1, -1)

    spare = extra_rows(heads_dev)
    count_chip = count_pb // 2

    def swap(array, number):
        return lax.ppermute(array, "pb", [(at, at ^ number) for at in range(count_pb)])

    def turn(array, step):
        return lax.ppermute(array, "ka", [(at, (at + step) % count_ka) for at in range(count_ka)])

    sends = pl.pallas_call(
        functools.partial(prepare_kernel, (count_ka, heads, heads_dev, share)),
        in_specs=in_vmem(2) + anywhere(2) + in_vmem(1),
        out_specs=in_vmem(count_ka),
        out_shape=[jax.ShapeDtypeStruct((TILE + spare, 2 * HEAD_DIM), BF16)] * count_ka,
        scratch_shapes=[VMEM((PARTS, TILE, feat_width // PARTS), BF16)] * 2
        + [VMEM((heads + 8, TILE), F32)] * 2
        + [pltpu.SemaphoreType.DMA((2, PARTS))],
        compiler_params=params(57),
        name="prepare",
    )(key_rows, values, attn_out, grad_out, log_sums)
    messages = [sends[0]] + [turn(sends[step], step) for step in range(1, count_ka)]

    later_queries, _ = lax.optimization_barrier((queries, sends[0]))
    own_queries = pl.pallas_call(
        own_heads_kernel,
        in_specs=anywhere(2),
        out_specs=in_vmem(1)[0],
        out_shape=jax.ShapeDtypeStruct((2, query_rows, width), BF16),
        scratch_shapes=[pltpu.SemaphoreType.DMA((2,))],
        compiler_params=params(48),
        cost_estimate=pl.CostEstimate(flops=0, bytes_accessed=8 * query_rows * width, transcendentals=0),
        name="own_heads",
    )(later_queries, grad_out)
    messages, own_queries = lax.optimization_barrier((messages, own_queries))
    other_queries = swap(own_queries, 1)
    own_block = jnp.concatenate([message[:TILE] for message in messages], axis=0)
    own_stats = jnp.concatenate([message[TILE:] for message in messages], axis=0)
    blocks = [own_block] + [swap(own_block, 2 * number) for number in range(1, count_chip)]
    other_stats = swap(own_stats, 1)
    later_order, _ = lax.optimization_barrier((block_order, own_block))

    key_tiles = count_chip * count_ka
    sum_shape = jax.ShapeDtypeStruct((key_tiles, TILE, HEAD_DIM), F32)
    key_shape = jax.ShapeDtypeStruct((key_tiles, TILE, HEAD_DIM), BF16)
    kv_shape = (query_rows + SPARE, 2 * HEAD_DIM)
    half = count_ka // 2
    late = tuple(step for step in range(count_ka) if step != half)
    order = (half,) + late
    table_shape = jax.ShapeDtypeStruct((ENTRY * (2 + count_ka * key_tiles),), jnp.int32)
    other_table, own_table = pl.pallas_call(
        functools.partial(plan_kernel, (count_chip, count_ka, order)),
        in_specs=in_smem(3),
        out_specs=in_smem(2),
        out_shape=[table_shape] * 2,
        cost_estimate=pl.CostEstimate(flops=0, bytes_accessed=1 << 22, transcendentals=0),
        name="plan",
    )(later_order, doc_ids, tile_mask)

    def attend(stage, tables, outs, scratch, *operands):
        return pl.pallas_call(
            functools.partial(attention_kernel, (count_chip, count_ka, heads_dev, share, stage)),
            in_specs=in_smem(len(tables)) + in_vmem(len(operands)),
            out_specs=in_vmem(len(outs)),
            out_shape=outs,
            scratch_shapes=scratch[0] + [
                VMEM((count_ka, head_rows(heads_dev), 2 * TILE), F32),
                VMEM((2, TILE, width), BF16),
                VMEM((2, TILE, width), BF16),
            ] + scratch[1],
            compiler_params=params(20 + key_tiles // 2),
            cost_estimate=pl.CostEstimate(
                flops=5 * count_ka * key_tiles * TILE * TILE * width if stage < 2 else 0,
                bytes_accessed=1 << 20 if stage < 2 else 0,
                transcendentals=0,
            ),
            name=("attention_first", "attention_second", "attention_third")[stage],
        )(*tables, *operands)

    dq_shape = (count_ka, HEAD_DIM, width)
    dq_sums = jax.ShapeDtypeStruct(dq_shape, F32)

    def add(part, other, first, count):
        return pl.pallas_call(
            functools.partial(add_kernel, first),
            in_specs=in_vmem(2),
            out_specs=in_vmem(count),
            out_shape=[jax.ShapeDtypeStruct((HEAD_DIM, width), BF16)] * count,
            compiler_params=params(4 * count_ka),
            name="add_queries",
        )(part, other)

    dq_other, dq_own, *state = attend(
        0, (other_table, own_table),
        [jax.ShapeDtypeStruct(dq_shape, BF16), dq_sums] + [key_shape] * 3 + [sum_shape] * 2,
        ([], [VMEM((count_ka, head_rows(heads_dev), 2 * TILE), F32), VMEM(dq_shape, F32)]),
        key_gain, value_gain, other_queries, other_stats, own_queries, own_stats, *blocks,
    )
    keys, sums = state[:3], state[3:]
    dq_back = swap(dq_other, 1)
    dq_own, *sums = attend(
        1, (own_table,), [dq_sums] + [sum_shape] * 2, ([], []), own_queries, own_stats, *keys, dq_own, *sums
    )
    dq_parts = [None] * count_ka
    dq_first, = add(dq_own, dq_back, 0, 1)
    dq_parts[half] = turn(dq_first, half)
    late_stats, _ = lax.optimization_barrier((own_stats, dq_first))
    dq_own, *kv_own = attend(
        2, (own_table,),
        [dq_sums, jax.ShapeDtypeStruct(kv_shape, F32)]
        + [jax.ShapeDtypeStruct(kv_shape, BF16)] * (count_chip - 1),
        ([VMEM(sum_shape.shape, F32)] * 2, []),
        own_queries, late_stats, *blocks, *keys, dq_own, *sums,
    )
    dq_own, dq_parts[half] = lax.optimization_barrier((dq_own, dq_parts[half]))
    for step, tile in zip(late, add(dq_own, dq_back, EARLY, len(late))):
        dq_parts[step] = turn(tile, step) if step else tile
    kv_parts = [kv_own[0]] + [swap(kv_own[number], 2 * number) for number in range(1, count_chip)]

    piece_type = BF16 if share == 1 else F32
    piece_shape = (TILE + SPARE, 2 * HEAD_DIM)
    totals = pl.pallas_call(
        functools.partial(collect_kernel, (count_chip, count_ka, share)),
        in_specs=in_vmem(2 + count_chip),
        out_specs=in_vmem(count_ka),
        out_shape=[jax.ShapeDtypeStruct(piece_shape, piece_type)] * count_ka,
        compiler_params=params(24),
        name="collect",
    )(key_gain, value_gain, *kv_parts)
    pieces = [totals[0]] + [turn(totals[step], -step) for step in range(1, count_ka)]

    grad_keys, grad_values, gains = pl.pallas_call(
        functools.partial(finish_kernel, (count_ka, share)),
        in_specs=in_vmem(2 + count_ka),
        out_specs=in_vmem(3),
        out_shape=[
            jax.ShapeDtypeStruct(key_rows.shape, BF16),
            jax.ShapeDtypeStruct(key_rows.shape, BF16),
            jax.ShapeDtypeStruct((2, key_rows.shape[1]), F32),
        ],
        scratch_shapes=[VMEM((kv_heads, TILE + SPARE, 2 * HEAD_DIM), F32)],
        compiler_params=params(16),
        name="finish",
    )(key_gain, value_gain, *pieces)
    first = [dq_parts[0], dq_parts[half]]
    turned = pl.pallas_call(
        turn_kernel,
        in_specs=in_vmem(len(first)),
        out_specs=in_vmem(len(first)),
        out_shape=[jax.ShapeDtypeStruct(part.shape, BF16) for part in first],
        compiler_params=params(8),
        cost_estimate=pl.CostEstimate(flops=0, bytes_accessed=1 << 22, transcendentals=0),
        name="turn_queries",
    )(*first)
    later = [step for step in late if step]
    where = ((0, False), (half, False)) + tuple((step, True) for step in later)
    grad_queries, grad_key_gain, grad_value_gain = pl.pallas_call(
        functools.partial(place_kernel, (count_ka, heads_dev, where)),
        in_specs=in_vmem(2 + len(where)),
        out_specs=anywhere(1) + in_vmem(2),
        out_shape=[jax.ShapeDtypeStruct((rows_dev, feat_width), BF16)]
        + [jax.ShapeDtypeStruct(key_gain.shape, F32)] * 2,
        scratch_shapes=[VMEM((TILE, width), BF16)] * len(later) + [pltpu.SemaphoreType.DMA((len(where),))],
        compiler_params=params(16),
        cost_estimate=pl.CostEstimate(flops=0, bytes_accessed=4 * rows_dev * feat_width, transcendentals=0),
        name="place_queries",
    )(gains, swap(gains, 1), *turned, *[dq_parts[step] for step in later])
    return grad_queries, grad_keys, grad_values, grad_key_gain.reshape(-1), grad_value_gain.reshape(-1)


def solution(mesh):
    placed = (
        P("pb", None),
        P(("pb", "ka"), None),
        P(("pb", "ka"), None),
        P(("pb", "ka"), None),
        P("pb", None),
        P(None, ("pb", "ka")),
        P(),
        P(),
        P(),
        P(),
        P(),
    )
    return jax.shard_map(
        shards,
        mesh=mesh,
        in_specs=placed,
        out_specs=(P(("pb", "ka"), None), P(("pb", "ka"), None), P(("pb", "ka"), None), P(), P()),
        check_vma=False,
    )
```

```python
import functools

import jax
import jax.numpy as jnp
from jax import lax
from jax.experimental import pallas as pl
from jax.experimental.pallas import tpu as pltpu
from jax.sharding import PartitionSpec as P

HEAD_DIM = 128
TILE = 128
SPARE = 16
LOG2E = 1.4426950408889634
ENTRY = 4
PARTS = 4
STAT_TERMS = 2
EARLY = 1
LAST_DIMS = (((1,), (1,)), ((), ()))
VMEM = pltpu.VMEM
SMEM = pltpu.SMEM
F32 = jnp.float32
BF16 = jnp.bfloat16


def split_float(x, count):
    terms = []
    for _ in range(count):
        terms.append(x.astype(BF16).astype(F32))
        x = x - terms[-1]
    return terms


def head_rows(heads_dev):
    return -(-heads_dev // 8) * 8


def extra_rows(heads_dev):
    return STAT_TERMS * head_rows(heads_dev)


def prepare_kernel(dims, key_ref, value_ref, attn_ref, grads_ref, lse_ref, *rest):
    count_ka, heads, heads_dev, share = dims
    outs, (attn, grad, lse_pad, delta_pad, sems) = rest[:count_ka], rest[count_ka:]
    _, place_ka = places()
    rows8 = head_rows(heads_dev)
    part_heads = heads // PARTS
    rows = pl.ds(pl.multiple_of(place_ka * TILE, TILE), TILE)
    copies = []
    for part in range(PARTS):
        columns = pl.ds(part * part_heads * HEAD_DIM, part_heads * HEAD_DIM)
        copies.append((
            pltpu.make_async_copy(attn_ref.at[:, columns], attn.at[part], sems.at[0, part]),
            pltpu.make_async_copy(grads_ref.at[rows, columns], grad.at[part], sems.at[1, part]),
        ))
        for copy in copies[-1]:
            copy.start()
    for step in range(count_ka):
        target = lax.rem(place_ka + step, count_ka)
        kv_at = pl.ds(pl.multiple_of(target // share * HEAD_DIM, HEAD_DIM), HEAD_DIM)
        outs[step][:TILE, :HEAD_DIM] = key_ref[:, kv_at]
        outs[step][:TILE, HEAD_DIM:] = value_ref[:, kv_at]
    lanes = lax.broadcasted_iota(jnp.int32, (TILE, TILE), 1)
    columns = jnp.zeros((TILE, TILE), F32)
    for part in range(PARTS):
        for copy in copies[part]:
            copy.wait()
        for head in range(part_heads):
            at = pl.ds(head * HEAD_DIM, HEAD_DIM)
            products = grad[part, :, at].astype(F32) * attn[part, :, at].astype(F32)
            total = jnp.sum(products, axis=1, keepdims=True)
            columns = jnp.where(lanes == part * part_heads + head, total, columns)
    delta_pad[...] = jnp.zeros_like(delta_pad)
    lse_pad[...] = jnp.zeros_like(lse_pad)
    delta_pad[:heads, :] = columns.T[:heads, :]
    lse_pad[:heads, :] = lse_ref[...]
    for step in range(count_ka):
        target = lax.rem(place_ka + step, count_ka)
        head_at = pl.ds(target * heads_dev, rows8)
        both = jnp.concatenate([lse_pad[head_at, :], delta_pad[head_at, :]], axis=1)
        outs[step][TILE:, :] = jnp.concatenate(split_float(both, STAT_TERMS), axis=0).astype(BF16)


def own_heads_kernel(queries_ref, grads_ref, out_ref, sems):
    _, place_ka = places()
    width = out_ref.shape[2]
    columns = pl.ds(pl.multiple_of(place_ka * width, HEAD_DIM), width)
    copies = [
        pltpu.make_async_copy(ref.at[:, columns], out_ref.at[number], sems.at[number])
        for number, ref in enumerate((queries_ref, grads_ref))
    ]
    for copy in copies:
        copy.start()
    for copy in copies:
        copy.wait()


def places():
    return lax.axis_index("pb"), lax.axis_index("ka")


def own_start(key_tiles, count_ka):
    return 3 + count_ka * key_tiles


def plan_kernel(dims, order_ref, doc_ref, mask_ref, table):
    count_chip, count_ka, order = dims
    place_pb, place_ka = places()
    own_at = own_start(count_chip * count_ka, count_ka)

    def walk(start, query_pb, key_pb, steps, units):
        def query_step(turn_q, units):
            step_q = jnp.int32(order[0])
            for number, step in enumerate(order):
                step_q = jnp.where(turn_q == number, step, step_q)
            tile_at = lax.rem(place_ka + step_q, count_ka)
            seq_q = order_ref[query_pb * count_ka + tile_at]
            doc_q = doc_ref[seq_q]

            def collect(number, units):
                for step in range(count_ka):
                    stored = (key_pb ^ (2 * number)) * count_ka + lax.rem(
                        place_ka - step + count_ka, count_ka
                    )
                    seq_k = order_ref[stored]
                    live = (mask_ref[seq_q, seq_k] == 1) & (doc_ref[seq_k] == doc_q) & (seq_q >= seq_k)
                    if start is not None:
                        base = ENTRY * (start + units)
                        table[base] = turn_q
                        table[base + 1] = tile_at
                        table[base + 2] = number * count_ka + step
                        table[base + 3] = jnp.where(seq_q == seq_k, 0, -TILE)
                    units = units + live.astype(jnp.int32)
                return units

            return lax.fori_loop(0, count_chip, collect, units)

        return lax.fori_loop(*steps, query_step, units)

    def close(start, units):
        base = ENTRY * (start + units)
        table[base] = 0
        table[base + 1] = 0
        table[base + 2] = 0
        table[base + 3] = TILE
        return (units + 1) // 2

    def steps_of(units):
        return (units + 1) // 2

    none = jnp.int32(0)
    sibling = place_pb ^ 1
    other_first = walk(2, place_pb, sibling, (0, EARLY), none)
    other = close(2, walk(2, place_pb, sibling, (EARLY, count_ka), other_first))
    own_first = walk(own_at, place_pb, place_pb, (0, EARLY), none)
    own = close(own_at, walk(own_at, place_pb, place_pb, (EARLY, count_ka), own_first))
    there = steps_of(walk(None, sibling, sibling, (0, EARLY), none))
    there = there + steps_of(walk(None, sibling, place_pb, (0, count_ka), none))
    lead = jnp.maximum(there - other - steps_of(own_first), 0)
    table[0] = steps_of(own_first)
    table[1] = jnp.minimum(steps_of(own_first) + lead, own)
    table[2] = own
    table[ENTRY] = steps_of(other_first)
    table[ENTRY + 1] = other


def attention_kernel(dims, *rest):
    count_chip, count_ka, heads_dev, share, stage = dims
    table, rest = rest[0], rest[1:]
    if stage < 2:
        (key_gain_ref, value_gain_ref), rest = rest[:2], rest[2:]
    (heads_ref, stats_ref), rest = rest[:2], rest[2:]
    if stage < 2:
        blocks, rest = rest[:count_chip], rest[count_chip:]
    if stage == 0:
        (dq_sum, *own), rest = rest[:6], rest[6:]
    elif stage == 1:
        (dq_start, dq_sum, *dq_halves), other, rest = rest[:4], rest[4:9], rest[9:]
    elif stage == 2:
        (dq_start, *own_start_refs), rest = rest[:6], rest[6:]
        other_refs, rest = rest[:5], rest[5:]
        (dq_sum, *own_sums, kv_other, other_key_sum, other_value_sum), rest = rest[:6], rest[6:]
        own = own_start_refs[:3] + own_sums
        other = other_refs[:3] + (other_key_sum, other_value_sum)
    else:
        (dq_start, *own_start_refs), rest = rest[:6], rest[6:]
        dq_outs, rest = rest[:count_ka - EARLY], rest[count_ka - EARLY:]
        (*own_sums, dq_sum), rest = rest[:3], rest[3:]
        own = own_start_refs[:3] + own_sums
    lse_delta, weights_low, dscores_low = rest
    _, place_ka = places()
    rows8 = head_rows(heads_dev)
    spare = extra_rows(heads_dev)
    score_scale = HEAD_DIM ** -0.5

    if stage < 2:
        kv_at = pl.ds(pl.multiple_of(place_ka // share * HEAD_DIM, HEAD_DIM), HEAD_DIM)
        key_gain = key_gain_ref[:, kv_at]
        value_gain = value_gain_ref[:, kv_at]
        keys, values, keys_t, key_sum, value_sum = other if stage else own
        for number in range(count_chip):
            for step in range(count_ka):
                part = pl.ds(step * TILE, TILE)
                local = number * count_ka + step
                key_tile = (blocks[number][part, :HEAD_DIM].astype(F32) * key_gain).astype(BF16)
                value_tile = (blocks[number][part, HEAD_DIM:].astype(F32) * value_gain).astype(BF16)
                keys[local] = key_tile
                values[local] = value_tile
                keys_t[local] = key_tile.T
        key_sum[...] = jnp.zeros_like(key_sum)
        value_sum[...] = jnp.zeros_like(value_sum)
    else:
        for target, source in zip(own_sums, own_start_refs[3:]):
            target[...] = source[...]
    if stage == 0:
        dq_sum[...] = jnp.zeros_like(dq_sum)
    else:
        dq_sum[...] = dq_start[...]
    if stage == 2:
        other_key_sum[...] = other_refs[3][...]
        other_value_sum[...] = other_refs[4][...]

    for slot in range(count_ka):
        packed = stats_ref[pl.ds(slot * spare, spare), :].astype(F32)
        terms = [packed[term * rows8:(term + 1) * rows8] for term in range(STAT_TERMS)]
        total = sum(terms[1:], terms[0])
        lse_delta[slot, :, :TILE] = total[:, :TILE] * LOG2E
        lse_delta[slot, :, TILE:] = total[:, TILE:]

    reach = (lax.broadcasted_iota(jnp.int32, (TILE, TILE), 1)
             - lax.broadcasted_iota(jnp.int32, (TILE, TILE), 0))
    reach = jnp.concatenate([reach, reach], axis=1)

    def run(start, refs, first, last):
        keys, values, keys_t, key_sum, value_sum = refs

        def heads_of(kind, tile_at, heads):
            rows = pl.ds(pl.multiple_of(tile_at * TILE, TILE), TILE)
            return jnp.concatenate(
                [heads_ref[kind, rows, pl.ds(head * HEAD_DIM, HEAD_DIM)] for head in heads], axis=0
            )

        def unit_step(at, carry):
            terms = []
            for lane in range(2):
                base = ENTRY * (start + 2 * at + lane)
                turn_q, tile_at, key_at = table[base], table[base + 1], table[base + 2]
                slot = lax.rem(place_ka - tile_at + count_ka, count_ka)
                allowed = reach >= table[base + 3]
                for head in range(0, heads_dev, 2):
                    part = pl.ds(head * HEAD_DIM, 2 * HEAD_DIM)
                    both = (head, head + 1)
                    scores = lax.dot_general(
                        keys[key_at], heads_of(0, tile_at, both), LAST_DIMS, preferred_element_type=F32
                    )
                    dweights = lax.dot_general(
                        values[key_at], heads_of(1, tile_at, both), LAST_DIMS, preferred_element_type=F32
                    )
                    lse_row, delta_row = [
                        jnp.concatenate(
                            [lse_delta[slot, number:number + 1, lanes] for number in both], axis=1
                        )
                        for lanes in (slice(0, TILE), slice(TILE, 2 * TILE))
                    ]
                    weights = jnp.exp2(scores * (score_scale * LOG2E) - lse_row)
                    weights = jnp.where(allowed, weights, 0.0)
                    weights_low[lane, :, part] = weights.astype(BF16)
                    dscores_low[lane, :, part] = (weights * (dweights - delta_row)).astype(BF16)
                every = range(heads_dev)
                terms.append((
                    turn_q,
                    key_at,
                    jnp.dot(weights_low[lane], heads_of(1, tile_at, every), preferred_element_type=F32),
                    jnp.dot(dscores_low[lane], heads_of(0, tile_at, every), preferred_element_type=F32),
                    jnp.dot(keys_t[key_at], dscores_low[lane], preferred_element_type=F32),
                ))
            for turn_q, key_at, value_term, key_term, dq_term in terms:
                value_sum[key_at] += value_term
                key_sum[key_at] += key_term
                dq_sum[turn_q] += dq_term
            return carry

        lax.fori_loop(first, last, unit_step, 0)

    own_at = own_start(count_chip * count_ka, count_ka)
    if stage == 0:
        run(own_at, own, 0, table[0])
    elif stage == 1:
        run(2, other, 0, table[ENTRY])
        for number, dq_half in enumerate(dq_halves):
            part = pl.ds(number * dq_half.shape[1], dq_half.shape[1])
            dq_half[...] = (dq_sum[0, :, part] * score_scale).astype(BF16)
    elif stage == 2:
        run(2, other, table[ENTRY], table[ENTRY + 1])
        run(own_at, own, table[0], table[1])
        for local in range(count_chip * count_ka):
            part = pl.ds(local * TILE, TILE)
            kv_other[part, :HEAD_DIM] = (other_key_sum[local] * score_scale).astype(BF16)
            kv_other[part, HEAD_DIM:] = other_value_sum[local].astype(BF16)
    else:
        run(own_at, own, table[1], table[2])
        for number, dq_out in enumerate(dq_outs, EARLY):
            dq_out[...] = (dq_sum[number] * score_scale).astype(BF16)


def merge_kernel(dims, key_sum, value_sum, kv_back, *rest):
    count_chip, count_ka = dims
    blocks, kv_outs = rest[:count_chip], rest[count_chip:]
    key_gains = jnp.zeros((8, HEAD_DIM), F32)
    value_gains = jnp.zeros((8, HEAD_DIM), F32)
    for number in range(count_chip):
        for step in range(count_ka):
            local = number * count_ka + step
            there = pl.ds(local * TILE, TILE)
            key_total = key_sum[local] * HEAD_DIM ** -0.5 + kv_back[there, :HEAD_DIM].astype(F32)
            value_total = value_sum[local] + kv_back[there, HEAD_DIM:].astype(F32)
            out_ref = kv_outs[number]
            part = pl.ds(step * TILE, TILE)
            out_ref[part, :HEAD_DIM] = key_total.astype(out_ref.dtype)
            out_ref[part, HEAD_DIM:] = value_total.astype(out_ref.dtype)
            key_raw = blocks[number][part, :HEAD_DIM].astype(F32)
            value_raw = blocks[number][part, HEAD_DIM:].astype(F32)
            key_gains += jnp.sum((key_total * key_raw).reshape(TILE // 8, 8, HEAD_DIM), axis=0)
            value_gains += jnp.sum((value_total * value_raw).reshape(TILE // 8, 8, HEAD_DIM), axis=0)
    gains = jnp.concatenate([jnp.sum(key_gains, axis=0, keepdims=True),
                             jnp.sum(value_gains, axis=0, keepdims=True)], axis=1)
    packed = pack_gains(gains)
    for out_ref in kv_outs:
        out_ref[count_ka * TILE:, :] = packed.astype(out_ref.dtype)


def pack_gains(gains):
    rows = lax.broadcasted_iota(jnp.int32, (SPARE, gains.shape[1]), 0)
    high, middle, low = split_float(gains, 3)
    packed = jnp.where(rows == 0, high, jnp.where(rows == 1, middle, low))
    return jnp.where(rows < 3, packed, 0.0)


def add_parts(parts, rows):
    total = parts[0][rows, :]
    for part in parts[1:]:
        total = total + part[rows, :].astype(F32)
    return total


def own_gain(key_gain_ref, value_gain_ref, share):
    kv_at = pl.ds(pl.multiple_of(places()[1] // share * HEAD_DIM, HEAD_DIM), HEAD_DIM)
    return jnp.concatenate([key_gain_ref[:, kv_at], value_gain_ref[:, kv_at]], axis=1)


def collect_kernel(dims, key_gain_ref, value_gain_ref, *rest):
    count_chip, count_ka, share = dims
    parts, outs = rest[:count_chip], rest[count_chip:]
    gain = own_gain(key_gain_ref, value_gain_ref, share)
    total = add_parts(parts, pl.ds(count_ka * TILE, SPARE))
    packed = pack_gains(jnp.sum(total, axis=0, keepdims=True))
    for step, out_ref in enumerate(outs):
        total = add_parts(parts, pl.ds(step * TILE, TILE))
        if share == 1:
            total = total * gain
        out_ref[:TILE, :] = total.astype(out_ref.dtype)
        out_ref[TILE:, :] = packed.astype(out_ref.dtype)


def place_kernel(dims, *rest):
    count_ka, heads_dev, where = dims
    pieces, (dq_out, turned, sems) = rest[:len(where)], rest[len(where):]
    copies = []
    for number, ((step, first), piece) in enumerate(zip(where, pieces)):
        source = lax.rem(places()[1] - step + count_ka, count_ka)
        columns = pl.ds(pl.multiple_of((source * heads_dev + first) * HEAD_DIM, HEAD_DIM), piece.shape[1])
        here = pl.ds(first * HEAD_DIM, piece.shape[1])
        for head in range(piece.shape[1] // HEAD_DIM):
            part = pl.ds(head * HEAD_DIM, HEAD_DIM)
            turned[step, :, pl.ds((first + head) * HEAD_DIM, HEAD_DIM)] = piece[:, part].T
        copies.append(pltpu.make_async_copy(turned.at[step, :, here], dq_out.at[:, columns], sems.at[number]))
        copies[-1].start()
    for copy in copies:
        copy.wait()


def gains_kernel(gains_ref, other_ref, key_gain_out, value_gain_out):
    key_gain_out[...] = gains_ref[0:1, :] + other_ref[0:1, :]
    value_gain_out[...] = gains_ref[1:2, :] + other_ref[1:2, :]


def finish_kernel(dims, key_gain_ref, value_gain_ref, *rest):
    count_ka, share = dims
    pieces, rest = rest[:count_ka], rest[count_ka:]
    dk_out, dv_out, gains_out, sums = rest
    _, place_ka = places()
    sums[...] = jnp.zeros_like(sums)
    for step in range(count_ka):
        source = lax.rem(place_ka + step, count_ka)
        sums[source // share] += pieces[step][...].astype(F32)
    for head in range(count_ka // share):
        part = pl.ds(head * HEAD_DIM, HEAD_DIM)
        key_total = sums[head, :TILE, :HEAD_DIM]
        value_total = sums[head, :TILE, HEAD_DIM:]
        if share > 1:
            key_total = key_total * key_gain_ref[:, part]
            value_total = value_total * value_gain_ref[:, part]
        dk_out[:, part] = key_total.astype(BF16)
        dv_out[:, part] = value_total.astype(BF16)
        gains = jnp.sum(sums[head, TILE:, :], axis=0, keepdims=True)
        gains_out[0:1, part] = gains[:, :HEAD_DIM]
        gains_out[1:2, part] = gains[:, HEAD_DIM:]


def in_vmem(count):
    return [pl.BlockSpec(memory_space=VMEM)] * count


def in_smem(count):
    return [pl.BlockSpec(memory_space=SMEM)] * count


def anywhere(count):
    return [pl.BlockSpec(memory_space=pl.ANY)] * count


def params(mib):
    return pltpu.CompilerParams(vmem_limit_bytes=mib * 1024 * 1024)


def shards(
    queries,
    key_rows,
    values,
    attn_out,
    grad_out,
    log_sums,
    key_gain,
    value_gain,
    doc_ids,
    tile_mask,
    block_order,
):
    count_pb = lax.axis_size("pb")
    count_ka = lax.axis_size("ka")
    rows_dev = key_rows.shape[0]
    query_rows = queries.shape[0]
    heads = log_sums.shape[0]
    feat_width = queries.shape[1]
    kv_heads = key_rows.shape[1] // HEAD_DIM
    heads_dev = heads // count_ka
    share = count_ka // kv_heads
    assert rows_dev == TILE and share * kv_heads == count_ka and count_pb & (count_pb - 1) == 0
    width = heads_dev * HEAD_DIM
    key_gain = key_gain.reshape(1, -1)
    value_gain = value_gain.reshape(1, -1)

    spare = extra_rows(heads_dev)
    count_chip = count_pb // 2

    def swap(array, number):
        return lax.ppermute(array, "pb", [(at, at ^ number) for at in range(count_pb)])

    def turn(array, step):
        return lax.ppermute(array, "ka", [(at, (at + step) % count_ka) for at in range(count_ka)])

    sends = pl.pallas_call(
        functools.partial(prepare_kernel, (count_ka, heads, heads_dev, share)),
        in_specs=in_vmem(2) + anywhere(2) + in_vmem(1),
        out_specs=in_vmem(count_ka),
        out_shape=[jax.ShapeDtypeStruct((TILE + spare, 2 * HEAD_DIM), BF16)] * count_ka,
        scratch_shapes=[VMEM((PARTS, TILE, feat_width // PARTS), BF16)] * 2
        + [VMEM((heads + 8, TILE), F32)] * 2
        + [pltpu.SemaphoreType.DMA((2, PARTS))],
        compiler_params=params(57),
        name="prepare",
    )(key_rows, values, attn_out, grad_out, log_sums)
    messages = [sends[0]] + [turn(sends[step], step) for step in range(1, count_ka)]

    later_queries, _ = lax.optimization_barrier((queries, sends[0]))
    own_queries = pl.pallas_call(
        own_heads_kernel,
        in_specs=anywhere(2),
        out_specs=in_vmem(1)[0],
        out_shape=jax.ShapeDtypeStruct((2, query_rows, width), BF16),
        scratch_shapes=[pltpu.SemaphoreType.DMA((2,))],
        compiler_params=params(48),
        cost_estimate=pl.CostEstimate(flops=0, bytes_accessed=8 * query_rows * width, transcendentals=0),
        name="own_heads",
    )(later_queries, grad_out)
    messages, own_queries = lax.optimization_barrier((messages, own_queries))
    own_block = jnp.concatenate([message[:TILE] for message in messages], axis=0)
    blocks = [own_block] + [swap(own_block, 2 * number) for number in range(1, count_chip)]
    other_blocks = [swap(block, 1) for block in blocks]
    own_stats = jnp.concatenate([message[TILE:] for message in messages], axis=0)
    later_order, _ = lax.optimization_barrier((block_order, own_block))

    key_tiles = count_chip * count_ka
    sum_shape = jax.ShapeDtypeStruct((key_tiles, TILE, HEAD_DIM), F32)
    key_shape = jax.ShapeDtypeStruct((key_tiles, TILE, HEAD_DIM), BF16)
    kv_shape = (query_rows + SPARE, 2 * HEAD_DIM)
    half = count_ka // 2
    late = tuple(step for step in range(count_ka) if step != half)
    order = (half,) + late
    entries = own_start(key_tiles, count_ka) + 1 + count_ka * key_tiles
    table = pl.pallas_call(
        functools.partial(plan_kernel, (count_chip, count_ka, order)),
        in_specs=in_smem(3),
        out_specs=in_smem(1)[0],
        out_shape=jax.ShapeDtypeStruct((ENTRY * entries,), jnp.int32),
        cost_estimate=pl.CostEstimate(flops=0, bytes_accessed=1 << 22, transcendentals=0),
        name="plan",
    )(later_order, doc_ids, tile_mask)

    def attend(stage, outs, scratch, *operands):
        return pl.pallas_call(
            functools.partial(attention_kernel, (count_chip, count_ka, heads_dev, share, stage)),
            in_specs=in_smem(1) + in_vmem(len(operands)),
            out_specs=in_vmem(len(outs)),
            out_shape=outs,
            scratch_shapes=scratch + [
                VMEM((count_ka, head_rows(heads_dev), 2 * TILE), F32),
                VMEM((2, TILE, width), BF16),
                VMEM((2, TILE, width), BF16),
            ],
            compiler_params=params(14 + key_tiles * 11 // 16),
            cost_estimate=pl.CostEstimate(
                flops=5 * count_ka * key_tiles * TILE * TILE * width, bytes_accessed=1 << 20, transcendentals=0
            ),
            name=("attention_first", "attention_leaving", "attention_other", "attention_own")[stage],
        )(table, *operands)

    dq_sums = jax.ShapeDtypeStruct((count_ka, HEAD_DIM, width), F32)
    dq_tile = jax.ShapeDtypeStruct((HEAD_DIM, width), BF16)
    state = [key_shape] * 3 + [sum_shape] * 2
    dq_sum, *own = attend(0, [dq_sums] + state, [], key_gain, value_gain, own_queries, own_stats, *blocks)
    dq_sum, *dq_halves = attend(
        1, [dq_sums] + [jax.ShapeDtypeStruct((HEAD_DIM, width // 2), BF16)] * 2 + state, [],
        key_gain, value_gain, own_queries, own_stats, *other_blocks, dq_sum,
    )
    dq_parts = [None] * count_ka
    dq_halves, other = [turn(part, half) for part in dq_halves[:2]], dq_halves[2:]
    dq_sum, *own[3:], kv_other = attend(
        2, [dq_sums] + [sum_shape] * 2 + [jax.ShapeDtypeStruct((key_tiles * TILE, 2 * HEAD_DIM), BF16)],
        [VMEM(sum_shape.shape, F32)] * 2,
        own_queries, own_stats, dq_sum, *own, *other,
    )
    kv_other, dq_halves[0] = lax.optimization_barrier((kv_other, dq_halves[0]))
    kv_back = swap(kv_other, 1)
    *dq_late, key_sum, value_sum = attend(
        3, [dq_tile] * len(late) + [sum_shape] * 2, [VMEM(dq_sums.shape, F32)],
        own_queries, own_stats, dq_sum, *own,
    )
    kv_own = pl.pallas_call(
        functools.partial(merge_kernel, (count_chip, count_ka)),
        in_specs=in_vmem(3 + count_chip),
        out_specs=in_vmem(count_chip),
        out_shape=[jax.ShapeDtypeStruct(kv_shape, BF16 if number else F32) for number in range(count_chip)],
        compiler_params=params(16 + key_tiles // 4),
        name="merge",
    )(key_sum, value_sum, kv_back, *blocks)
    kv_parts = [kv_own[0]] + [swap(kv_own[number], 2 * number) for number in range(1, count_chip)]
    dq_late, dq_halves[1] = lax.optimization_barrier((dq_late, dq_halves[1]))
    for step, tile in zip(late, dq_late):
        dq_parts[step] = turn(tile, step) if step else tile

    piece_type = BF16 if share == 1 else F32
    piece_shape = (TILE + SPARE, 2 * HEAD_DIM)
    pieces = list(pl.pallas_call(
        functools.partial(collect_kernel, (count_chip, count_ka, share)),
        in_specs=in_vmem(2 + count_chip),
        out_specs=in_vmem(count_ka),
        out_shape=[jax.ShapeDtypeStruct(piece_shape, piece_type if step else F32) for step in range(count_ka)],
        compiler_params=params(24),
        name="collect",
    )(key_gain, value_gain, *kv_parts))
    where = ((half, 0), (half, heads_dev // 2)) + tuple((step, 0) for step in late)
    pieces = [pieces[0]] + [turn(piece, -step) for step, piece in enumerate(pieces[1:], 1)]
    grad_queries = pl.pallas_call(
        functools.partial(place_kernel, (count_ka, heads_dev, where)),
        in_specs=in_vmem(len(where)),
        out_specs=anywhere(1)[0],
        out_shape=jax.ShapeDtypeStruct((rows_dev, feat_width), BF16),
        scratch_shapes=[VMEM((count_ka, TILE, width), BF16), pltpu.SemaphoreType.DMA((len(where),))],
        compiler_params=params(16),
        cost_estimate=pl.CostEstimate(flops=0, bytes_accessed=4 * rows_dev * feat_width, transcendentals=0),
        name="place_queries",
    )(*dq_halves, *[dq_parts[step] for step in late])
    pieces, grad_queries = lax.optimization_barrier((pieces, grad_queries))
    grad_keys, grad_values, gains = pl.pallas_call(
        functools.partial(finish_kernel, (count_ka, share)),
        in_specs=in_vmem(2 + count_ka),
        out_specs=in_vmem(3),
        out_shape=[
            jax.ShapeDtypeStruct(key_rows.shape, BF16),
            jax.ShapeDtypeStruct(key_rows.shape, BF16),
            jax.ShapeDtypeStruct((2, key_rows.shape[1]), F32),
        ],
        scratch_shapes=[VMEM((kv_heads, TILE + SPARE, 2 * HEAD_DIM), F32)],
        compiler_params=params(16),
        name="finish",
    )(key_gain, value_gain, *pieces)
    grad_key_gain, grad_value_gain = pl.pallas_call(
        gains_kernel,
        in_specs=in_vmem(2),
        out_specs=in_vmem(2),
        out_shape=[jax.ShapeDtypeStruct(key_gain.shape, F32)] * 2,
        compiler_params=params(4),
        name="add_gains",
    )(gains, swap(gains, 1))
    return grad_queries, grad_keys, grad_values, grad_key_gain.reshape(-1), grad_value_gain.reshape(-1)


def solution(mesh):
    placed = (
        P("pb", None),
        P(("pb", "ka"), None),
        P(("pb", "ka"), None),
        P(("pb", "ka"), None),
        P("pb", None),
        P(None, ("pb", "ka")),
        P(),
        P(),
        P(),
        P(),
        P(),
    )
    return jax.shard_map(
        shards,
        mesh=mesh,
        in_specs=placed,
        out_specs=(P(("pb", "ka"), None), P(("pb", "ka"), None), P(("pb", "ka"), None), P(), P()),
        check_vma=False,
    )
```

```python
import functools

import jax
import jax.numpy as jnp
from jax import lax
from jax.experimental import pallas as pl
from jax.experimental.pallas import tpu as pltpu
from jax.sharding import PartitionSpec as P

HEAD_DIM = 128
TILE = 128
SPARE = 16
LOG2E = 1.4426950408889634
ENTRY = 4
PARTS = 4
STAT_TERMS = 2
EARLY = 2
LAST_DIMS = (((1,), (1,)), ((), ()))
VMEM = pltpu.VMEM
SMEM = pltpu.SMEM
F32 = jnp.float32
BF16 = jnp.bfloat16


def split_float(x, count):
    terms = []
    for _ in range(count):
        terms.append(x.astype(BF16).astype(F32))
        x = x - terms[-1]
    return terms


def head_rows(heads_dev):
    return -(-heads_dev // 8) * 8


def extra_rows(heads_dev):
    return STAT_TERMS * head_rows(heads_dev)


def prepare_kernel(dims, key_ref, value_ref, attn_ref, grads_ref, lse_ref, *rest):
    count_ka, heads, heads_dev, share = dims
    outs, (attn, grad, kv, lse_pad, delta_pad, sems) = rest[:count_ka], rest[count_ka:]
    _, place_ka = places()
    rows8 = head_rows(heads_dev)
    part_heads = heads // PARTS
    rows = pl.ds(pl.multiple_of(place_ka * TILE, TILE), TILE)
    copies = []
    for part in range(PARTS):
        columns = pl.ds(part * part_heads * HEAD_DIM, part_heads * HEAD_DIM)
        copies.append((
            pltpu.make_async_copy(attn_ref.at[:, columns], attn.at[part], sems.at[0, part]),
            pltpu.make_async_copy(grads_ref.at[rows, columns], grad.at[part], sems.at[1, part]),
        ))
    copies.append((
        pltpu.make_async_copy(key_ref, kv.at[0], sems.at[2, 0]),
        pltpu.make_async_copy(value_ref, kv.at[1], sems.at[2, 1]),
        pltpu.make_async_copy(lse_ref, lse_pad.at[pl.ds(0, heads), :], sems.at[2, 2]),
    ))
    for pair in copies:
        for copy in pair:
            copy.start()
    lanes = lax.broadcasted_iota(jnp.int32, (TILE, TILE), 1)
    columns = jnp.zeros((TILE, TILE), F32)
    for part in range(PARTS):
        for copy in copies[part]:
            copy.wait()
        for head in range(part_heads):
            at = pl.ds(head * HEAD_DIM, HEAD_DIM)
            products = grad[part, :, at].astype(F32) * attn[part, :, at].astype(F32)
            total = jnp.sum(products, axis=1, keepdims=True)
            columns = jnp.where(lanes == part * part_heads + head, total, columns)
    delta_pad[...] = jnp.zeros_like(delta_pad)
    lse_pad[pl.ds(heads, 8), :] = jnp.zeros((8, TILE), F32)
    delta_pad[:heads, :] = columns.T[:heads, :]
    for copy in copies[-1]:
        copy.wait()
    for step in range(count_ka):
        target = lax.rem(place_ka + step, count_ka)
        kv_at = pl.ds(pl.multiple_of(target // share * HEAD_DIM, HEAD_DIM), HEAD_DIM)
        outs[step][:TILE, :HEAD_DIM] = kv[0, :, kv_at]
        outs[step][:TILE, HEAD_DIM:] = kv[1, :, kv_at]
        head_at = pl.ds(target * heads_dev, rows8)
        both = jnp.concatenate([lse_pad[head_at, :], delta_pad[head_at, :]], axis=1)
        outs[step][TILE:, :] = jnp.concatenate(split_float(both, STAT_TERMS), axis=0).astype(BF16)


def own_heads_kernel(queries_ref, grads_ref, out_ref, sems):
    _, place_ka = places()
    width = out_ref.shape[2]
    columns = pl.ds(pl.multiple_of(place_ka * width, HEAD_DIM), width)
    copies = [
        pltpu.make_async_copy(ref.at[:, columns], out_ref.at[number], sems.at[number])
        for number, ref in enumerate((queries_ref, grads_ref))
    ]
    for copy in copies:
        copy.start()
    for copy in copies:
        copy.wait()


def places():
    return lax.axis_index("pb"), lax.axis_index("ka")


def own_start(key_tiles, count_ka):
    return 3 + count_ka * key_tiles


def plan_kernel(dims, order_ref, doc_ref, mask_ref, table):
    count_chip, count_ka, order = dims
    place_pb, place_ka = places()
    own_at = own_start(count_chip * count_ka, count_ka)

    def walk(start, query_pb, key_pb, steps, units):
        def query_step(turn_q, units):
            step_q = jnp.int32(order[0])
            for number, step in enumerate(order):
                step_q = jnp.where(turn_q == number, step, step_q)
            tile_at = lax.rem(place_ka + step_q, count_ka)
            seq_q = order_ref[query_pb * count_ka + tile_at]
            doc_q = doc_ref[seq_q]

            def collect(number, units):
                for step in range(count_ka):
                    stored = (key_pb ^ (2 * number)) * count_ka + lax.rem(
                        place_ka - step + count_ka, count_ka
                    )
                    seq_k = order_ref[stored]
                    live = (mask_ref[seq_q, seq_k] == 1) & (doc_ref[seq_k] == doc_q) & (seq_q >= seq_k)
                    if start is not None:
                        base = ENTRY * (start + units)
                        table[base] = turn_q
                        table[base + 1] = tile_at
                        table[base + 2] = number * count_ka + step
                        table[base + 3] = jnp.where(seq_q == seq_k, 0, -TILE)
                    units = units + live.astype(jnp.int32)
                return units

            return lax.fori_loop(0, count_chip, collect, units)

        return lax.fori_loop(*steps, query_step, units)

    def close(start, units):
        base = ENTRY * (start + units)
        table[base] = 0
        table[base + 1] = 0
        table[base + 2] = 0
        table[base + 3] = TILE
        return (units + 1) // 2

    def steps_of(units):
        return (units + 1) // 2

    none = jnp.int32(0)
    sibling = place_pb ^ 1
    other_first = walk(2, place_pb, sibling, (0, EARLY), none)
    other = close(2, walk(2, place_pb, sibling, (EARLY, count_ka), other_first))
    own_first = walk(own_at, place_pb, place_pb, (0, EARLY), none)
    own = close(own_at, walk(own_at, place_pb, place_pb, (EARLY, count_ka), own_first))
    there = steps_of(walk(None, sibling, sibling, (0, EARLY), none))
    there = there + steps_of(walk(None, sibling, place_pb, (0, count_ka), none))
    lead = jnp.maximum(there - other - steps_of(own_first), 0)
    table[0] = steps_of(own_first)
    table[1] = jnp.minimum(steps_of(own_first) + lead, own)
    table[2] = own
    table[ENTRY] = steps_of(other_first)
    table[ENTRY + 1] = other


def attention_kernel(dims, *rest):
    count_chip, count_ka, heads_dev, share, stage = dims
    table, rest = rest[0], rest[1:]
    if stage < 2:
        (key_gain_ref, value_gain_ref), rest = rest[:2], rest[2:]
    (heads_ref, stats_ref), rest = rest[:2], rest[2:]
    if stage < 2:
        blocks, rest = rest[:count_chip], rest[count_chip:]
    if stage == 0:
        (dq_sum, *own), rest = rest[:6], rest[6:]
    elif stage == 1:
        (dq_start, dq_sum, *dq_early), other, rest = rest[:2 + EARLY], rest[2 + EARLY:7 + EARLY], rest[7 + EARLY:]
    elif stage == 2:
        (dq_start, *own_start_refs), rest = rest[:6], rest[6:]
        other_refs, rest = rest[:5], rest[5:]
        (dq_sum, *own_sums, kv_other, other_key_sum, other_value_sum), rest = rest[:6], rest[6:]
        own = own_start_refs[:3] + own_sums
        other = other_refs[:3] + (other_key_sum, other_value_sum)
    else:
        (dq_start, *own_start_refs), rest = rest[:6], rest[6:]
        dq_outs, rest = rest[:count_ka - EARLY], rest[count_ka - EARLY:]
        (*own_sums, dq_sum), rest = rest[:3], rest[3:]
        own = own_start_refs[:3] + own_sums
    lse_delta, weights_low, dscores_low = rest
    _, place_ka = places()
    rows8 = head_rows(heads_dev)
    spare = extra_rows(heads_dev)
    score_scale = HEAD_DIM ** -0.5

    if stage < 2:
        kv_at = pl.ds(pl.multiple_of(place_ka // share * HEAD_DIM, HEAD_DIM), HEAD_DIM)
        key_gain = key_gain_ref[:, kv_at]
        value_gain = value_gain_ref[:, kv_at]
        keys, values, keys_t, key_sum, value_sum = other if stage else own
        for number in range(count_chip):
            for step in range(count_ka):
                part = pl.ds(step * TILE, TILE)
                local = number * count_ka + step
                key_tile = (blocks[number][part, :HEAD_DIM].astype(F32) * key_gain).astype(BF16)
                value_tile = (blocks[number][part, HEAD_DIM:].astype(F32) * value_gain).astype(BF16)
                keys[local] = key_tile
                values[local] = value_tile
                keys_t[local] = key_tile.T
        key_sum[...] = jnp.zeros_like(key_sum)
        value_sum[...] = jnp.zeros_like(value_sum)
    else:
        for target, source in zip(own_sums, own_start_refs[3:]):
            target[...] = source[...]
    if stage == 0:
        dq_sum[...] = jnp.zeros_like(dq_sum)
    else:
        dq_sum[...] = dq_start[...]
    if stage == 2:
        other_key_sum[...] = other_refs[3][...]
        other_value_sum[...] = other_refs[4][...]

    for slot in range(count_ka):
        packed = stats_ref[pl.ds(slot * spare, spare), :].astype(F32)
        terms = [packed[term * rows8:(term + 1) * rows8] for term in range(STAT_TERMS)]
        total = sum(terms[1:], terms[0])
        lse_delta[slot, :, :TILE] = total[:, :TILE] * LOG2E
        lse_delta[slot, :, TILE:] = total[:, TILE:]

    reach = (lax.broadcasted_iota(jnp.int32, (TILE, TILE), 1)
             - lax.broadcasted_iota(jnp.int32, (TILE, TILE), 0))
    reach = jnp.concatenate([reach, reach], axis=1)

    def run(start, refs, first, last):
        keys, values, keys_t, key_sum, value_sum = refs

        def heads_of(kind, tile_at, heads):
            rows = pl.ds(pl.multiple_of(tile_at * TILE, TILE), TILE)
            return jnp.concatenate(
                [heads_ref[kind, rows, pl.ds(head * HEAD_DIM, HEAD_DIM)] for head in heads], axis=0
            )

        def unit_step(at, carry):
            terms = []
            for lane in range(2):
                base = ENTRY * (start + 2 * at + lane)
                turn_q, tile_at, key_at = table[base], table[base + 1], table[base + 2]
                slot = lax.rem(place_ka - tile_at + count_ka, count_ka)
                allowed = reach >= table[base + 3]
                for head in range(0, heads_dev, 2):
                    part = pl.ds(head * HEAD_DIM, 2 * HEAD_DIM)
                    both = (head, head + 1)
                    scores = lax.dot_general(
                        keys[key_at], heads_of(0, tile_at, both), LAST_DIMS, preferred_element_type=F32
                    )
                    dweights = lax.dot_general(
                        values[key_at], heads_of(1, tile_at, both), LAST_DIMS, preferred_element_type=F32
                    )
                    lse_row, delta_row = [
                        jnp.concatenate(
                            [lse_delta[slot, number:number + 1, lanes] for number in both], axis=1
                        )
                        for lanes in (slice(0, TILE), slice(TILE, 2 * TILE))
                    ]
                    weights = jnp.exp2(scores * (score_scale * LOG2E) - lse_row)
                    weights = jnp.where(allowed, weights, 0.0)
                    weights_low[lane, :, part] = weights.astype(BF16)
                    dscores_low[lane, :, part] = (weights * (dweights - delta_row)).astype(BF16)
                every = range(heads_dev)
                terms.append((
                    turn_q,
                    key_at,
                    jnp.dot(weights_low[lane], heads_of(1, tile_at, every), preferred_element_type=F32),
                    jnp.dot(dscores_low[lane], heads_of(0, tile_at, every), preferred_element_type=F32),
                    jnp.dot(keys_t[key_at], dscores_low[lane], preferred_element_type=F32),
                ))
            for turn_q, key_at, value_term, key_term, dq_term in terms:
                value_sum[key_at] += value_term
                key_sum[key_at] += key_term
                dq_sum[turn_q] += dq_term
            return carry

        lax.fori_loop(first, last, unit_step, 0)

    own_at = own_start(count_chip * count_ka, count_ka)
    if stage == 0:
        run(own_at, own, 0, table[0])
    elif stage == 1:
        run(2, other, 0, table[ENTRY])
        for number, dq_out in enumerate(dq_early):
            dq_out[...] = (dq_sum[number] * score_scale).astype(BF16)
    elif stage == 2:
        run(2, other, table[ENTRY], table[ENTRY + 1])
        run(own_at, own, table[0], table[1])
        for local in range(count_chip * count_ka):
            part = pl.ds(local * TILE, TILE)
            kv_other[part, :HEAD_DIM] = (other_key_sum[local] * score_scale).astype(BF16)
            kv_other[part, HEAD_DIM:] = other_value_sum[local].astype(BF16)
    else:
        run(own_at, own, table[1], table[2])
        for number, dq_out in enumerate(dq_outs, EARLY):
            dq_out[...] = (dq_sum[number] * score_scale).astype(BF16)


def merge_kernel(dims, key_sum, value_sum, kv_back, *rest):
    count_chip, count_ka = dims
    blocks, kv_outs = rest[:count_chip], rest[count_chip:]
    key_gains = jnp.zeros((8, HEAD_DIM), F32)
    value_gains = jnp.zeros((8, HEAD_DIM), F32)
    for number in range(count_chip):
        for step in range(count_ka):
            local = number * count_ka + step
            there = pl.ds(local * TILE, TILE)
            key_total = key_sum[local] * HEAD_DIM ** -0.5 + kv_back[there, :HEAD_DIM].astype(F32)
            value_total = value_sum[local] + kv_back[there, HEAD_DIM:].astype(F32)
            out_ref = kv_outs[number]
            part = pl.ds(step * TILE, TILE)
            out_ref[part, :HEAD_DIM] = key_total.astype(out_ref.dtype)
            out_ref[part, HEAD_DIM:] = value_total.astype(out_ref.dtype)
            key_raw = blocks[number][part, :HEAD_DIM].astype(F32)
            value_raw = blocks[number][part, HEAD_DIM:].astype(F32)
            key_gains += jnp.sum((key_total * key_raw).reshape(TILE // 8, 8, HEAD_DIM), axis=0)
            value_gains += jnp.sum((value_total * value_raw).reshape(TILE // 8, 8, HEAD_DIM), axis=0)
    gains = jnp.concatenate([jnp.sum(key_gains, axis=0, keepdims=True),
                             jnp.sum(value_gains, axis=0, keepdims=True)], axis=1)
    packed = pack_gains(gains)
    for out_ref in kv_outs:
        out_ref[count_ka * TILE:, :] = packed.astype(out_ref.dtype)


def pack_gains(gains):
    rows = lax.broadcasted_iota(jnp.int32, (SPARE, gains.shape[1]), 0)
    high, middle, low = split_float(gains, 3)
    packed = jnp.where(rows == 0, high, jnp.where(rows == 1, middle, low))
    return jnp.where(rows < 3, packed, 0.0)


def add_parts(parts, rows):
    total = parts[0][rows, :]
    for part in parts[1:]:
        total = total + part[rows, :].astype(F32)
    return total


def own_gain(key_gain_ref, value_gain_ref, share):
    kv_at = pl.ds(pl.multiple_of(places()[1] // share * HEAD_DIM, HEAD_DIM), HEAD_DIM)
    return jnp.concatenate([key_gain_ref[:, kv_at], value_gain_ref[:, kv_at]], axis=1)


def collect_kernel(dims, key_gain_ref, value_gain_ref, *rest):
    count_chip, count_ka, share = dims
    parts, outs = rest[:count_chip], rest[count_chip:]
    gain = own_gain(key_gain_ref, value_gain_ref, share)
    total = add_parts(parts, pl.ds(count_ka * TILE, SPARE))
    packed = pack_gains(jnp.sum(total, axis=0, keepdims=True))
    for step, out_ref in enumerate(outs):
        total = add_parts(parts, pl.ds(step * TILE, TILE))
        if share == 1:
            total = total * gain
        out_ref[:TILE, :] = total.astype(out_ref.dtype)
        out_ref[TILE:, :] = packed.astype(out_ref.dtype)


def place_kernel(dims, *rest):
    count_ka, steps = dims
    pieces, (dq_out, turned, sems) = rest[:count_ka], rest[count_ka:]
    copies = []
    for number, (step, piece) in enumerate(zip(steps, pieces)):
        width = piece.shape[1]
        source = lax.rem(places()[1] - step + count_ka, count_ka)
        columns = pl.ds(pl.multiple_of(source * width, HEAD_DIM), width)
        for head in range(width // HEAD_DIM):
            part = pl.ds(head * HEAD_DIM, HEAD_DIM)
            turned[number, :, part] = piece[:, part].T
        copies.append(pltpu.make_async_copy(turned.at[number], dq_out.at[:, columns], sems.at[number]))
        copies[-1].start()
    for copy in copies:
        copy.wait()


def gains_kernel(gains_ref, other_ref, key_gain_out, value_gain_out):
    key_gain_out[...] = gains_ref[0:1, :] + other_ref[0:1, :]
    value_gain_out[...] = gains_ref[1:2, :] + other_ref[1:2, :]


def finish_kernel(dims, key_gain_ref, value_gain_ref, *rest):
    count_ka, share = dims
    pieces, rest = rest[:count_ka], rest[count_ka:]
    dk_out, dv_out, gains_out, sums = rest
    _, place_ka = places()
    sums[...] = jnp.zeros_like(sums)
    for step in range(count_ka):
        source = lax.rem(place_ka + step, count_ka)
        sums[source // share] += pieces[step][...].astype(F32)
    for head in range(count_ka // share):
        part = pl.ds(head * HEAD_DIM, HEAD_DIM)
        key_total = sums[head, :TILE, :HEAD_DIM]
        value_total = sums[head, :TILE, HEAD_DIM:]
        if share > 1:
            key_total = key_total * key_gain_ref[:, part]
            value_total = value_total * value_gain_ref[:, part]
        dk_out[:, part] = key_total.astype(BF16)
        dv_out[:, part] = value_total.astype(BF16)
        gains = jnp.sum(sums[head, TILE:, :], axis=0, keepdims=True)
        gains_out[0:1, part] = gains[:, :HEAD_DIM]
        gains_out[1:2, part] = gains[:, HEAD_DIM:]


def in_vmem(count):
    return [pl.BlockSpec(memory_space=VMEM)] * count


def in_smem(count):
    return [pl.BlockSpec(memory_space=SMEM)] * count


def anywhere(count):
    return [pl.BlockSpec(memory_space=pl.ANY)] * count


def params(mib):
    return pltpu.CompilerParams(vmem_limit_bytes=mib * 1024 * 1024)


def shards(
    queries,
    key_rows,
    values,
    attn_out,
    grad_out,
    log_sums,
    key_gain,
    value_gain,
    doc_ids,
    tile_mask,
    block_order,
):
    count_pb = lax.axis_size("pb")
    count_ka = lax.axis_size("ka")
    rows_dev = key_rows.shape[0]
    query_rows = queries.shape[0]
    heads = log_sums.shape[0]
    feat_width = queries.shape[1]
    kv_heads = key_rows.shape[1] // HEAD_DIM
    heads_dev = heads // count_ka
    share = count_ka // kv_heads
    assert rows_dev == TILE and share * kv_heads == count_ka and count_pb & (count_pb - 1) == 0
    width = heads_dev * HEAD_DIM
    key_gain = key_gain.reshape(1, -1)
    value_gain = value_gain.reshape(1, -1)

    spare = extra_rows(heads_dev)
    count_chip = count_pb // 2

    def swap(array, number):
        return lax.ppermute(array, "pb", [(at, at ^ number) for at in range(count_pb)])

    def turn(array, step):
        return lax.ppermute(array, "ka", [(at, (at + step) % count_ka) for at in range(count_ka)])

    sends = pl.pallas_call(
        functools.partial(prepare_kernel, (count_ka, heads, heads_dev, share)),
        in_specs=anywhere(5),
        out_specs=in_vmem(count_ka),
        out_shape=[jax.ShapeDtypeStruct((TILE + spare, 2 * HEAD_DIM), BF16)] * count_ka,
        scratch_shapes=[VMEM((PARTS, TILE, feat_width // PARTS), BF16)] * 2
        + [VMEM((2, *key_rows.shape), BF16)]
        + [VMEM((heads + 8, TILE), F32)] * 2
        + [pltpu.SemaphoreType.DMA((3, PARTS))],
        compiler_params=params(57),
        name="prepare",
    )(key_rows, values, attn_out, grad_out, log_sums)
    messages = [sends[0]] + [turn(sends[step], step) for step in range(1, count_ka)]

    later_queries, _ = lax.optimization_barrier((queries, sends[0]))
    own_queries = pl.pallas_call(
        own_heads_kernel,
        in_specs=anywhere(2),
        out_specs=in_vmem(1)[0],
        out_shape=jax.ShapeDtypeStruct((2, query_rows, width), BF16),
        scratch_shapes=[pltpu.SemaphoreType.DMA((2,))],
        compiler_params=params(48),
        cost_estimate=pl.CostEstimate(flops=0, bytes_accessed=8 * query_rows * width, transcendentals=0),
        name="own_heads",
    )(later_queries, grad_out)
    messages, own_queries = lax.optimization_barrier((messages, own_queries))
    own_block = jnp.concatenate([message[:TILE] for message in messages], axis=0)
    blocks = [own_block] + [swap(own_block, 2 * number) for number in range(1, count_chip)]
    other_blocks = [swap(block, 1) for block in blocks]
    own_stats = jnp.concatenate([message[TILE:] for message in messages], axis=0)
    later_order, _ = lax.optimization_barrier((block_order, own_block))

    key_tiles = count_chip * count_ka
    sum_shape = jax.ShapeDtypeStruct((key_tiles, TILE, HEAD_DIM), F32)
    key_shape = jax.ShapeDtypeStruct((key_tiles, TILE, HEAD_DIM), BF16)
    kv_shape = (query_rows + SPARE, 2 * HEAD_DIM)
    half = count_ka // 2
    early = (half, 1)
    late = tuple(step for step in range(count_ka) if step not in early)
    order = early + late
    entries = own_start(key_tiles, count_ka) + 1 + count_ka * key_tiles
    table = pl.pallas_call(
        functools.partial(plan_kernel, (count_chip, count_ka, order)),
        in_specs=in_smem(3),
        out_specs=in_smem(1)[0],
        out_shape=jax.ShapeDtypeStruct((ENTRY * entries,), jnp.int32),
        cost_estimate=pl.CostEstimate(flops=0, bytes_accessed=1 << 22, transcendentals=0),
        name="plan",
    )(later_order, doc_ids, tile_mask)

    def attend(stage, outs, scratch, *operands):
        return pl.pallas_call(
            functools.partial(attention_kernel, (count_chip, count_ka, heads_dev, share, stage)),
            in_specs=in_smem(1) + in_vmem(len(operands)),
            out_specs=in_vmem(len(outs)),
            out_shape=outs,
            scratch_shapes=scratch + [
                VMEM((count_ka, head_rows(heads_dev), 2 * TILE), F32),
                VMEM((2, TILE, width), BF16),
                VMEM((2, TILE, width), BF16),
            ],
            compiler_params=params(14 + key_tiles * 11 // 16),
            cost_estimate=pl.CostEstimate(
                flops=5 * count_ka * key_tiles * TILE * TILE * width, bytes_accessed=1 << 20, transcendentals=0
            ),
            name=("attention_first", "attention_leaving", "attention_other", "attention_own")[stage],
        )(table, *operands)

    dq_sums = jax.ShapeDtypeStruct((count_ka, HEAD_DIM, width), F32)
    dq_tile = jax.ShapeDtypeStruct((HEAD_DIM, width), BF16)
    state = [key_shape] * 3 + [sum_shape] * 2
    dq_sum, *own = attend(0, [dq_sums] + state, [], key_gain, value_gain, own_queries, own_stats, *blocks)
    dq_sum, *other = attend(
        1, [dq_sums] + [dq_tile] * EARLY + state, [],
        key_gain, value_gain, own_queries, own_stats, *other_blocks, dq_sum,
    )
    dq_parts = [None] * count_ka
    for step, tile in zip(early, other):
        dq_parts[step] = turn(tile, step)
    other = other[EARLY:]
    dq_sum, *own[3:], kv_other = attend(
        2, [dq_sums] + [sum_shape] * 2 + [jax.ShapeDtypeStruct((key_tiles * TILE, 2 * HEAD_DIM), BF16)],
        [VMEM(sum_shape.shape, F32)] * 2,
        own_queries, own_stats, dq_sum, *own, *other,
    )
    kv_back = swap(kv_other, 1)
    *dq_late, key_sum, value_sum = attend(
        3, [dq_tile] * len(late) + [sum_shape] * 2, [VMEM(dq_sums.shape, F32)],
        own_queries, own_stats, dq_sum, *own,
    )
    kv_own = pl.pallas_call(
        functools.partial(merge_kernel, (count_chip, count_ka)),
        in_specs=in_vmem(3 + count_chip),
        out_specs=in_vmem(count_chip),
        out_shape=[jax.ShapeDtypeStruct(kv_shape, BF16 if number else F32) for number in range(count_chip)],
        compiler_params=params(16 + key_tiles // 4),
        name="merge",
    )(key_sum, value_sum, kv_back, *blocks)
    kv_parts = [kv_own[0]] + [swap(kv_own[number], 2 * number) for number in range(1, count_chip)]
    dq_late, dq_parts[half], dq_parts[1] = lax.optimization_barrier((dq_late, dq_parts[half], dq_parts[1]))
    for step, tile in zip(late, dq_late):
        dq_parts[step] = turn(tile, step) if step else tile

    piece_type = BF16 if share == 1 else F32
    piece_shape = (TILE + SPARE, 2 * HEAD_DIM)
    pieces = list(pl.pallas_call(
        functools.partial(collect_kernel, (count_chip, count_ka, share)),
        in_specs=in_vmem(2 + count_chip),
        out_specs=in_vmem(count_ka),
        out_shape=[jax.ShapeDtypeStruct(piece_shape, piece_type if step else F32) for step in range(count_ka)],
        compiler_params=params(24),
        name="collect",
    )(key_gain, value_gain, *kv_parts))
    pieces = [pieces[0]] + [turn(piece, -step) for step, piece in enumerate(pieces[1:], 1)]
    grad_queries = pl.pallas_call(
        functools.partial(place_kernel, (count_ka, order)),
        in_specs=in_vmem(count_ka),
        out_specs=anywhere(1)[0],
        out_shape=jax.ShapeDtypeStruct((rows_dev, feat_width), BF16),
        scratch_shapes=[VMEM((count_ka, TILE, width), BF16), pltpu.SemaphoreType.DMA((count_ka,))],
        compiler_params=params(16),
        cost_estimate=pl.CostEstimate(flops=0, bytes_accessed=4 * rows_dev * feat_width, transcendentals=0),
        name="place_queries",
    )(*[dq_parts[step] for step in order])
    pieces, grad_queries = lax.optimization_barrier((pieces, grad_queries))
    grad_keys, grad_values, gains = pl.pallas_call(
        functools.partial(finish_kernel, (count_ka, share)),
        in_specs=in_vmem(2 + count_ka),
        out_specs=in_vmem(3),
        out_shape=[
            jax.ShapeDtypeStruct(key_rows.shape, BF16),
            jax.ShapeDtypeStruct(key_rows.shape, BF16),
            jax.ShapeDtypeStruct((2, key_rows.shape[1]), F32),
        ],
        scratch_shapes=[VMEM((kv_heads, TILE + SPARE, 2 * HEAD_DIM), F32)],
        compiler_params=params(16),
        name="finish",
    )(key_gain, value_gain, *pieces)
    grad_key_gain, grad_value_gain = pl.pallas_call(
        gains_kernel,
        in_specs=in_vmem(2),
        out_specs=in_vmem(2),
        out_shape=[jax.ShapeDtypeStruct(key_gain.shape, F32)] * 2,
        compiler_params=params(4),
        name="add_gains",
    )(gains, swap(gains, 1))
    return grad_queries, grad_keys, grad_values, grad_key_gain.reshape(-1), grad_value_gain.reshape(-1)


def solution(mesh):
    placed = (
        P("pb", None),
        P(("pb", "ka"), None),
        P(("pb", "ka"), None),
        P(("pb", "ka"), None),
        P("pb", None),
        P(None, ("pb", "ka")),
        P(),
        P(),
        P(),
        P(),
        P(),
    )
    return jax.shard_map(
        shards,
        mesh=mesh,
        in_specs=placed,
        out_specs=(P(("pb", "ka"), None), P(("pb", "ka"), None), P(("pb", "ka"), None), P(), P()),
        check_vma=False,
    )
```

```python
import functools

import jax
import jax.numpy as jnp
from jax import lax
from jax.experimental import pallas as pl
from jax.experimental.pallas import tpu as pltpu
from jax.sharding import PartitionSpec as P

HEAD_DIM = 128
TILE = 128
SPARE = 16
LOG2E = 1.4426950408889634
ENTRY = 4
PARTS = 4
STAT_TERMS = 2
LAST_DIMS = (((1,), (1,)), ((), ()))
VMEM = pltpu.VMEM
SMEM = pltpu.SMEM
F32 = jnp.float32
BF16 = jnp.bfloat16


def split_float(x, count):
    terms = []
    for _ in range(count):
        terms.append(x.astype(BF16).astype(F32))
        x = x - terms[-1]
    return terms


def head_rows(heads_dev):
    return -(-heads_dev // 8) * 8


def extra_rows(heads_dev):
    return STAT_TERMS * head_rows(heads_dev)


def prepare_kernel(dims, key_ref, value_ref, attn_ref, grads_ref, lse_ref, *rest):
    count_ka, heads, heads_dev, share = dims
    outs, (attn, grad, kv, lse_pad, delta_pad, sems) = rest[:count_ka], rest[count_ka:]
    _, place_ka = places()
    rows8 = head_rows(heads_dev)
    part_heads = heads // PARTS
    rows = pl.ds(pl.multiple_of(place_ka * TILE, TILE), TILE)
    copies = []
    for part in range(PARTS):
        columns = pl.ds(part * part_heads * HEAD_DIM, part_heads * HEAD_DIM)
        copies.append((
            pltpu.make_async_copy(attn_ref.at[:, columns], attn.at[part], sems.at[0, part]),
            pltpu.make_async_copy(grads_ref.at[rows, columns], grad.at[part], sems.at[1, part]),
        ))
    copies.append((
        pltpu.make_async_copy(key_ref, kv.at[0], sems.at[2, 0]),
        pltpu.make_async_copy(value_ref, kv.at[1], sems.at[2, 1]),
        pltpu.make_async_copy(lse_ref, lse_pad.at[pl.ds(0, heads), :], sems.at[2, 2]),
    ))
    for pair in copies:
        for copy in pair:
            copy.start()
    lanes = lax.broadcasted_iota(jnp.int32, (TILE, TILE), 1)
    columns = jnp.zeros((TILE, TILE), F32)
    for part in range(PARTS):
        for copy in copies[part]:
            copy.wait()
        for head in range(part_heads):
            at = pl.ds(head * HEAD_DIM, HEAD_DIM)
            products = grad[part, :, at].astype(F32) * attn[part, :, at].astype(F32)
            total = jnp.sum(products, axis=1, keepdims=True)
            columns = jnp.where(lanes == part * part_heads + head, total, columns)
    delta_pad[...] = jnp.zeros_like(delta_pad)
    lse_pad[pl.ds(heads, 8), :] = jnp.zeros((8, TILE), F32)
    delta_pad[:heads, :] = columns.T[:heads, :]
    for copy in copies[-1]:
        copy.wait()
    for step in range(count_ka):
        target = lax.rem(place_ka + step, count_ka)
        kv_at = pl.ds(pl.multiple_of(target // share * HEAD_DIM, HEAD_DIM), HEAD_DIM)
        outs[step][:TILE, :HEAD_DIM] = kv[0, :, kv_at]
        outs[step][:TILE, HEAD_DIM:] = kv[1, :, kv_at]
        head_at = pl.ds(target * heads_dev, rows8)
        both = jnp.concatenate([lse_pad[head_at, :], delta_pad[head_at, :]], axis=1)
        outs[step][TILE:, :] = jnp.concatenate(split_float(both, STAT_TERMS), axis=0).astype(BF16)


def own_heads_kernel(queries_ref, grads_ref, out_ref, sems):
    _, place_ka = places()
    width = out_ref.shape[2]
    columns = pl.ds(pl.multiple_of(place_ka * width, HEAD_DIM), width)
    copies = [
        pltpu.make_async_copy(ref.at[:, columns], out_ref.at[number], sems.at[number])
        for number, ref in enumerate((queries_ref, grads_ref))
    ]
    for copy in copies:
        copy.start()
    for copy in copies:
        copy.wait()


def places():
    return lax.axis_index("pb"), lax.axis_index("ka")


def own_start(key_tiles, count_ka):
    return 3 + count_ka * key_tiles


def plan_kernel(dims, order_ref, doc_ref, mask_ref, table, counts):
    count_chip, count_ka, order = dims
    place_pb, place_ka = places()
    own_at = own_start(count_chip * count_ka, count_ka)

    def walk(start, query_pb, key_pb, steps, units, count_at=None):
        def query_step(turn_q, units):
            before = units
            step_q = jnp.int32(order[0])
            for number, step in enumerate(order):
                step_q = jnp.where(turn_q == number, step, step_q)
            tile_at = lax.rem(place_ka + step_q, count_ka)
            seq_q = order_ref[query_pb * count_ka + tile_at]
            doc_q = doc_ref[seq_q]

            def collect(number, units):
                for step in range(count_ka):
                    stored = (key_pb ^ (2 * number)) * count_ka + lax.rem(
                        place_ka - step + count_ka, count_ka
                    )
                    seq_k = order_ref[stored]
                    live = (mask_ref[seq_q, seq_k] == 1) & (doc_ref[seq_k] == doc_q) & (seq_q >= seq_k)
                    if start is not None:
                        base = ENTRY * (start + units)
                        table[base] = turn_q
                        table[base + 1] = tile_at
                        table[base + 2] = number * count_ka + step
                        table[base + 3] = jnp.where(seq_q == seq_k, 0, -TILE)
                    units = units + live.astype(jnp.int32)
                return units

            units = lax.fori_loop(0, count_chip, collect, units)
            if count_at is not None:
                counts[count_at + tile_at] = units - before
            return units

        return lax.fori_loop(*steps, query_step, units)

    def close(start, units):
        base = ENTRY * (start + units)
        table[base] = 0
        table[base + 1] = 0
        table[base + 2] = 0
        table[base + 3] = TILE
        return (units + 1) // 2

    def steps_of(units):
        return (units + 1) // 2

    none = jnp.int32(0)
    sibling = place_pb ^ 1
    every = (0, count_ka)
    other = close(2, walk(2, place_pb, sibling, every, none, 2 * count_ka))
    own = close(own_at, walk(own_at, place_pb, place_pb, every, none, 0))
    walk(None, sibling, sibling, every, none, count_ka)
    sibling_other = steps_of(walk(None, sibling, place_pb, every, none))

    def first_steps(place):
        tile = lax.rem(place + order[0], count_ka)
        return steps_of(counts[tile]), steps_of(counts[2 * count_ka + tile])

    first, second = none, none
    for place in range(count_ka):
        first = jnp.maximum(first, sum(first_steps(place)))
        for core, others in enumerate((other, sibling_other)):
            units = sum([counts[core * count_ka + (place + step) % count_ka] for step in order[:2]])
            second = jnp.maximum(second, others + steps_of(units))
    own_first, other_first = first_steps(place_ka)
    table[0] = own_first
    table[1] = jnp.minimum(second - other, own)
    table[2] = own
    table[ENTRY] = jnp.clip(first - own_first, other_first, other)
    table[ENTRY + 1] = other


def attention_kernel(dims, *rest):
    count_chip, count_ka, heads_dev, share, stage = dims
    table, rest = rest[0], rest[1:]
    if stage < 2:
        (key_gain_ref, value_gain_ref), rest = rest[:2], rest[2:]
    (heads_ref, stats_ref), rest = rest[:2], rest[2:]
    if stage < 2:
        blocks, rest = rest[:count_chip], rest[count_chip:]
    if stage == 0:
        (dq_sum, *own), rest = rest[:6], rest[6:]
    elif stage == 1:
        (dq_start, dq_sum, *dq_halves), other, rest = rest[:4], rest[4:9], rest[9:]
    elif stage == 2:
        (dq_start, *own_start_refs), rest = rest[:6], rest[6:]
        other_refs, rest = rest[:5], rest[5:]
        (dq_sum, *own_sums, kv_other, dq_out, other_key_sum, other_value_sum), rest = rest[:7], rest[7:]
        own = own_start_refs[:3] + own_sums
        other = other_refs[:3] + (other_key_sum, other_value_sum)
    else:
        (dq_start, *own_start_refs), rest = rest[:6], rest[6:]
        dq_outs, rest = rest[:count_ka - 2], rest[count_ka - 2:]
        (*own_sums, dq_sum), rest = rest[:3], rest[3:]
        own = own_start_refs[:3] + own_sums
    lse_delta, weights_low, dscores_low = rest
    _, place_ka = places()
    rows8 = head_rows(heads_dev)
    spare = extra_rows(heads_dev)
    score_scale = HEAD_DIM ** -0.5

    if stage < 2:
        kv_at = pl.ds(pl.multiple_of(place_ka // share * HEAD_DIM, HEAD_DIM), HEAD_DIM)
        key_gain = key_gain_ref[:, kv_at]
        value_gain = value_gain_ref[:, kv_at]
        keys, values, keys_t, key_sum, value_sum = other if stage else own
        for number in range(count_chip):
            for step in range(count_ka):
                part = pl.ds(step * TILE, TILE)
                local = number * count_ka + step
                key_tile = (blocks[number][part, :HEAD_DIM].astype(F32) * key_gain).astype(BF16)
                value_tile = (blocks[number][part, HEAD_DIM:].astype(F32) * value_gain).astype(BF16)
                keys[local] = key_tile
                values[local] = value_tile
                keys_t[local] = key_tile.T
        key_sum[...] = jnp.zeros_like(key_sum)
        value_sum[...] = jnp.zeros_like(value_sum)
    else:
        for target, source in zip(own_sums, own_start_refs[3:]):
            target[...] = source[...]
    if stage == 0:
        dq_sum[...] = jnp.zeros_like(dq_sum)
    else:
        dq_sum[...] = dq_start[...]
    if stage == 2:
        other_key_sum[...] = other_refs[3][...]
        other_value_sum[...] = other_refs[4][...]

    for slot in range(count_ka):
        packed = stats_ref[pl.ds(slot * spare, spare), :].astype(F32)
        terms = [packed[term * rows8:(term + 1) * rows8] for term in range(STAT_TERMS)]
        total = sum(terms[1:], terms[0])
        lse_delta[slot, :, :TILE] = total[:, :TILE] * LOG2E
        lse_delta[slot, :, TILE:] = total[:, TILE:]

    reach = (lax.broadcasted_iota(jnp.int32, (TILE, TILE), 1)
             - lax.broadcasted_iota(jnp.int32, (TILE, TILE), 0))
    reach = jnp.concatenate([reach, reach], axis=1)

    def run(start, refs, first, last):
        keys, values, keys_t, key_sum, value_sum = refs

        def heads_of(kind, tile_at, heads):
            rows = pl.ds(pl.multiple_of(tile_at * TILE, TILE), TILE)
            return jnp.concatenate(
                [heads_ref[kind, rows, pl.ds(head * HEAD_DIM, HEAD_DIM)] for head in heads], axis=0
            )

        def unit_step(at, carry):
            terms = []
            for lane in range(2):
                base = ENTRY * (start + 2 * at + lane)
                turn_q, tile_at, key_at = table[base], table[base + 1], table[base + 2]
                slot = lax.rem(place_ka - tile_at + count_ka, count_ka)
                allowed = reach >= table[base + 3]
                for head in range(0, heads_dev, 2):
                    part = pl.ds(head * HEAD_DIM, 2 * HEAD_DIM)
                    both = (head, head + 1)
                    scores = lax.dot_general(
                        keys[key_at], heads_of(0, tile_at, both), LAST_DIMS, preferred_element_type=F32
                    )
                    dweights = lax.dot_general(
                        values[key_at], heads_of(1, tile_at, both), LAST_DIMS, preferred_element_type=F32
                    )
                    lse_row, delta_row = [
                        jnp.concatenate(
                            [lse_delta[slot, number:number + 1, lanes] for number in both], axis=1
                        )
                        for lanes in (slice(0, TILE), slice(TILE, 2 * TILE))
                    ]
                    weights = jnp.exp2(scores * (score_scale * LOG2E) - lse_row)
                    weights = jnp.where(allowed, weights, 0.0)
                    weights_low[lane, :, part] = weights.astype(BF16)
                    dscores_low[lane, :, part] = (weights * (dweights - delta_row)).astype(BF16)
                every = range(heads_dev)
                terms.append((
                    turn_q,
                    key_at,
                    jnp.dot(weights_low[lane], heads_of(1, tile_at, every), preferred_element_type=F32),
                    jnp.dot(dscores_low[lane], heads_of(0, tile_at, every), preferred_element_type=F32),
                    jnp.dot(keys_t[key_at], dscores_low[lane], preferred_element_type=F32),
                ))
            for turn_q, key_at, value_term, key_term, dq_term in terms:
                value_sum[key_at] += value_term
                key_sum[key_at] += key_term
                dq_sum[turn_q] += dq_term
            return carry

        lax.fori_loop(first, last, unit_step, 0)

    own_at = own_start(count_chip * count_ka, count_ka)
    if stage == 0:
        run(own_at, own, 0, table[0])
    elif stage == 1:
        run(2, other, 0, table[ENTRY])
        for number, dq_half in enumerate(dq_halves):
            part = pl.ds(number * dq_half.shape[1], dq_half.shape[1])
            dq_half[...] = (dq_sum[0, :, part] * score_scale).astype(BF16)
    elif stage == 2:
        run(2, other, table[ENTRY], table[ENTRY + 1])
        run(own_at, own, table[0], table[1])
        dq_out[...] = (dq_sum[1] * score_scale).astype(BF16)
        for local in range(count_chip * count_ka):
            part = pl.ds(local * TILE, TILE)
            kv_other[part, :HEAD_DIM] = (other_key_sum[local] * score_scale).astype(BF16)
            kv_other[part, HEAD_DIM:] = other_value_sum[local].astype(BF16)
    else:
        run(own_at, own, table[1], table[2])
        for number, dq_out in enumerate(dq_outs, 2):
            dq_out[...] = (dq_sum[number] * score_scale).astype(BF16)


def merge_kernel(dims, key_sum, value_sum, kv_back, *rest):
    count_chip, count_ka = dims
    blocks, kv_outs = rest[:count_chip], rest[count_chip:]
    key_gains = jnp.zeros((8, HEAD_DIM), F32)
    value_gains = jnp.zeros((8, HEAD_DIM), F32)
    for number in range(count_chip):
        for step in range(count_ka):
            local = number * count_ka + step
            there = pl.ds(local * TILE, TILE)
            key_total = key_sum[local] * HEAD_DIM ** -0.5 + kv_back[there, :HEAD_DIM].astype(F32)
            value_total = value_sum[local] + kv_back[there, HEAD_DIM:].astype(F32)
            out_ref = kv_outs[number]
            part = pl.ds(step * TILE, TILE)
            out_ref[part, :HEAD_DIM] = key_total.astype(out_ref.dtype)
            out_ref[part, HEAD_DIM:] = value_total.astype(out_ref.dtype)
            key_raw = blocks[number][part, :HEAD_DIM].astype(F32)
            value_raw = blocks[number][part, HEAD_DIM:].astype(F32)
            key_gains += jnp.sum((key_total * key_raw).reshape(TILE // 8, 8, HEAD_DIM), axis=0)
            value_gains += jnp.sum((value_total * value_raw).reshape(TILE // 8, 8, HEAD_DIM), axis=0)
    gains = jnp.concatenate([jnp.sum(key_gains, axis=0, keepdims=True),
                             jnp.sum(value_gains, axis=0, keepdims=True)], axis=1)
    packed = pack_gains(gains)
    for out_ref in kv_outs:
        out_ref[count_ka * TILE:, :] = packed.astype(out_ref.dtype)


def pack_gains(gains):
    rows = lax.broadcasted_iota(jnp.int32, (SPARE, gains.shape[1]), 0)
    high, middle, low = split_float(gains, 3)
    packed = jnp.where(rows == 0, high, jnp.where(rows == 1, middle, low))
    return jnp.where(rows < 3, packed, 0.0)


def add_parts(parts, rows):
    total = parts[0][rows, :]
    for part in parts[1:]:
        total = total + part[rows, :].astype(F32)
    return total


def own_gain(key_gain_ref, value_gain_ref, share):
    kv_at = pl.ds(pl.multiple_of(places()[1] // share * HEAD_DIM, HEAD_DIM), HEAD_DIM)
    return jnp.concatenate([key_gain_ref[:, kv_at], value_gain_ref[:, kv_at]], axis=1)


def collect_kernel(dims, key_gain_ref, value_gain_ref, *rest):
    count_chip, count_ka, share = dims
    parts, outs = rest[:count_chip], rest[count_chip:]
    gain = own_gain(key_gain_ref, value_gain_ref, share)
    total = add_parts(parts, pl.ds(count_ka * TILE, SPARE))
    packed = pack_gains(jnp.sum(total, axis=0, keepdims=True))
    for step, out_ref in enumerate(outs):
        total = add_parts(parts, pl.ds(step * TILE, TILE))
        if share == 1:
            total = total * gain
        out_ref[:TILE, :] = total.astype(out_ref.dtype)
        out_ref[TILE:, :] = packed.astype(out_ref.dtype)


def place_kernel(dims, *rest):
    count_ka, heads_dev, where = dims
    pieces, (dq_out, turned, sems) = rest[:len(where)], rest[len(where):]
    copies = []
    for number, ((step, first), piece) in enumerate(zip(where, pieces)):
        source = lax.rem(places()[1] - step + count_ka, count_ka)
        columns = pl.ds(pl.multiple_of((source * heads_dev + first) * HEAD_DIM, HEAD_DIM), piece.shape[1])
        here = pl.ds(first * HEAD_DIM, piece.shape[1])
        for head in range(piece.shape[1] // HEAD_DIM):
            part = pl.ds(head * HEAD_DIM, HEAD_DIM)
            turned[step, :, pl.ds((first + head) * HEAD_DIM, HEAD_DIM)] = piece[:, part].T
        copies.append(pltpu.make_async_copy(turned.at[step, :, here], dq_out.at[:, columns], sems.at[number]))
        copies[-1].start()
    for copy in copies:
        copy.wait()


def gains_kernel(gains_ref, other_ref, key_gain_out, value_gain_out):
    key_gain_out[...] = gains_ref[0:1, :] + other_ref[0:1, :]
    value_gain_out[...] = gains_ref[1:2, :] + other_ref[1:2, :]


def finish_kernel(dims, key_gain_ref, value_gain_ref, *rest):
    count_ka, share = dims
    pieces, rest = rest[:count_ka], rest[count_ka:]
    dk_out, dv_out, gains_out, sums = rest
    _, place_ka = places()
    sums[...] = jnp.zeros_like(sums)
    for step in range(count_ka):
        source = lax.rem(place_ka + step, count_ka)
        sums[source // share] += pieces[step][...].astype(F32)
    for head in range(count_ka // share):
        part = pl.ds(head * HEAD_DIM, HEAD_DIM)
        key_total = sums[head, :TILE, :HEAD_DIM]
        value_total = sums[head, :TILE, HEAD_DIM:]
        if share > 1:
            key_total = key_total * key_gain_ref[:, part]
            value_total = value_total * value_gain_ref[:, part]
        dk_out[:, part] = key_total.astype(BF16)
        dv_out[:, part] = value_total.astype(BF16)
        gains = jnp.sum(sums[head, TILE:, :], axis=0, keepdims=True)
        gains_out[0:1, part] = gains[:, :HEAD_DIM]
        gains_out[1:2, part] = gains[:, HEAD_DIM:]


def in_vmem(count):
    return [pl.BlockSpec(memory_space=VMEM)] * count


def in_smem(count):
    return [pl.BlockSpec(memory_space=SMEM)] * count


def anywhere(count):
    return [pl.BlockSpec(memory_space=pl.ANY)] * count


def params(mib):
    return pltpu.CompilerParams(vmem_limit_bytes=mib * 1024 * 1024)


def shards(
    queries,
    key_rows,
    values,
    attn_out,
    grad_out,
    log_sums,
    key_gain,
    value_gain,
    doc_ids,
    tile_mask,
    block_order,
):
    count_pb = lax.axis_size("pb")
    count_ka = lax.axis_size("ka")
    rows_dev = key_rows.shape[0]
    query_rows = queries.shape[0]
    heads = log_sums.shape[0]
    feat_width = queries.shape[1]
    kv_heads = key_rows.shape[1] // HEAD_DIM
    heads_dev = heads // count_ka
    share = count_ka // kv_heads
    assert rows_dev == TILE and share * kv_heads == count_ka and count_pb & (count_pb - 1) == 0
    width = heads_dev * HEAD_DIM
    key_gain = key_gain.reshape(1, -1)
    value_gain = value_gain.reshape(1, -1)

    spare = extra_rows(heads_dev)
    count_chip = count_pb // 2

    def swap(array, number):
        return lax.ppermute(array, "pb", [(at, at ^ number) for at in range(count_pb)])

    def turn(array, step):
        return lax.ppermute(array, "ka", [(at, (at + step) % count_ka) for at in range(count_ka)])

    sends = pl.pallas_call(
        functools.partial(prepare_kernel, (count_ka, heads, heads_dev, share)),
        in_specs=anywhere(5),
        out_specs=in_vmem(count_ka),
        out_shape=[jax.ShapeDtypeStruct((TILE + spare, 2 * HEAD_DIM), BF16)] * count_ka,
        scratch_shapes=[VMEM((PARTS, TILE, feat_width // PARTS), BF16)] * 2
        + [VMEM((2, *key_rows.shape), BF16)]
        + [VMEM((heads + 8, TILE), F32)] * 2
        + [pltpu.SemaphoreType.DMA((3, PARTS))],
        compiler_params=params(57),
        name="prepare",
    )(key_rows, values, attn_out, grad_out, log_sums)
    messages = [sends[0]] + [turn(sends[step], step) for step in range(1, count_ka)]

    later_queries, _ = lax.optimization_barrier((queries, sends[0]))
    own_queries = pl.pallas_call(
        own_heads_kernel,
        in_specs=anywhere(2),
        out_specs=in_vmem(1)[0],
        out_shape=jax.ShapeDtypeStruct((2, query_rows, width), BF16),
        scratch_shapes=[pltpu.SemaphoreType.DMA((2,))],
        compiler_params=params(48),
        cost_estimate=pl.CostEstimate(flops=0, bytes_accessed=8 * query_rows * width, transcendentals=0),
        name="own_heads",
    )(later_queries, grad_out)
    messages, own_queries = lax.optimization_barrier((messages, own_queries))
    own_block = jnp.concatenate([message[:TILE] for message in messages], axis=0)
    blocks = [own_block] + [swap(own_block, 2 * number) for number in range(1, count_chip)]
    other_blocks = [swap(block, 1) for block in blocks]
    own_stats = jnp.concatenate([message[TILE:] for message in messages], axis=0)
    later_order, _ = lax.optimization_barrier((block_order, own_block))

    key_tiles = count_chip * count_ka
    sum_shape = jax.ShapeDtypeStruct((key_tiles, TILE, HEAD_DIM), F32)
    key_shape = jax.ShapeDtypeStruct((key_tiles, TILE, HEAD_DIM), BF16)
    kv_shape = (query_rows + SPARE, 2 * HEAD_DIM)
    half = count_ka // 2
    early = (half, 1)
    late = tuple(step for step in range(count_ka) if step not in early)
    order = early + late
    entries = own_start(key_tiles, count_ka) + 1 + count_ka * key_tiles
    table = pl.pallas_call(
        functools.partial(plan_kernel, (count_chip, count_ka, order)),
        in_specs=in_smem(3),
        out_specs=in_smem(1)[0],
        out_shape=jax.ShapeDtypeStruct((ENTRY * entries,), jnp.int32),
        scratch_shapes=[SMEM((3 * count_ka,), jnp.int32)],
        cost_estimate=pl.CostEstimate(flops=0, bytes_accessed=1 << 22, transcendentals=0),
        name="plan",
    )(later_order, doc_ids, tile_mask)

    def attend(stage, outs, scratch, *operands):
        return pl.pallas_call(
            functools.partial(attention_kernel, (count_chip, count_ka, heads_dev, share, stage)),
            in_specs=in_smem(1) + in_vmem(len(operands)),
            out_specs=in_vmem(len(outs)),
            out_shape=outs,
            scratch_shapes=scratch + [
                VMEM((count_ka, head_rows(heads_dev), 2 * TILE), F32),
                VMEM((2, TILE, width), BF16),
                VMEM((2, TILE, width), BF16),
            ],
            compiler_params=params(14 + key_tiles * 11 // 16),
            cost_estimate=pl.CostEstimate(
                flops=5 * count_ka * key_tiles * TILE * TILE * width, bytes_accessed=1 << 20, transcendentals=0
            ),
            name=("attention_first", "attention_leaving", "attention_other", "attention_own")[stage],
        )(table, *operands)

    dq_sums = jax.ShapeDtypeStruct((count_ka, HEAD_DIM, width), F32)
    dq_tile = jax.ShapeDtypeStruct((HEAD_DIM, width), BF16)
    state = [key_shape] * 3 + [sum_shape] * 2
    dq_sum, *own = attend(0, [dq_sums] + state, [], key_gain, value_gain, own_queries, own_stats, *blocks)
    dq_sum, *other = attend(
        1, [dq_sums] + [jax.ShapeDtypeStruct((HEAD_DIM, width // 2), BF16)] * 2 + state, [],
        key_gain, value_gain, own_queries, own_stats, *other_blocks, dq_sum,
    )
    dq_parts = [None] * count_ka
    dq_halves, other = [turn(part, half) for part in other[:2]], other[2:]
    dq_sum, *own[3:], kv_other, dq_second = attend(
        2,
        [dq_sums] + [sum_shape] * 2
        + [jax.ShapeDtypeStruct((key_tiles * TILE, 2 * HEAD_DIM), BF16), dq_tile],
        [VMEM(sum_shape.shape, F32)] * 2,
        own_queries, own_stats, dq_sum, *own, *other,
    )
    kv_other, dq_halves[0] = lax.optimization_barrier((kv_other, dq_halves[0]))
    kv_back = swap(kv_other, 1)
    dq_parts[1] = turn(dq_second, 1)
    *dq_late, key_sum, value_sum = attend(
        3, [dq_tile] * len(late) + [sum_shape] * 2, [VMEM(dq_sums.shape, F32)],
        own_queries, own_stats, dq_sum, *own,
    )
    kv_own = pl.pallas_call(
        functools.partial(merge_kernel, (count_chip, count_ka)),
        in_specs=in_vmem(3 + count_chip),
        out_specs=in_vmem(count_chip),
        out_shape=[jax.ShapeDtypeStruct(kv_shape, BF16 if number else F32) for number in range(count_chip)],
        compiler_params=params(16 + key_tiles // 4),
        name="merge",
    )(key_sum, value_sum, kv_back, *blocks)
    kv_parts = [kv_own[0]] + [swap(kv_own[number], 2 * number) for number in range(1, count_chip)]
    dq_late, dq_parts[1], dq_halves[1] = lax.optimization_barrier((dq_late, dq_parts[1], dq_halves[1]))
    for step, tile in zip(late, dq_late):
        dq_parts[step] = turn(tile, step) if step else tile

    piece_type = BF16 if share == 1 else F32
    piece_shape = (TILE + SPARE, 2 * HEAD_DIM)
    pieces = list(pl.pallas_call(
        functools.partial(collect_kernel, (count_chip, count_ka, share)),
        in_specs=in_vmem(2 + count_chip),
        out_specs=in_vmem(count_ka),
        out_shape=[jax.ShapeDtypeStruct(piece_shape, piece_type if step else F32) for step in range(count_ka)],
        compiler_params=params(24),
        name="collect",
    )(key_gain, value_gain, *kv_parts))
    pieces = [pieces[0]] + [turn(piece, -step) for step, piece in enumerate(pieces[1:], 1)]
    where = ((half, 0), (half, heads_dev // 2)) + tuple((step, 0) for step in order[1:])
    grad_queries = pl.pallas_call(
        functools.partial(place_kernel, (count_ka, heads_dev, where)),
        in_specs=in_vmem(len(where)),
        out_specs=anywhere(1)[0],
        out_shape=jax.ShapeDtypeStruct((rows_dev, feat_width), BF16),
        scratch_shapes=[VMEM((count_ka, TILE, width), BF16), pltpu.SemaphoreType.DMA((len(where),))],
        compiler_params=params(16),
        cost_estimate=pl.CostEstimate(flops=0, bytes_accessed=4 * rows_dev * feat_width, transcendentals=0),
        name="place_queries",
    )(*dq_halves, *[dq_parts[step] for step in order[1:]])
    pieces, grad_queries = lax.optimization_barrier((pieces, grad_queries))
    grad_keys, grad_values, gains = pl.pallas_call(
        functools.partial(finish_kernel, (count_ka, share)),
        in_specs=in_vmem(2 + count_ka),
        out_specs=in_vmem(3),
        out_shape=[
            jax.ShapeDtypeStruct(key_rows.shape, BF16),
            jax.ShapeDtypeStruct(key_rows.shape, BF16),
            jax.ShapeDtypeStruct((2, key_rows.shape[1]), F32),
        ],
        scratch_shapes=[VMEM((kv_heads, TILE + SPARE, 2 * HEAD_DIM), F32)],
        compiler_params=params(16),
        name="finish",
    )(key_gain, value_gain, *pieces)
    grad_key_gain, grad_value_gain = pl.pallas_call(
        gains_kernel,
        in_specs=in_vmem(2),
        out_specs=in_vmem(2),
        out_shape=[jax.ShapeDtypeStruct(key_gain.shape, F32)] * 2,
        compiler_params=params(4),
        name="add_gains",
    )(gains, swap(gains, 1))
    return grad_queries, grad_keys, grad_values, grad_key_gain.reshape(-1), grad_value_gain.reshape(-1)


def solution(mesh):
    placed = (
        P("pb", None),
        P(("pb", "ka"), None),
        P(("pb", "ka"), None),
        P(("pb", "ka"), None),
        P("pb", None),
        P(None, ("pb", "ka")),
        P(),
        P(),
        P(),
        P(),
        P(),
    )
    return jax.shard_map(
        shards,
        mesh=mesh,
        in_specs=placed,
        out_specs=(P(("pb", "ka"), None), P(("pb", "ka"), None), P(("pb", "ka"), None), P(), P()),
        check_vma=False,
    )
```

```python
import functools

import jax
import jax.numpy as jnp
from jax import lax
from jax.experimental import pallas as pl
from jax.experimental.pallas import tpu as pltpu
from jax.sharding import PartitionSpec as P

HEAD_DIM = 128
TILE = 128
SPARE = 16
LOG2E = 1.4426950408889634
ENTRY = 4
PARTS = 4
STAT_TERMS = 2
LAST_DIMS = (((1,), (1,)), ((), ()))
VMEM = pltpu.VMEM
SMEM = pltpu.SMEM
F32 = jnp.float32
BF16 = jnp.bfloat16


def split_float(x, count):
    terms = []
    for _ in range(count):
        terms.append(x.astype(BF16).astype(F32))
        x = x - terms[-1]
    return terms


def head_rows(heads_dev):
    return -(-heads_dev // 8) * 8


def extra_rows(heads_dev):
    return STAT_TERMS * head_rows(heads_dev)


def prepare_kernel(dims, key_ref, value_ref, attn_ref, grads_ref, lse_ref, *rest):
    count_ka, heads, heads_dev, share = dims
    outs, (attn, grad, kv, lse_pad, delta_pad, sems) = rest[:count_ka], rest[count_ka:]
    _, place_ka = places()
    rows8 = head_rows(heads_dev)
    part_heads = heads // PARTS
    rows = pl.ds(pl.multiple_of(place_ka * TILE, TILE), TILE)
    copies = []
    for part in range(PARTS):
        columns = pl.ds(part * part_heads * HEAD_DIM, part_heads * HEAD_DIM)
        copies.append((
            pltpu.make_async_copy(attn_ref.at[:, columns], attn.at[part], sems.at[0, part]),
            pltpu.make_async_copy(grads_ref.at[rows, columns], grad.at[part], sems.at[1, part]),
        ))
    copies.append((
        pltpu.make_async_copy(key_ref, kv.at[0], sems.at[2, 0]),
        pltpu.make_async_copy(value_ref, kv.at[1], sems.at[2, 1]),
        pltpu.make_async_copy(lse_ref, lse_pad.at[pl.ds(0, heads), :], sems.at[2, 2]),
    ))
    for pair in copies:
        for copy in pair:
            copy.start()
    lanes = lax.broadcasted_iota(jnp.int32, (TILE, TILE), 1)
    columns = jnp.zeros((TILE, TILE), F32)
    for part in range(PARTS):
        for copy in copies[part]:
            copy.wait()
        for head in range(part_heads):
            at = pl.ds(head * HEAD_DIM, HEAD_DIM)
            products = grad[part, :, at].astype(F32) * attn[part, :, at].astype(F32)
            total = jnp.sum(products, axis=1, keepdims=True)
            columns = jnp.where(lanes == part * part_heads + head, total, columns)
    delta_pad[...] = jnp.zeros_like(delta_pad)
    lse_pad[pl.ds(heads, 8), :] = jnp.zeros((8, TILE), F32)
    delta_pad[:heads, :] = columns.T[:heads, :]
    for copy in copies[-1]:
        copy.wait()
    for step in range(count_ka):
        target = lax.rem(place_ka + step, count_ka)
        kv_at = pl.ds(pl.multiple_of(target // share * HEAD_DIM, HEAD_DIM), HEAD_DIM)
        outs[step][:TILE, :HEAD_DIM] = kv[0, :, kv_at]
        outs[step][:TILE, HEAD_DIM:] = kv[1, :, kv_at]
        head_at = pl.ds(target * heads_dev, rows8)
        both = jnp.concatenate([lse_pad[head_at, :], delta_pad[head_at, :]], axis=1)
        outs[step][TILE:, :] = jnp.concatenate(split_float(both, STAT_TERMS), axis=0).astype(BF16)


def own_heads_kernel(queries_ref, grads_ref, out_ref, sems):
    _, place_ka = places()
    width = out_ref.shape[2]
    columns = pl.ds(pl.multiple_of(place_ka * width, HEAD_DIM), width)
    copies = [
        pltpu.make_async_copy(ref.at[:, columns], out_ref.at[number], sems.at[number])
        for number, ref in enumerate((queries_ref, grads_ref))
    ]
    for copy in copies:
        copy.start()
    for copy in copies:
        copy.wait()


def places():
    return lax.axis_index("pb"), lax.axis_index("ka")


def own_start(key_tiles, count_ka):
    return 3 + count_ka * key_tiles


def plan_kernel(dims, order_ref, doc_ref, mask_ref, table, counts):
    count_chip, count_ka, order = dims
    place_pb, place_ka = places()
    own_at = own_start(count_chip * count_ka, count_ka)

    def walk(start, query_pb, key_pb, steps, units, count_at=None):
        def query_step(turn_q, units):
            before = units
            step_q = jnp.int32(order[0])
            for number, step in enumerate(order):
                step_q = jnp.where(turn_q == number, step, step_q)
            tile_at = lax.rem(place_ka + step_q, count_ka)
            seq_q = order_ref[query_pb * count_ka + tile_at]
            doc_q = doc_ref[seq_q]

            def collect(number, units):
                for step in range(count_ka):
                    stored = (key_pb ^ (2 * number)) * count_ka + lax.rem(
                        place_ka - step + count_ka, count_ka
                    )
                    seq_k = order_ref[stored]
                    live = (mask_ref[seq_q, seq_k] == 1) & (doc_ref[seq_k] == doc_q) & (seq_q >= seq_k)
                    if start is not None:
                        base = ENTRY * (start + units)
                        table[base] = turn_q
                        table[base + 1] = tile_at
                        table[base + 2] = number * count_ka + step
                        table[base + 3] = jnp.where(seq_q == seq_k, 0, -TILE)
                    units = units + live.astype(jnp.int32)
                return units

            units = lax.fori_loop(0, count_chip, collect, units)
            if count_at is not None:
                counts[count_at + tile_at] = units - before
            return units

        return lax.fori_loop(*steps, query_step, units)

    def close(start, units):
        base = ENTRY * (start + units)
        table[base] = 0
        table[base + 1] = 0
        table[base + 2] = 0
        table[base + 3] = TILE
        return (units + 1) // 2

    def steps_of(units):
        return (units + 1) // 2

    none = jnp.int32(0)
    sibling = place_pb ^ 1
    every = (0, count_ka)
    other = close(2, walk(2, place_pb, sibling, every, none, 2 * count_ka))
    own = close(own_at, walk(own_at, place_pb, place_pb, every, none, 0))
    walk(None, sibling, sibling, every, none, count_ka)
    sibling_other = steps_of(walk(None, sibling, place_pb, every, none))

    def first_steps(place):
        tile = lax.rem(place + order[0], count_ka)
        return steps_of(counts[tile]), steps_of(counts[2 * count_ka + tile])

    first, second = none, none
    for place in range(count_ka):
        first = jnp.maximum(first, sum(first_steps(place)))
        for core, others in enumerate((other, sibling_other)):
            units = sum([counts[core * count_ka + (place + step) % count_ka] for step in order[:2]])
            second = jnp.maximum(second, others + steps_of(units))
    own_first, other_first = first_steps(place_ka)
    table[0] = own_first
    table[1] = jnp.minimum(second - other, own)
    table[2] = own
    table[ENTRY] = jnp.clip(first - own_first, other_first, other)
    table[ENTRY + 1] = other


def attention_kernel(dims, *rest):
    count_chip, count_ka, heads_dev, share, stage = dims
    table, rest = rest[0], rest[1:]
    if stage < 2:
        (key_gain_ref, value_gain_ref), rest = rest[:2], rest[2:]
    (heads_ref, stats_ref), rest = rest[:2], rest[2:]
    if stage < 2:
        blocks, rest = rest[:count_chip], rest[count_chip:]
    if stage == 0:
        (dq_sum, *own), rest = rest[:6], rest[6:]
    elif stage == 1:
        (dq_start, dq_sum, *dq_halves), other, rest = rest[:4], rest[4:9], rest[9:]
    elif stage == 2:
        (dq_start, *own_start_refs), rest = rest[:6], rest[6:]
        other_refs, rest = rest[:5], rest[5:]
        (dq_sum, *own_sums, kv_other, dq_out, other_key_sum, other_value_sum), rest = rest[:7], rest[7:]
        own = own_start_refs[:3] + own_sums
        other = other_refs[:3] + (other_key_sum, other_value_sum)
    else:
        (dq_start, *own_start_refs), rest = rest[:6], rest[6:]
        dq_outs, rest = rest[:count_ka - 2], rest[count_ka - 2:]
        (*own_sums, dq_sum), rest = rest[:3], rest[3:]
        own = own_start_refs[:3] + own_sums
    lse_delta, both_low = rest
    _, place_ka = places()
    rows8 = head_rows(heads_dev)
    spare = extra_rows(heads_dev)
    score_scale = HEAD_DIM ** -0.5

    if stage < 2:
        kv_at = pl.ds(pl.multiple_of(place_ka // share * HEAD_DIM, HEAD_DIM), HEAD_DIM)
        key_gain = key_gain_ref[:, kv_at]
        value_gain = value_gain_ref[:, kv_at]
        keys, values, keys_t, key_sum, value_sum = other if stage else own
        for number in range(count_chip):
            for step in range(count_ka):
                part = pl.ds(step * TILE, TILE)
                local = number * count_ka + step
                key_tile = (blocks[number][part, :HEAD_DIM].astype(F32) * key_gain).astype(BF16)
                value_tile = (blocks[number][part, HEAD_DIM:].astype(F32) * value_gain).astype(BF16)
                keys[local] = key_tile
                values[local] = value_tile
                keys_t[local] = key_tile.T
        key_sum[...] = jnp.zeros_like(key_sum)
        value_sum[...] = jnp.zeros_like(value_sum)
    else:
        for target, source in zip(own_sums, own_start_refs[3:]):
            target[...] = source[...]
    if stage == 0:
        dq_sum[...] = jnp.zeros_like(dq_sum)
    else:
        dq_sum[...] = dq_start[...]
    if stage == 2:
        other_key_sum[...] = other_refs[3][...]
        other_value_sum[...] = other_refs[4][...]

    for slot in range(count_ka):
        packed = stats_ref[pl.ds(slot * spare, spare), :].astype(F32)
        terms = [packed[term * rows8:(term + 1) * rows8] for term in range(STAT_TERMS)]
        total = sum(terms[1:], terms[0])
        lse_delta[slot, :, :TILE] = total[:, :TILE] * LOG2E
        lse_delta[slot, :, TILE:] = total[:, TILE:]

    reach = (lax.broadcasted_iota(jnp.int32, (TILE, TILE), 1)
             - lax.broadcasted_iota(jnp.int32, (TILE, TILE), 0))
    reach = jnp.concatenate([reach, reach], axis=1)

    def run(start, refs, first, last):
        keys, values, keys_t, key_sum, value_sum = refs

        def heads_of(kind, tile_at, heads):
            rows = pl.ds(pl.multiple_of(tile_at * TILE, TILE), TILE)
            return jnp.concatenate(
                [heads_ref[kind, rows, pl.ds(head * HEAD_DIM, HEAD_DIM)] for head in heads], axis=0
            )

        def unit_step(at, carry):
            terms = []
            for lane in range(2):
                base = ENTRY * (start + 2 * at + lane)
                turn_q, tile_at, key_at = table[base], table[base + 1], table[base + 2]
                slot = lax.rem(place_ka - tile_at + count_ka, count_ka)
                allowed = reach >= table[base + 3]
                for head in range(0, heads_dev, 2):
                    part = pl.ds(head * HEAD_DIM, 2 * HEAD_DIM)
                    both = (head, head + 1)
                    scores = lax.dot_general(
                        keys[key_at], heads_of(0, tile_at, both), LAST_DIMS, preferred_element_type=F32
                    )
                    dweights = lax.dot_general(
                        values[key_at], heads_of(1, tile_at, both), LAST_DIMS, preferred_element_type=F32
                    )
                    lse_row, delta_row = [
                        jnp.concatenate(
                            [lse_delta[slot, number:number + 1, lanes] for number in both], axis=1
                        )
                        for lanes in (slice(0, TILE), slice(TILE, 2 * TILE))
                    ]
                    weights = jnp.exp2(scores * (score_scale * LOG2E) - lse_row)
                    weights = jnp.where(allowed, weights, 0.0)
                    both_low[lane, :TILE, part] = weights.astype(BF16)
                    both_low[lane, TILE:, part] = (weights * (dweights - delta_row)).astype(BF16)
                every = range(heads_dev)
                right = jnp.concatenate([heads_of(1, tile_at, every), heads_of(0, tile_at, every)], axis=1)
                blocks_of = jnp.dot(both_low[lane], right, preferred_element_type=F32)
                terms.append((
                    turn_q,
                    key_at,
                    blocks_of[:TILE, :HEAD_DIM],
                    blocks_of[TILE:, HEAD_DIM:],
                    jnp.dot(keys_t[key_at], both_low[lane, TILE:, :], preferred_element_type=F32),
                ))
            for turn_q, key_at, value_term, key_term, dq_term in terms:
                value_sum[key_at] += value_term
                key_sum[key_at] += key_term
                dq_sum[turn_q] += dq_term
            return carry

        lax.fori_loop(first, last, unit_step, 0)

    own_at = own_start(count_chip * count_ka, count_ka)
    if stage == 0:
        run(own_at, own, 0, table[0])
    elif stage == 1:
        run(2, other, 0, table[ENTRY])
        for number, dq_half in enumerate(dq_halves):
            part = pl.ds(number * dq_half.shape[1], dq_half.shape[1])
            dq_half[...] = (dq_sum[0, :, part] * score_scale).astype(BF16)
    elif stage == 2:
        run(2, other, table[ENTRY], table[ENTRY + 1])
        run(own_at, own, table[0], table[1])
        dq_out[...] = (dq_sum[1] * score_scale).astype(BF16)
        for local in range(count_chip * count_ka):
            part = pl.ds(local * TILE, TILE)
            kv_other[part, :HEAD_DIM] = (other_key_sum[local] * score_scale).astype(BF16)
            kv_other[part, HEAD_DIM:] = other_value_sum[local].astype(BF16)
    else:
        run(own_at, own, table[1], table[2])
        for number, dq_out in enumerate(dq_outs, 2):
            dq_out[...] = (dq_sum[number] * score_scale).astype(BF16)


def merge_kernel(dims, key_sum, value_sum, kv_back, *rest):
    count_chip, count_ka = dims
    blocks, kv_outs = rest[:count_chip], rest[count_chip:]
    key_gains = jnp.zeros((8, HEAD_DIM), F32)
    value_gains = jnp.zeros((8, HEAD_DIM), F32)
    for number in range(count_chip):
        for step in range(count_ka):
            local = number * count_ka + step
            there = pl.ds(local * TILE, TILE)
            key_total = key_sum[local] * HEAD_DIM ** -0.5 + kv_back[there, :HEAD_DIM].astype(F32)
            value_total = value_sum[local] + kv_back[there, HEAD_DIM:].astype(F32)
            out_ref = kv_outs[number]
            part = pl.ds(step * TILE, TILE)
            out_ref[part, :HEAD_DIM] = key_total.astype(out_ref.dtype)
            out_ref[part, HEAD_DIM:] = value_total.astype(out_ref.dtype)
            key_raw = blocks[number][part, :HEAD_DIM].astype(F32)
            value_raw = blocks[number][part, HEAD_DIM:].astype(F32)
            key_gains += jnp.sum((key_total * key_raw).reshape(TILE // 8, 8, HEAD_DIM), axis=0)
            value_gains += jnp.sum((value_total * value_raw).reshape(TILE // 8, 8, HEAD_DIM), axis=0)
    gains = jnp.concatenate([jnp.sum(key_gains, axis=0, keepdims=True),
                             jnp.sum(value_gains, axis=0, keepdims=True)], axis=1)
    packed = pack_gains(gains)
    for out_ref in kv_outs:
        out_ref[count_ka * TILE:, :] = packed.astype(out_ref.dtype)


def pack_gains(gains):
    rows = lax.broadcasted_iota(jnp.int32, (SPARE, gains.shape[1]), 0)
    high, middle, low = split_float(gains, 3)
    packed = jnp.where(rows == 0, high, jnp.where(rows == 1, middle, low))
    return jnp.where(rows < 3, packed, 0.0)


def add_parts(parts, rows):
    total = parts[0][rows, :]
    for part in parts[1:]:
        total = total + part[rows, :].astype(F32)
    return total


def own_gain(key_gain_ref, value_gain_ref, share):
    kv_at = pl.ds(pl.multiple_of(places()[1] // share * HEAD_DIM, HEAD_DIM), HEAD_DIM)
    return jnp.concatenate([key_gain_ref[:, kv_at], value_gain_ref[:, kv_at]], axis=1)


def collect_kernel(dims, key_gain_ref, value_gain_ref, *rest):
    count_chip, count_ka, share = dims
    parts, outs = rest[:count_chip], rest[count_chip:]
    gain = own_gain(key_gain_ref, value_gain_ref, share)
    total = add_parts(parts, pl.ds(count_ka * TILE, SPARE))
    packed = pack_gains(jnp.sum(total, axis=0, keepdims=True))
    for step, out_ref in enumerate(outs):
        total = add_parts(parts, pl.ds(step * TILE, TILE))
        if share == 1:
            total = total * gain
        out_ref[:TILE, :] = total.astype(out_ref.dtype)
        out_ref[TILE:, :] = packed.astype(out_ref.dtype)


def place_kernel(dims, *rest):
    count_ka, heads_dev, where = dims
    pieces, (dq_out, turned, sems) = rest[:len(where)], rest[len(where):]
    copies = []
    for number, ((step, first), piece) in enumerate(zip(where, pieces)):
        source = lax.rem(places()[1] - step + count_ka, count_ka)
        columns = pl.ds(pl.multiple_of((source * heads_dev + first) * HEAD_DIM, HEAD_DIM), piece.shape[1])
        here = pl.ds(first * HEAD_DIM, piece.shape[1])
        for head in range(piece.shape[1] // HEAD_DIM):
            part = pl.ds(head * HEAD_DIM, HEAD_DIM)
            turned[step, :, pl.ds((first + head) * HEAD_DIM, HEAD_DIM)] = piece[:, part].T
        copies.append(pltpu.make_async_copy(turned.at[step, :, here], dq_out.at[:, columns], sems.at[number]))
        copies[-1].start()
    for copy in copies:
        copy.wait()


def gains_kernel(gains_ref, other_ref, key_gain_out, value_gain_out):
    key_gain_out[...] = gains_ref[0:1, :] + other_ref[0:1, :]
    value_gain_out[...] = gains_ref[1:2, :] + other_ref[1:2, :]


def finish_kernel(dims, key_gain_ref, value_gain_ref, *rest):
    count_ka, share = dims
    pieces, rest = rest[:count_ka], rest[count_ka:]
    dk_out, dv_out, gains_out, sums = rest
    _, place_ka = places()
    sums[...] = jnp.zeros_like(sums)
    for step in range(count_ka):
        source = lax.rem(place_ka + step, count_ka)
        sums[source // share] += pieces[step][...].astype(F32)
    for head in range(count_ka // share):
        part = pl.ds(head * HEAD_DIM, HEAD_DIM)
        key_total = sums[head, :TILE, :HEAD_DIM]
        value_total = sums[head, :TILE, HEAD_DIM:]
        if share > 1:
            key_total = key_total * key_gain_ref[:, part]
            value_total = value_total * value_gain_ref[:, part]
        dk_out[:, part] = key_total.astype(BF16)
        dv_out[:, part] = value_total.astype(BF16)
        gains = jnp.sum(sums[head, TILE:, :], axis=0, keepdims=True)
        gains_out[0:1, part] = gains[:, :HEAD_DIM]
        gains_out[1:2, part] = gains[:, HEAD_DIM:]


def in_vmem(count):
    return [pl.BlockSpec(memory_space=VMEM)] * count


def in_smem(count):
    return [pl.BlockSpec(memory_space=SMEM)] * count


def anywhere(count):
    return [pl.BlockSpec(memory_space=pl.ANY)] * count


def params(mib):
    return pltpu.CompilerParams(vmem_limit_bytes=mib * 1024 * 1024)


def shards(
    queries,
    key_rows,
    values,
    attn_out,
    grad_out,
    log_sums,
    key_gain,
    value_gain,
    doc_ids,
    tile_mask,
    block_order,
):
    count_pb = lax.axis_size("pb")
    count_ka = lax.axis_size("ka")
    rows_dev = key_rows.shape[0]
    query_rows = queries.shape[0]
    heads = log_sums.shape[0]
    feat_width = queries.shape[1]
    kv_heads = key_rows.shape[1] // HEAD_DIM
    heads_dev = heads // count_ka
    share = count_ka // kv_heads
    assert rows_dev == TILE and share * kv_heads == count_ka and count_pb & (count_pb - 1) == 0
    width = heads_dev * HEAD_DIM
    key_gain = key_gain.reshape(1, -1)
    value_gain = value_gain.reshape(1, -1)

    spare = extra_rows(heads_dev)
    count_chip = count_pb // 2

    def swap(array, number):
        return lax.ppermute(array, "pb", [(at, at ^ number) for at in range(count_pb)])

    def turn(array, step):
        return lax.ppermute(array, "ka", [(at, (at + step) % count_ka) for at in range(count_ka)])

    sends = pl.pallas_call(
        functools.partial(prepare_kernel, (count_ka, heads, heads_dev, share)),
        in_specs=anywhere(5),
        out_specs=in_vmem(count_ka),
        out_shape=[jax.ShapeDtypeStruct((TILE + spare, 2 * HEAD_DIM), BF16)] * count_ka,
        scratch_shapes=[VMEM((PARTS, TILE, feat_width // PARTS), BF16)] * 2
        + [VMEM((2, *key_rows.shape), BF16)]
        + [VMEM((heads + 8, TILE), F32)] * 2
        + [pltpu.SemaphoreType.DMA((3, PARTS))],
        compiler_params=params(57),
        name="prepare",
    )(key_rows, values, attn_out, grad_out, log_sums)
    messages = [sends[0]] + [turn(sends[step], step) for step in range(1, count_ka)]

    later_queries, _ = lax.optimization_barrier((queries, sends[0]))
    own_queries = pl.pallas_call(
        own_heads_kernel,
        in_specs=anywhere(2),
        out_specs=in_vmem(1)[0],
        out_shape=jax.ShapeDtypeStruct((2, query_rows, width), BF16),
        scratch_shapes=[pltpu.SemaphoreType.DMA((2,))],
        compiler_params=params(48),
        cost_estimate=pl.CostEstimate(flops=0, bytes_accessed=8 * query_rows * width, transcendentals=0),
        name="own_heads",
    )(later_queries, grad_out)
    messages, own_queries = lax.optimization_barrier((messages, own_queries))
    own_block = jnp.concatenate([message[:TILE] for message in messages], axis=0)
    blocks = [own_block] + [swap(own_block, 2 * number) for number in range(1, count_chip)]
    other_blocks = [swap(block, 1) for block in blocks]
    own_stats = jnp.concatenate([message[TILE:] for message in messages], axis=0)
    later_order, _ = lax.optimization_barrier((block_order, own_block))

    key_tiles = count_chip * count_ka
    sum_shape = jax.ShapeDtypeStruct((key_tiles, TILE, HEAD_DIM), F32)
    key_shape = jax.ShapeDtypeStruct((key_tiles, TILE, HEAD_DIM), BF16)
    kv_shape = (query_rows + SPARE, 2 * HEAD_DIM)
    half = count_ka // 2
    early = (half, 1)
    late = tuple(step for step in range(count_ka) if step not in early)
    order = early + late
    entries = own_start(key_tiles, count_ka) + 1 + count_ka * key_tiles
    table = pl.pallas_call(
        functools.partial(plan_kernel, (count_chip, count_ka, order)),
        in_specs=in_smem(3),
        out_specs=in_smem(1)[0],
        out_shape=jax.ShapeDtypeStruct((ENTRY * entries,), jnp.int32),
        scratch_shapes=[SMEM((3 * count_ka,), jnp.int32)],
        cost_estimate=pl.CostEstimate(flops=0, bytes_accessed=1 << 22, transcendentals=0),
        name="plan",
    )(later_order, doc_ids, tile_mask)

    def attend(stage, outs, scratch, *operands):
        return pl.pallas_call(
            functools.partial(attention_kernel, (count_chip, count_ka, heads_dev, share, stage)),
            in_specs=in_smem(1) + in_vmem(len(operands)),
            out_specs=in_vmem(len(outs)),
            out_shape=outs,
            scratch_shapes=scratch + [
                VMEM((count_ka, head_rows(heads_dev), 2 * TILE), F32),
                VMEM((2, 2 * TILE, width), BF16),
            ],
            compiler_params=params(14 + key_tiles * 11 // 16),
            cost_estimate=pl.CostEstimate(
                flops=5 * count_ka * key_tiles * TILE * TILE * width, bytes_accessed=1 << 20, transcendentals=0
            ),
            name=("attention_first", "attention_leaving", "attention_other", "attention_own")[stage],
        )(table, *operands)

    dq_sums = jax.ShapeDtypeStruct((count_ka, HEAD_DIM, width), F32)
    dq_tile = jax.ShapeDtypeStruct((HEAD_DIM, width), BF16)
    state = [key_shape] * 3 + [sum_shape] * 2
    dq_sum, *own = attend(0, [dq_sums] + state, [], key_gain, value_gain, own_queries, own_stats, *blocks)
    dq_sum, *other = attend(
        1, [dq_sums] + [jax.ShapeDtypeStruct((HEAD_DIM, width // 2), BF16)] * 2 + state, [],
        key_gain, value_gain, own_queries, own_stats, *other_blocks, dq_sum,
    )
    dq_parts = [None] * count_ka
    dq_halves, other = [turn(part, half) for part in other[:2]], other[2:]
    dq_sum, *own[3:], kv_other, dq_second = attend(
        2,
        [dq_sums] + [sum_shape] * 2
        + [jax.ShapeDtypeStruct((key_tiles * TILE, 2 * HEAD_DIM), BF16), dq_tile],
        [VMEM(sum_shape.shape, F32)] * 2,
        own_queries, own_stats, dq_sum, *own, *other,
    )
    kv_other, dq_halves[0] = lax.optimization_barrier((kv_other, dq_halves[0]))
    kv_back = swap(kv_other, 1)
    dq_parts[1] = turn(dq_second, 1)
    *dq_late, key_sum, value_sum = attend(
        3, [dq_tile] * len(late) + [sum_shape] * 2, [VMEM(dq_sums.shape, F32)],
        own_queries, own_stats, dq_sum, *own,
    )
    kv_own = pl.pallas_call(
        functools.partial(merge_kernel, (count_chip, count_ka)),
        in_specs=in_vmem(3 + count_chip),
        out_specs=in_vmem(count_chip),
        out_shape=[jax.ShapeDtypeStruct(kv_shape, BF16 if number else F32) for number in range(count_chip)],
        compiler_params=params(16 + key_tiles // 4),
        name="merge",
    )(key_sum, value_sum, kv_back, *blocks)
    kv_parts = [kv_own[0]] + [swap(kv_own[number], 2 * number) for number in range(1, count_chip)]
    dq_late, dq_parts[1], dq_halves[1] = lax.optimization_barrier((dq_late, dq_parts[1], dq_halves[1]))
    for step, tile in zip(late, dq_late):
        dq_parts[step] = turn(tile, step) if step else tile

    piece_type = BF16 if share == 1 else F32
    piece_shape = (TILE + SPARE, 2 * HEAD_DIM)
    pieces = list(pl.pallas_call(
        functools.partial(collect_kernel, (count_chip, count_ka, share)),
        in_specs=in_vmem(2 + count_chip),
        out_specs=in_vmem(count_ka),
        out_shape=[jax.ShapeDtypeStruct(piece_shape, piece_type if step else F32) for step in range(count_ka)],
        compiler_params=params(24),
        name="collect",
    )(key_gain, value_gain, *kv_parts))
    pieces = [pieces[0]] + [turn(piece, -step) for step, piece in enumerate(pieces[1:], 1)]
    where = ((half, 0), (half, heads_dev // 2)) + tuple((step, 0) for step in order[1:])
    grad_queries = pl.pallas_call(
        functools.partial(place_kernel, (count_ka, heads_dev, where)),
        in_specs=in_vmem(len(where)),
        out_specs=anywhere(1)[0],
        out_shape=jax.ShapeDtypeStruct((rows_dev, feat_width), BF16),
        scratch_shapes=[VMEM((count_ka, TILE, width), BF16), pltpu.SemaphoreType.DMA((len(where),))],
        compiler_params=params(16),
        cost_estimate=pl.CostEstimate(flops=0, bytes_accessed=4 * rows_dev * feat_width, transcendentals=0),
        name="place_queries",
    )(*dq_halves, *[dq_parts[step] for step in order[1:]])
    pieces, grad_queries = lax.optimization_barrier((pieces, grad_queries))
    grad_keys, grad_values, gains = pl.pallas_call(
        functools.partial(finish_kernel, (count_ka, share)),
        in_specs=in_vmem(2 + count_ka),
        out_specs=in_vmem(3),
        out_shape=[
            jax.ShapeDtypeStruct(key_rows.shape, BF16),
            jax.ShapeDtypeStruct(key_rows.shape, BF16),
            jax.ShapeDtypeStruct((2, key_rows.shape[1]), F32),
        ],
        scratch_shapes=[VMEM((kv_heads, TILE + SPARE, 2 * HEAD_DIM), F32)],
        compiler_params=params(16),
        name="finish",
    )(key_gain, value_gain, *pieces)
    grad_key_gain, grad_value_gain = pl.pallas_call(
        gains_kernel,
        in_specs=in_vmem(2),
        out_specs=in_vmem(2),
        out_shape=[jax.ShapeDtypeStruct(key_gain.shape, F32)] * 2,
        compiler_params=params(4),
        name="add_gains",
    )(gains, swap(gains, 1))
    return grad_queries, grad_keys, grad_values, grad_key_gain.reshape(-1), grad_value_gain.reshape(-1)


def solution(mesh):
    placed = (
        P("pb", None),
        P(("pb", "ka"), None),
        P(("pb", "ka"), None),
        P(("pb", "ka"), None),
        P("pb", None),
        P(None, ("pb", "ka")),
        P(),
        P(),
        P(),
        P(),
        P(),
    )
    return jax.shard_map(
        shards,
        mesh=mesh,
        in_specs=placed,
        out_specs=(P(("pb", "ka"), None), P(("pb", "ka"), None), P(("pb", "ka"), None), P(), P()),
        check_vma=False,
    )
```

```python
import functools

import jax
import jax.numpy as jnp
from jax import lax
from jax.experimental import pallas as pl
from jax.experimental.pallas import tpu as pltpu
from jax.sharding import PartitionSpec as P

HEAD_DIM = 128
TILE = 128
SPARE = 16
LOG2E = 1.4426950408889634
ENTRY = 4
PARTS = 4
STAT_TERMS = 2
LAST_DIMS = (((1,), (1,)), ((), ()))
VMEM = pltpu.VMEM
SMEM = pltpu.SMEM
F32 = jnp.float32
BF16 = jnp.bfloat16


def split_float(x, count):
    terms = []
    for _ in range(count):
        terms.append(x.astype(BF16).astype(F32))
        x = x - terms[-1]
    return terms


def head_rows(heads_dev):
    return -(-heads_dev // 8) * 8


def extra_rows(heads_dev):
    return STAT_TERMS * head_rows(heads_dev)


def prepare_kernel(dims, key_ref, value_ref, attn_ref, grads_ref, lse_ref, *rest):
    count_ka, heads, heads_dev, share = dims
    outs, (attn, grad, kv, lse_pad, delta_pad, sems) = rest[:count_ka], rest[count_ka:]
    _, place_ka = places()
    rows8 = head_rows(heads_dev)
    part_heads = heads // PARTS
    rows = pl.ds(pl.multiple_of(place_ka * TILE, TILE), TILE)
    copies = []
    for part in range(PARTS):
        columns = pl.ds(part * part_heads * HEAD_DIM, part_heads * HEAD_DIM)
        copies.append((
            pltpu.make_async_copy(attn_ref.at[:, columns], attn.at[part], sems.at[0, part]),
            pltpu.make_async_copy(grads_ref.at[rows, columns], grad.at[part], sems.at[1, part]),
        ))
    copies.append((
        pltpu.make_async_copy(key_ref, kv.at[0], sems.at[2, 0]),
        pltpu.make_async_copy(value_ref, kv.at[1], sems.at[2, 1]),
        pltpu.make_async_copy(lse_ref, lse_pad.at[pl.ds(0, heads), :], sems.at[2, 2]),
    ))
    for pair in copies:
        for copy in pair:
            copy.start()
    lanes = lax.broadcasted_iota(jnp.int32, (TILE, TILE), 1)
    columns = jnp.zeros((TILE, TILE), F32)
    for part in range(PARTS):
        for copy in copies[part]:
            copy.wait()
        for head in range(part_heads):
            at = pl.ds(head * HEAD_DIM, HEAD_DIM)
            products = grad[part, :, at].astype(F32) * attn[part, :, at].astype(F32)
            total = jnp.sum(products, axis=1, keepdims=True)
            columns = jnp.where(lanes == part * part_heads + head, total, columns)
    delta_pad[...] = jnp.zeros_like(delta_pad)
    lse_pad[pl.ds(heads, 8), :] = jnp.zeros((8, TILE), F32)
    delta_pad[:heads, :] = columns.T[:heads, :]
    for copy in copies[-1]:
        copy.wait()
    for step in range(count_ka):
        target = lax.rem(place_ka + step, count_ka)
        kv_at = pl.ds(pl.multiple_of(target // share * HEAD_DIM, HEAD_DIM), HEAD_DIM)
        outs[step][:TILE, :HEAD_DIM] = kv[0, :, kv_at]
        outs[step][:TILE, HEAD_DIM:] = kv[1, :, kv_at]
        head_at = pl.ds(target * heads_dev, rows8)
        both = jnp.concatenate([lse_pad[head_at, :], delta_pad[head_at, :]], axis=1)
        outs[step][TILE:, :] = jnp.concatenate(split_float(both, STAT_TERMS), axis=0).astype(BF16)


def own_heads_kernel(queries_ref, grads_ref, out_ref, sems):
    _, place_ka = places()
    width = out_ref.shape[2]
    columns = pl.ds(pl.multiple_of(place_ka * width, HEAD_DIM), width)
    copies = [
        pltpu.make_async_copy(ref.at[:, columns], out_ref.at[number], sems.at[number])
        for number, ref in enumerate((queries_ref, grads_ref))
    ]
    for copy in copies:
        copy.start()
    for copy in copies:
        copy.wait()


def places():
    return lax.axis_index("pb"), lax.axis_index("ka")


def own_start(key_tiles, count_ka):
    return 3 + count_ka * key_tiles


def plan_kernel(dims, order_ref, doc_ref, mask_ref, table, counts):
    count_chip, count_ka, order = dims
    place_pb, place_ka = places()
    own_at = own_start(count_chip * count_ka, count_ka)

    def walk(start, query_pb, key_pb, steps, units, count_at=None):
        def query_step(turn_q, units):
            before = units
            step_q = jnp.int32(order[0])
            for number, step in enumerate(order):
                step_q = jnp.where(turn_q == number, step, step_q)
            tile_at = lax.rem(place_ka + step_q, count_ka)
            seq_q = order_ref[query_pb * count_ka + tile_at]
            doc_q = doc_ref[seq_q]

            def collect(number, units):
                for step in range(count_ka):
                    stored = (key_pb ^ (2 * number)) * count_ka + lax.rem(
                        place_ka - step + count_ka, count_ka
                    )
                    seq_k = order_ref[stored]
                    live = (mask_ref[seq_q, seq_k] == 1) & (doc_ref[seq_k] == doc_q) & (seq_q >= seq_k)
                    if start is not None:
                        base = ENTRY * (start + units)
                        table[base] = turn_q
                        table[base + 1] = tile_at
                        table[base + 2] = number * count_ka + step
                        table[base + 3] = jnp.where(seq_q == seq_k, 0, -TILE)
                    units = units + live.astype(jnp.int32)
                return units

            units = lax.fori_loop(0, count_chip, collect, units)
            if start is not None:
                base = ENTRY * (start + units)
                table[base] = turn_q
                table[base + 1] = tile_at
                table[base + 2] = 0
                table[base + 3] = TILE
            units = 2 * ((units + 1) // 2)
            if count_at is not None:
                counts[count_at + tile_at] = units - before
            return units

        return lax.fori_loop(*steps, query_step, units)

    def steps_of(units):
        return units // 2

    none = jnp.int32(0)
    sibling = place_pb ^ 1
    every = (0, count_ka)
    other = steps_of(walk(2, place_pb, sibling, every, none, 2 * count_ka))
    own = steps_of(walk(own_at, place_pb, place_pb, every, none, 0))
    walk(None, sibling, sibling, every, none, count_ka)
    sibling_other = steps_of(walk(None, sibling, place_pb, every, none))

    def first_steps(place):
        tile = lax.rem(place + order[0], count_ka)
        return steps_of(counts[tile]), steps_of(counts[2 * count_ka + tile])

    first, second = none, none
    for place in range(count_ka):
        first = jnp.maximum(first, sum(first_steps(place)))
        for core, others in enumerate((other, sibling_other)):
            units = sum([counts[core * count_ka + (place + step) % count_ka] for step in order[:2]])
            second = jnp.maximum(second, others + steps_of(units))
    own_first, other_first = first_steps(place_ka)
    table[0] = own_first
    table[1] = jnp.minimum(second - other, own)
    table[2] = own
    table[ENTRY] = jnp.clip(first - own_first, other_first, other)
    table[ENTRY + 1] = other


def attention_kernel(dims, *rest):
    count_chip, count_ka, heads_dev, share, stage = dims
    table, rest = rest[0], rest[1:]
    if stage < 2:
        (key_gain_ref, value_gain_ref), rest = rest[:2], rest[2:]
    (heads_ref, stats_ref), rest = rest[:2], rest[2:]
    if stage < 2:
        blocks, rest = rest[:count_chip], rest[count_chip:]
    if stage == 0:
        (dq_sum, *own), rest = rest[:6], rest[6:]
    elif stage == 1:
        (dq_start, dq_sum, *dq_halves), other, rest = rest[:4], rest[4:9], rest[9:]
    elif stage == 2:
        (dq_start, *own_start_refs), rest = rest[:6], rest[6:]
        other_refs, rest = rest[:5], rest[5:]
        (dq_sum, *own_sums, kv_other, dq_out, other_key_sum, other_value_sum), rest = rest[:7], rest[7:]
        own = own_start_refs[:3] + own_sums
        other = other_refs[:3] + (other_key_sum, other_value_sum)
    else:
        (dq_start, *own_start_refs), rest = rest[:6], rest[6:]
        dq_outs, rest = rest[:count_ka - 2], rest[count_ka - 2:]
        (*own_sums, dq_sum), rest = rest[:3], rest[3:]
        own = own_start_refs[:3] + own_sums
    lse_delta, weights_low, dscores_low = rest
    _, place_ka = places()
    rows8 = head_rows(heads_dev)
    spare = extra_rows(heads_dev)
    score_scale = HEAD_DIM ** -0.5

    if stage < 2:
        kv_at = pl.ds(pl.multiple_of(place_ka // share * HEAD_DIM, HEAD_DIM), HEAD_DIM)
        key_gain = key_gain_ref[:, kv_at]
        value_gain = value_gain_ref[:, kv_at]
        keys, values, keys_t, key_sum, value_sum = other if stage else own
        for number in range(count_chip):
            for step in range(count_ka):
                part = pl.ds(step * TILE, TILE)
                local = number * count_ka + step
                key_tile = (blocks[number][part, :HEAD_DIM].astype(F32) * key_gain).astype(BF16)
                value_tile = (blocks[number][part, HEAD_DIM:].astype(F32) * value_gain).astype(BF16)
                keys[local] = key_tile
                values[local] = value_tile
                keys_t[local] = key_tile.T
        key_sum[...] = jnp.zeros_like(key_sum)
        value_sum[...] = jnp.zeros_like(value_sum)
    else:
        for target, source in zip(own_sums, own_start_refs[3:]):
            target[...] = source[...]
    if stage == 0:
        dq_sum[...] = jnp.zeros_like(dq_sum)
    else:
        dq_sum[...] = dq_start[...]
    if stage == 2:
        other_key_sum[...] = other_refs[3][...]
        other_value_sum[...] = other_refs[4][...]

    for slot in range(count_ka):
        packed = stats_ref[pl.ds(slot * spare, spare), :].astype(F32)
        terms = [packed[term * rows8:(term + 1) * rows8] for term in range(STAT_TERMS)]
        total = sum(terms[1:], terms[0])
        lse_delta[slot, :, :TILE] = total[:, :TILE] * LOG2E
        lse_delta[slot, :, TILE:] = total[:, TILE:]

    reach = (lax.broadcasted_iota(jnp.int32, (TILE, TILE), 1)
             - lax.broadcasted_iota(jnp.int32, (TILE, TILE), 0))
    reach = jnp.concatenate([jnp.concatenate([reach, reach], axis=1)] * 2, axis=0)
    lower = lax.broadcasted_iota(jnp.int32, (2 * TILE, 2 * TILE), 0) < TILE

    def run(start, refs, first, last):
        keys, values, keys_t, key_sum, value_sum = refs

        def heads_of(kind, tile_at, heads):
            rows = pl.ds(pl.multiple_of(tile_at * TILE, TILE), TILE)
            return jnp.concatenate(
                [heads_ref[kind, rows, pl.ds(head * HEAD_DIM, HEAD_DIM)] for head in heads], axis=0
            )

        def pair_step(at, carry):
            base = ENTRY * (start + 2 * at)
            turn_q, tile_at, one = table[base], table[base + 1], table[base + 2]
            two = table[base + ENTRY + 2]
            slot = lax.rem(place_ka - tile_at + count_ka, count_ka)
            allowed = reach >= jnp.where(lower, table[base + 3], table[base + ENTRY + 3])
            key_pair = jnp.concatenate([keys[one], keys[two]], axis=0)
            value_pair = jnp.concatenate([values[one], values[two]], axis=0)
            key_turn = jnp.concatenate([keys_t[one], keys_t[two]], axis=1)
            for head in range(0, heads_dev, 2):
                part = pl.ds(head * HEAD_DIM, 2 * HEAD_DIM)
                both = (head, head + 1)
                scores = lax.dot_general(
                    key_pair, heads_of(0, tile_at, both), LAST_DIMS, preferred_element_type=F32
                )
                dweights = lax.dot_general(
                    value_pair, heads_of(1, tile_at, both), LAST_DIMS, preferred_element_type=F32
                )
                lse_row, delta_row = [
                    jnp.concatenate([lse_delta[slot, number:number + 1, lanes] for number in both], axis=1)
                    for lanes in (slice(0, TILE), slice(TILE, 2 * TILE))
                ]
                weights = jnp.exp2(scores * (score_scale * LOG2E) - lse_row)
                weights = jnp.where(allowed, weights, 0.0)
                weights_low[:, part] = weights.astype(BF16)
                dscores_low[:, part] = (weights * (dweights - delta_row)).astype(BF16)
            every = range(heads_dev)
            value_term = jnp.dot(weights_low[...], heads_of(1, tile_at, every), preferred_element_type=F32)
            key_term = jnp.dot(dscores_low[...], heads_of(0, tile_at, every), preferred_element_type=F32)
            dq_sum[turn_q] += jnp.dot(key_turn, dscores_low[...], preferred_element_type=F32)
            value_sum[one] += value_term[:TILE]
            key_sum[one] += key_term[:TILE]
            value_sum[two] += value_term[TILE:]
            key_sum[two] += key_term[TILE:]
            return carry

        lax.fori_loop(first, last, pair_step, 0)

    own_at = own_start(count_chip * count_ka, count_ka)
    if stage == 0:
        run(own_at, own, 0, table[0])
    elif stage == 1:
        run(2, other, 0, table[ENTRY])
        for number, dq_half in enumerate(dq_halves):
            part = pl.ds(number * dq_half.shape[1], dq_half.shape[1])
            dq_half[...] = (dq_sum[0, :, part] * score_scale).astype(BF16)
    elif stage == 2:
        run(2, other, table[ENTRY], table[ENTRY + 1])
        run(own_at, own, table[0], table[1])
        dq_out[...] = (dq_sum[1] * score_scale).astype(BF16)
        for local in range(count_chip * count_ka):
            part = pl.ds(local * TILE, TILE)
            kv_other[part, :HEAD_DIM] = (other_key_sum[local] * score_scale).astype(BF16)
            kv_other[part, HEAD_DIM:] = other_value_sum[local].astype(BF16)
    else:
        run(own_at, own, table[1], table[2])
        for number, dq_out in enumerate(dq_outs, 2):
            dq_out[...] = (dq_sum[number] * score_scale).astype(BF16)


def merge_kernel(dims, key_sum, value_sum, kv_back, *rest):
    count_chip, count_ka = dims
    blocks, kv_outs = rest[:count_chip], rest[count_chip:]
    key_gains = jnp.zeros((8, HEAD_DIM), F32)
    value_gains = jnp.zeros((8, HEAD_DIM), F32)
    for number in range(count_chip):
        for step in range(count_ka):
            local = number * count_ka + step
            there = pl.ds(local * TILE, TILE)
            key_total = key_sum[local] * HEAD_DIM ** -0.5 + kv_back[there, :HEAD_DIM].astype(F32)
            value_total = value_sum[local] + kv_back[there, HEAD_DIM:].astype(F32)
            out_ref = kv_outs[number]
            part = pl.ds(step * TILE, TILE)
            out_ref[part, :HEAD_DIM] = key_total.astype(out_ref.dtype)
            out_ref[part, HEAD_DIM:] = value_total.astype(out_ref.dtype)
            key_raw = blocks[number][part, :HEAD_DIM].astype(F32)
            value_raw = blocks[number][part, HEAD_DIM:].astype(F32)
            key_gains += jnp.sum((key_total * key_raw).reshape(TILE // 8, 8, HEAD_DIM), axis=0)
            value_gains += jnp.sum((value_total * value_raw).reshape(TILE // 8, 8, HEAD_DIM), axis=0)
    gains = jnp.concatenate([jnp.sum(key_gains, axis=0, keepdims=True),
                             jnp.sum(value_gains, axis=0, keepdims=True)], axis=1)
    packed = pack_gains(gains)
    for out_ref in kv_outs:
        out_ref[count_ka * TILE:, :] = packed.astype(out_ref.dtype)


def pack_gains(gains):
    rows = lax.broadcasted_iota(jnp.int32, (SPARE, gains.shape[1]), 0)
    high, middle, low = split_float(gains, 3)
    packed = jnp.where(rows == 0, high, jnp.where(rows == 1, middle, low))
    return jnp.where(rows < 3, packed, 0.0)


def add_parts(parts, rows):
    total = parts[0][rows, :]
    for part in parts[1:]:
        total = total + part[rows, :].astype(F32)
    return total


def own_gain(key_gain_ref, value_gain_ref, share):
    kv_at = pl.ds(pl.multiple_of(places()[1] // share * HEAD_DIM, HEAD_DIM), HEAD_DIM)
    return jnp.concatenate([key_gain_ref[:, kv_at], value_gain_ref[:, kv_at]], axis=1)


def collect_kernel(dims, key_gain_ref, value_gain_ref, *rest):
    count_chip, count_ka, share = dims
    parts, outs = rest[:count_chip], rest[count_chip:]
    gain = own_gain(key_gain_ref, value_gain_ref, share)
    total = add_parts(parts, pl.ds(count_ka * TILE, SPARE))
    packed = pack_gains(jnp.sum(total, axis=0, keepdims=True))
    for step, out_ref in enumerate(outs):
        total = add_parts(parts, pl.ds(step * TILE, TILE))
        if share == 1:
            total = total * gain
        out_ref[:TILE, :] = total.astype(out_ref.dtype)
        out_ref[TILE:, :] = packed.astype(out_ref.dtype)


def place_kernel(dims, *rest):
    count_ka, heads_dev, where = dims
    pieces, (dq_out, turned, sems) = rest[:len(where)], rest[len(where):]
    copies = []
    for number, ((step, first), piece) in enumerate(zip(where, pieces)):
        source = lax.rem(places()[1] - step + count_ka, count_ka)
        columns = pl.ds(pl.multiple_of((source * heads_dev + first) * HEAD_DIM, HEAD_DIM), piece.shape[1])
        here = pl.ds(first * HEAD_DIM, piece.shape[1])
        for head in range(piece.shape[1] // HEAD_DIM):
            part = pl.ds(head * HEAD_DIM, HEAD_DIM)
            turned[step, :, pl.ds((first + head) * HEAD_DIM, HEAD_DIM)] = piece[:, part].T
        copies.append(pltpu.make_async_copy(turned.at[step, :, here], dq_out.at[:, columns], sems.at[number]))
        copies[-1].start()
    for copy in copies:
        copy.wait()


def gains_kernel(gains_ref, other_ref, key_gain_out, value_gain_out):
    key_gain_out[...] = gains_ref[0:1, :] + other_ref[0:1, :]
    value_gain_out[...] = gains_ref[1:2, :] + other_ref[1:2, :]


def finish_kernel(dims, key_gain_ref, value_gain_ref, *rest):
    count_ka, share = dims
    pieces, rest = rest[:count_ka], rest[count_ka:]
    dk_out, dv_out, gains_out, sums = rest
    _, place_ka = places()
    sums[...] = jnp.zeros_like(sums)
    for step in range(count_ka):
        source = lax.rem(place_ka + step, count_ka)
        sums[source // share] += pieces[step][...].astype(F32)
    for head in range(count_ka // share):
        part = pl.ds(head * HEAD_DIM, HEAD_DIM)
        key_total = sums[head, :TILE, :HEAD_DIM]
        value_total = sums[head, :TILE, HEAD_DIM:]
        if share > 1:
            key_total = key_total * key_gain_ref[:, part]
            value_total = value_total * value_gain_ref[:, part]
        dk_out[:, part] = key_total.astype(BF16)
        dv_out[:, part] = value_total.astype(BF16)
        gains = jnp.sum(sums[head, TILE:, :], axis=0, keepdims=True)
        gains_out[0:1, part] = gains[:, :HEAD_DIM]
        gains_out[1:2, part] = gains[:, HEAD_DIM:]


def in_vmem(count):
    return [pl.BlockSpec(memory_space=VMEM)] * count


def in_smem(count):
    return [pl.BlockSpec(memory_space=SMEM)] * count


def anywhere(count):
    return [pl.BlockSpec(memory_space=pl.ANY)] * count


def params(mib):
    return pltpu.CompilerParams(vmem_limit_bytes=mib * 1024 * 1024)


def shards(
    queries,
    key_rows,
    values,
    attn_out,
    grad_out,
    log_sums,
    key_gain,
    value_gain,
    doc_ids,
    tile_mask,
    block_order,
):
    count_pb = lax.axis_size("pb")
    count_ka = lax.axis_size("ka")
    rows_dev = key_rows.shape[0]
    query_rows = queries.shape[0]
    heads = log_sums.shape[0]
    feat_width = queries.shape[1]
    kv_heads = key_rows.shape[1] // HEAD_DIM
    heads_dev = heads // count_ka
    share = count_ka // kv_heads
    assert rows_dev == TILE and share * kv_heads == count_ka and count_pb & (count_pb - 1) == 0
    width = heads_dev * HEAD_DIM
    key_gain = key_gain.reshape(1, -1)
    value_gain = value_gain.reshape(1, -1)

    spare = extra_rows(heads_dev)
    count_chip = count_pb // 2

    def swap(array, number):
        return lax.ppermute(array, "pb", [(at, at ^ number) for at in range(count_pb)])

    def turn(array, step):
        return lax.ppermute(array, "ka", [(at, (at + step) % count_ka) for at in range(count_ka)])

    sends = pl.pallas_call(
        functools.partial(prepare_kernel, (count_ka, heads, heads_dev, share)),
        in_specs=anywhere(5),
        out_specs=in_vmem(count_ka),
        out_shape=[jax.ShapeDtypeStruct((TILE + spare, 2 * HEAD_DIM), BF16)] * count_ka,
        scratch_shapes=[VMEM((PARTS, TILE, feat_width // PARTS), BF16)] * 2
        + [VMEM((2, *key_rows.shape), BF16)]
        + [VMEM((heads + 8, TILE), F32)] * 2
        + [pltpu.SemaphoreType.DMA((3, PARTS))],
        compiler_params=params(57),
        name="prepare",
    )(key_rows, values, attn_out, grad_out, log_sums)
    messages = [sends[0]] + [turn(sends[step], step) for step in range(1, count_ka)]

    later_queries, _ = lax.optimization_barrier((queries, sends[0]))
    own_queries = pl.pallas_call(
        own_heads_kernel,
        in_specs=anywhere(2),
        out_specs=in_vmem(1)[0],
        out_shape=jax.ShapeDtypeStruct((2, query_rows, width), BF16),
        scratch_shapes=[pltpu.SemaphoreType.DMA((2,))],
        compiler_params=params(48),
        cost_estimate=pl.CostEstimate(flops=0, bytes_accessed=8 * query_rows * width, transcendentals=0),
        name="own_heads",
    )(later_queries, grad_out)
    messages, own_queries = lax.optimization_barrier((messages, own_queries))
    own_block = jnp.concatenate([message[:TILE] for message in messages], axis=0)
    blocks = [own_block] + [swap(own_block, 2 * number) for number in range(1, count_chip)]
    other_blocks = [swap(block, 1) for block in blocks]
    own_stats = jnp.concatenate([message[TILE:] for message in messages], axis=0)
    later_order, _ = lax.optimization_barrier((block_order, own_block))

    key_tiles = count_chip * count_ka
    sum_shape = jax.ShapeDtypeStruct((key_tiles, TILE, HEAD_DIM), F32)
    key_shape = jax.ShapeDtypeStruct((key_tiles, TILE, HEAD_DIM), BF16)
    kv_shape = (query_rows + SPARE, 2 * HEAD_DIM)
    half = count_ka // 2
    early = (half, 1)
    late = tuple(step for step in range(count_ka) if step not in early)
    order = early + late
    entries = own_start(key_tiles, count_ka) + 1 + count_ka * key_tiles
    table = pl.pallas_call(
        functools.partial(plan_kernel, (count_chip, count_ka, order)),
        in_specs=in_smem(3),
        out_specs=in_smem(1)[0],
        out_shape=jax.ShapeDtypeStruct((ENTRY * entries,), jnp.int32),
        scratch_shapes=[SMEM((3 * count_ka,), jnp.int32)],
        cost_estimate=pl.CostEstimate(flops=0, bytes_accessed=1 << 22, transcendentals=0),
        name="plan",
    )(later_order, doc_ids, tile_mask)

    def attend(stage, outs, scratch, *operands):
        return pl.pallas_call(
            functools.partial(attention_kernel, (count_chip, count_ka, heads_dev, share, stage)),
            in_specs=in_smem(1) + in_vmem(len(operands)),
            out_specs=in_vmem(len(outs)),
            out_shape=outs,
            scratch_shapes=scratch + [
                VMEM((count_ka, head_rows(heads_dev), 2 * TILE), F32),
                VMEM((2 * TILE, width), BF16),
                VMEM((2 * TILE, width), BF16),
            ],
            compiler_params=params(14 + key_tiles * 11 // 16),
            cost_estimate=pl.CostEstimate(
                flops=5 * count_ka * key_tiles * TILE * TILE * width, bytes_accessed=1 << 20, transcendentals=0
            ),
            name=("attention_first", "attention_leaving", "attention_other", "attention_own")[stage],
        )(table, *operands)

    dq_sums = jax.ShapeDtypeStruct((count_ka, HEAD_DIM, width), F32)
    dq_tile = jax.ShapeDtypeStruct((HEAD_DIM, width), BF16)
    state = [key_shape] * 3 + [sum_shape] * 2
    dq_sum, *own = attend(0, [dq_sums] + state, [], key_gain, value_gain, own_queries, own_stats, *blocks)
    dq_sum, *other = attend(
        1, [dq_sums] + [jax.ShapeDtypeStruct((HEAD_DIM, width // 2), BF16)] * 2 + state, [],
        key_gain, value_gain, own_queries, own_stats, *other_blocks, dq_sum,
    )
    dq_parts = [None] * count_ka
    dq_halves, other = [turn(part, half) for part in other[:2]], other[2:]
    dq_sum, *own[3:], kv_other, dq_second = attend(
        2,
        [dq_sums] + [sum_shape] * 2
        + [jax.ShapeDtypeStruct((key_tiles * TILE, 2 * HEAD_DIM), BF16), dq_tile],
        [VMEM(sum_shape.shape, F32)] * 2,
        own_queries, own_stats, dq_sum, *own, *other,
    )
    kv_other, dq_halves[0] = lax.optimization_barrier((kv_other, dq_halves[0]))
    kv_back = swap(kv_other, 1)
    dq_parts[1] = turn(dq_second, 1)
    *dq_late, key_sum, value_sum = attend(
        3, [dq_tile] * len(late) + [sum_shape] * 2, [VMEM(dq_sums.shape, F32)],
        own_queries, own_stats, dq_sum, *own,
    )
    kv_own = pl.pallas_call(
        functools.partial(merge_kernel, (count_chip, count_ka)),
        in_specs=in_vmem(3 + count_chip),
        out_specs=in_vmem(count_chip),
        out_shape=[jax.ShapeDtypeStruct(kv_shape, BF16 if number else F32) for number in range(count_chip)],
        compiler_params=params(16 + key_tiles // 4),
        name="merge",
    )(key_sum, value_sum, kv_back, *blocks)
    kv_parts = [kv_own[0]] + [swap(kv_own[number], 2 * number) for number in range(1, count_chip)]
    dq_late, dq_parts[1], dq_halves[1] = lax.optimization_barrier((dq_late, dq_parts[1], dq_halves[1]))
    for step, tile in zip(late, dq_late):
        dq_parts[step] = turn(tile, step) if step else tile

    piece_type = BF16 if share == 1 else F32
    piece_shape = (TILE + SPARE, 2 * HEAD_DIM)
    pieces = list(pl.pallas_call(
        functools.partial(collect_kernel, (count_chip, count_ka, share)),
        in_specs=in_vmem(2 + count_chip),
        out_specs=in_vmem(count_ka),
        out_shape=[jax.ShapeDtypeStruct(piece_shape, piece_type if step else F32) for step in range(count_ka)],
        compiler_params=params(24),
        name="collect",
    )(key_gain, value_gain, *kv_parts))
    pieces = [pieces[0]] + [turn(piece, -step) for step, piece in enumerate(pieces[1:], 1)]
    where = ((half, 0), (half, heads_dev // 2)) + tuple((step, 0) for step in order[1:])
    grad_queries = pl.pallas_call(
        functools.partial(place_kernel, (count_ka, heads_dev, where)),
        in_specs=in_vmem(len(where)),
        out_specs=anywhere(1)[0],
        out_shape=jax.ShapeDtypeStruct((rows_dev, feat_width), BF16),
        scratch_shapes=[VMEM((count_ka, TILE, width), BF16), pltpu.SemaphoreType.DMA((len(where),))],
        compiler_params=params(16),
        cost_estimate=pl.CostEstimate(flops=0, bytes_accessed=4 * rows_dev * feat_width, transcendentals=0),
        name="place_queries",
    )(*dq_halves, *[dq_parts[step] for step in order[1:]])
    pieces, grad_queries = lax.optimization_barrier((pieces, grad_queries))
    grad_keys, grad_values, gains = pl.pallas_call(
        functools.partial(finish_kernel, (count_ka, share)),
        in_specs=in_vmem(2 + count_ka),
        out_specs=in_vmem(3),
        out_shape=[
            jax.ShapeDtypeStruct(key_rows.shape, BF16),
            jax.ShapeDtypeStruct(key_rows.shape, BF16),
            jax.ShapeDtypeStruct((2, key_rows.shape[1]), F32),
        ],
        scratch_shapes=[VMEM((kv_heads, TILE + SPARE, 2 * HEAD_DIM), F32)],
        compiler_params=params(16),
        name="finish",
    )(key_gain, value_gain, *pieces)
    grad_key_gain, grad_value_gain = pl.pallas_call(
        gains_kernel,
        in_specs=in_vmem(2),
        out_specs=in_vmem(2),
        out_shape=[jax.ShapeDtypeStruct(key_gain.shape, F32)] * 2,
        compiler_params=params(4),
        name="add_gains",
    )(gains, swap(gains, 1))
    return grad_queries, grad_keys, grad_values, grad_key_gain.reshape(-1), grad_value_gain.reshape(-1)


def solution(mesh):
    placed = (
        P("pb", None),
        P(("pb", "ka"), None),
        P(("pb", "ka"), None),
        P(("pb", "ka"), None),
        P("pb", None),
        P(None, ("pb", "ka")),
        P(),
        P(),
        P(),
        P(),
        P(),
    )
    return jax.shard_map(
        shards,
        mesh=mesh,
        in_specs=placed,
        out_specs=(P(("pb", "ka"), None), P(("pb", "ka"), None), P(("pb", "ka"), None), P(), P()),
        check_vma=False,
    )
```

```python
import functools

import jax
import jax.numpy as jnp
from jax import lax
from jax.experimental import pallas as pl
from jax.experimental.pallas import tpu as pltpu
from jax.sharding import PartitionSpec as P

HEAD_DIM = 128
TILE = 128
SPARE = 16
LOG2E = 1.4426950408889634
ENTRY = 4
PARTS = 4
STAT_TERMS = 2
LAST_DIMS = (((1,), (1,)), ((), ()))
VMEM = pltpu.VMEM
SMEM = pltpu.SMEM
F32 = jnp.float32
BF16 = jnp.bfloat16


def split_float(x, count):
    terms = []
    for _ in range(count):
        terms.append(x.astype(BF16).astype(F32))
        x = x - terms[-1]
    return terms


def head_rows(heads_dev):
    return -(-heads_dev // 8) * 8


def extra_rows(heads_dev):
    return STAT_TERMS * head_rows(heads_dev)


def prepare_kernel(dims, key_ref, value_ref, attn_ref, grads_ref, lse_ref, *rest):
    count_ka, heads, heads_dev, share = dims
    outs, (attn, grad, kv, lse_pad, delta_pad, sems) = rest[:count_ka], rest[count_ka:]
    _, place_ka = places()
    rows8 = head_rows(heads_dev)
    part_heads = heads // PARTS
    rows = pl.ds(pl.multiple_of(place_ka * TILE, TILE), TILE)
    copies = []
    for part in range(PARTS):
        columns = pl.ds(part * part_heads * HEAD_DIM, part_heads * HEAD_DIM)
        copies.append((
            pltpu.make_async_copy(attn_ref.at[:, columns], attn.at[part], sems.at[0, part]),
            pltpu.make_async_copy(grads_ref.at[rows, columns], grad.at[part], sems.at[1, part]),
        ))
    copies.append((
        pltpu.make_async_copy(key_ref, kv.at[0], sems.at[2, 0]),
        pltpu.make_async_copy(value_ref, kv.at[1], sems.at[2, 1]),
        pltpu.make_async_copy(lse_ref, lse_pad.at[pl.ds(0, heads), :], sems.at[2, 2]),
    ))
    for pair in copies:
        for copy in pair:
            copy.start()
    lanes = lax.broadcasted_iota(jnp.int32, (TILE, TILE), 1)
    columns = jnp.zeros((TILE, TILE), F32)
    for part in range(PARTS):
        for copy in copies[part]:
            copy.wait()
        for head in range(part_heads):
            at = pl.ds(head * HEAD_DIM, HEAD_DIM)
            products = grad[part, :, at].astype(F32) * attn[part, :, at].astype(F32)
            total = jnp.sum(products, axis=1, keepdims=True)
            columns = jnp.where(lanes == part * part_heads + head, total, columns)
    delta_pad[...] = jnp.zeros_like(delta_pad)
    lse_pad[pl.ds(heads, 8), :] = jnp.zeros((8, TILE), F32)
    delta_pad[:heads, :] = columns.T[:heads, :]
    for copy in copies[-1]:
        copy.wait()
    for step in range(count_ka):
        target = lax.rem(place_ka + step, count_ka)
        kv_at = pl.ds(pl.multiple_of(target // share * HEAD_DIM, HEAD_DIM), HEAD_DIM)
        outs[step][:TILE, :HEAD_DIM] = kv[0, :, kv_at]
        outs[step][:TILE, HEAD_DIM:] = kv[1, :, kv_at]
        head_at = pl.ds(target * heads_dev, rows8)
        both = jnp.concatenate([lse_pad[head_at, :], delta_pad[head_at, :]], axis=1)
        outs[step][TILE:, :] = jnp.concatenate(split_float(both, STAT_TERMS), axis=0).astype(BF16)


def own_heads_kernel(queries_ref, grads_ref, out_ref, sems):
    _, place_ka = places()
    width = out_ref.shape[2]
    columns = pl.ds(pl.multiple_of(place_ka * width, HEAD_DIM), width)
    copies = [
        pltpu.make_async_copy(ref.at[:, columns], out_ref.at[number], sems.at[number])
        for number, ref in enumerate((queries_ref, grads_ref))
    ]
    for copy in copies:
        copy.start()
    for copy in copies:
        copy.wait()


def places():
    return lax.axis_index("pb"), lax.axis_index("ka")


def own_start(key_tiles, count_ka):
    return 3 + count_ka * key_tiles


def plan_kernel(dims, order_ref, doc_ref, mask_ref, table, counts):
    count_chip, count_ka, order = dims
    place_pb, place_ka = places()
    own_at = own_start(count_chip * count_ka, count_ka)

    def walk(start, query_pb, key_pb, steps, units, count_at=None):
        def query_step(turn_q, units):
            before = units
            step_q = jnp.int32(order[0])
            for number, step in enumerate(order):
                step_q = jnp.where(turn_q == number, step, step_q)
            tile_at = lax.rem(place_ka + step_q, count_ka)
            seq_q = order_ref[query_pb * count_ka + tile_at]
            doc_q = doc_ref[seq_q]

            def collect(number, units):
                for step in range(count_ka):
                    stored = (key_pb ^ (2 * number)) * count_ka + lax.rem(
                        place_ka - step + count_ka, count_ka
                    )
                    seq_k = order_ref[stored]
                    live = (mask_ref[seq_q, seq_k] == 1) & (doc_ref[seq_k] == doc_q) & (seq_q >= seq_k)
                    if start is not None:
                        base = ENTRY * (start + units)
                        table[base] = turn_q
                        table[base + 1] = tile_at
                        table[base + 2] = number * count_ka + step
                        table[base + 3] = jnp.where(seq_q == seq_k, 0, -TILE)
                    units = units + live.astype(jnp.int32)
                return units

            units = lax.fori_loop(0, count_chip, collect, units)
            if start is not None:
                base = ENTRY * (start + units)
                table[base] = turn_q
                table[base + 1] = tile_at
                table[base + 2] = 0
                table[base + 3] = TILE
            units = 2 * ((units + 1) // 2)
            if count_at is not None:
                counts[count_at + tile_at] = units - before
            return units

        return lax.fori_loop(*steps, query_step, units)

    def steps_of(units):
        return units // 2

    none = jnp.int32(0)
    sibling = place_pb ^ 1
    every = (0, count_ka)
    other = steps_of(walk(2, place_pb, sibling, every, none, 2 * count_ka))
    own = steps_of(walk(own_at, place_pb, place_pb, every, none, 0))
    walk(None, sibling, sibling, every, none, count_ka)
    sibling_other = steps_of(walk(None, sibling, place_pb, every, none))

    def first_steps(place):
        tile = lax.rem(place + order[0], count_ka)
        return steps_of(counts[tile]), steps_of(counts[2 * count_ka + tile])

    first, second = none, none
    for place in range(count_ka):
        first = jnp.maximum(first, sum(first_steps(place)))
        for core, others in enumerate((other, sibling_other)):
            units = sum([counts[core * count_ka + (place + step) % count_ka] for step in order[:1]])
            second = jnp.maximum(second, others + steps_of(units))
    own_first, other_first = first_steps(place_ka)
    table[0] = own_first
    table[1] = jnp.minimum(second - other, own)
    table[2] = own
    table[ENTRY] = jnp.clip(first - own_first, other_first, other)
    table[ENTRY + 1] = other


def attention_kernel(dims, *rest):
    count_chip, count_ka, heads_dev, share, stage = dims
    table, rest = rest[0], rest[1:]
    if stage < 2:
        (key_gain_ref, value_gain_ref), rest = rest[:2], rest[2:]
    (heads_ref, stats_ref), rest = rest[:2], rest[2:]
    if stage < 2:
        blocks, rest = rest[:count_chip], rest[count_chip:]
    if stage == 0:
        (dq_sum, *own), rest = rest[:6], rest[6:]
    elif stage == 1:
        (dq_start, dq_sum, *dq_halves), other, rest = rest[:4], rest[4:9], rest[9:]
    elif stage == 2:
        (dq_start, *own_start_refs), rest = rest[:6], rest[6:]
        other_refs, rest = rest[:5], rest[5:]
        (dq_sum, *own_sums, kv_other, other_key_sum, other_value_sum), rest = rest[:6], rest[6:]
        own = own_start_refs[:3] + own_sums
        other = other_refs[:3] + (other_key_sum, other_value_sum)
    else:
        (dq_start, *own_start_refs), rest = rest[:6], rest[6:]
        dq_outs, rest = rest[:count_ka - 1], rest[count_ka - 1:]
        (*own_sums, dq_sum), rest = rest[:3], rest[3:]
        own = own_start_refs[:3] + own_sums
    lse_delta, weights_low, dscores_low = rest
    _, place_ka = places()
    rows8 = head_rows(heads_dev)
    spare = extra_rows(heads_dev)
    score_scale = HEAD_DIM ** -0.5

    if stage < 2:
        kv_at = pl.ds(pl.multiple_of(place_ka // share * HEAD_DIM, HEAD_DIM), HEAD_DIM)
        key_gain = key_gain_ref[:, kv_at]
        value_gain = value_gain_ref[:, kv_at]
        keys, values, keys_t, key_sum, value_sum = other if stage else own
        for number in range(count_chip):
            for step in range(count_ka):
                part = pl.ds(step * TILE, TILE)
                local = number * count_ka + step
                key_tile = (blocks[number][part, :HEAD_DIM].astype(F32) * key_gain).astype(BF16)
                value_tile = (blocks[number][part, HEAD_DIM:].astype(F32) * value_gain).astype(BF16)
                keys[local] = key_tile
                values[local] = value_tile
                keys_t[local] = key_tile.T
        key_sum[...] = jnp.zeros_like(key_sum)
        value_sum[...] = jnp.zeros_like(value_sum)
    else:
        for target, source in zip(own_sums, own_start_refs[3:]):
            target[...] = source[...]
    if stage == 0:
        dq_sum[...] = jnp.zeros_like(dq_sum)
    else:
        dq_sum[...] = dq_start[...]
    if stage == 2:
        other_key_sum[...] = other_refs[3][...]
        other_value_sum[...] = other_refs[4][...]

    for slot in range(count_ka):
        packed = stats_ref[pl.ds(slot * spare, spare), :].astype(F32)
        terms = [packed[term * rows8:(term + 1) * rows8] for term in range(STAT_TERMS)]
        total = sum(terms[1:], terms[0])
        lse_delta[slot, :, :TILE] = total[:, :TILE] * LOG2E
        lse_delta[slot, :, TILE:] = total[:, TILE:]

    reach = (lax.broadcasted_iota(jnp.int32, (TILE, TILE), 1)
             - lax.broadcasted_iota(jnp.int32, (TILE, TILE), 0))
    reach = jnp.concatenate([jnp.concatenate([reach, reach], axis=1)] * 2, axis=0)
    lower = lax.broadcasted_iota(jnp.int32, (2 * TILE, 2 * TILE), 0) < TILE

    def run(start, refs, first, last):
        keys, values, keys_t, key_sum, value_sum = refs

        def heads_of(kind, tile_at, heads):
            rows = pl.ds(pl.multiple_of(tile_at * TILE, TILE), TILE)
            return jnp.concatenate(
                [heads_ref[kind, rows, pl.ds(head * HEAD_DIM, HEAD_DIM)] for head in heads], axis=0
            )

        def pair_step(at, carry):
            base = ENTRY * (start + 2 * at)
            turn_q, tile_at, one = table[base], table[base + 1], table[base + 2]
            two = table[base + ENTRY + 2]
            slot = lax.rem(place_ka - tile_at + count_ka, count_ka)
            allowed = reach >= jnp.where(lower, table[base + 3], table[base + ENTRY + 3])
            key_pair = jnp.concatenate([keys[one], keys[two]], axis=0)
            value_pair = jnp.concatenate([values[one], values[two]], axis=0)
            key_turn = jnp.concatenate([keys_t[one], keys_t[two]], axis=1)
            for head in range(0, heads_dev, 2):
                part = pl.ds(head * HEAD_DIM, 2 * HEAD_DIM)
                both = (head, head + 1)
                scores = lax.dot_general(
                    key_pair, heads_of(0, tile_at, both), LAST_DIMS, preferred_element_type=F32
                )
                dweights = lax.dot_general(
                    value_pair, heads_of(1, tile_at, both), LAST_DIMS, preferred_element_type=F32
                )
                lse_row, delta_row = [
                    jnp.concatenate([lse_delta[slot, number:number + 1, lanes] for number in both], axis=1)
                    for lanes in (slice(0, TILE), slice(TILE, 2 * TILE))
                ]
                weights = jnp.exp2(scores * (score_scale * LOG2E) - lse_row)
                weights = jnp.where(allowed, weights, 0.0)
                weights_low[:, part] = weights.astype(BF16)
                dscores_low[:, part] = (weights * (dweights - delta_row)).astype(BF16)
            every = range(heads_dev)
            value_term = jnp.dot(weights_low[...], heads_of(1, tile_at, every), preferred_element_type=F32)
            key_term = jnp.dot(dscores_low[...], heads_of(0, tile_at, every), preferred_element_type=F32)
            dq_sum[turn_q] += jnp.dot(key_turn, dscores_low[...], preferred_element_type=F32)
            value_sum[one] += value_term[:TILE]
            key_sum[one] += key_term[:TILE]
            value_sum[two] += value_term[TILE:]
            key_sum[two] += key_term[TILE:]
            return carry

        lax.fori_loop(first, last, pair_step, 0)

    own_at = own_start(count_chip * count_ka, count_ka)
    if stage == 0:
        run(own_at, own, 0, table[0])
    elif stage == 1:
        run(2, other, 0, table[ENTRY])
        for number, dq_half in enumerate(dq_halves):
            part = pl.ds(number * dq_half.shape[1], dq_half.shape[1])
            dq_half[...] = (dq_sum[0, :, part] * score_scale).astype(BF16)
    elif stage == 2:
        run(2, other, table[ENTRY], table[ENTRY + 1])
        run(own_at, own, table[0], table[1])
        for local in range(count_chip * count_ka):
            part = pl.ds(local * TILE, TILE)
            kv_other[part, :HEAD_DIM] = (other_key_sum[local] * score_scale).astype(BF16)
            kv_other[part, HEAD_DIM:] = other_value_sum[local].astype(BF16)
    else:
        run(own_at, own, table[1], table[2])
        for number, dq_out in enumerate(dq_outs, 1):
            dq_out[...] = (dq_sum[number] * score_scale).astype(BF16)


def merge_kernel(dims, key_sum, value_sum, kv_back, *rest):
    count_chip, count_ka = dims
    blocks, kv_outs = rest[:count_chip], rest[count_chip:]
    key_gains = jnp.zeros((8, HEAD_DIM), F32)
    value_gains = jnp.zeros((8, HEAD_DIM), F32)
    for number in range(count_chip):
        for step in range(count_ka):
            local = number * count_ka + step
            there = pl.ds(local * TILE, TILE)
            key_total = key_sum[local] * HEAD_DIM ** -0.5 + kv_back[there, :HEAD_DIM].astype(F32)
            value_total = value_sum[local] + kv_back[there, HEAD_DIM:].astype(F32)
            out_ref = kv_outs[number]
            part = pl.ds(step * TILE, TILE)
            out_ref[part, :HEAD_DIM] = key_total.astype(out_ref.dtype)
            out_ref[part, HEAD_DIM:] = value_total.astype(out_ref.dtype)
            key_raw = blocks[number][part, :HEAD_DIM].astype(F32)
            value_raw = blocks[number][part, HEAD_DIM:].astype(F32)
            key_gains += jnp.sum((key_total * key_raw).reshape(TILE // 8, 8, HEAD_DIM), axis=0)
            value_gains += jnp.sum((value_total * value_raw).reshape(TILE // 8, 8, HEAD_DIM), axis=0)
    gains = jnp.concatenate([jnp.sum(key_gains, axis=0, keepdims=True),
                             jnp.sum(value_gains, axis=0, keepdims=True)], axis=1)
    packed = pack_gains(gains)
    for out_ref in kv_outs:
        out_ref[count_ka * TILE:, :] = packed.astype(out_ref.dtype)


def pack_gains(gains):
    rows = lax.broadcasted_iota(jnp.int32, (SPARE, gains.shape[1]), 0)
    high, middle, low = split_float(gains, 3)
    packed = jnp.where(rows == 0, high, jnp.where(rows == 1, middle, low))
    return jnp.where(rows < 3, packed, 0.0)


def add_parts(parts, rows):
    total = parts[0][rows, :]
    for part in parts[1:]:
        total = total + part[rows, :].astype(F32)
    return total


def own_gain(key_gain_ref, value_gain_ref, share):
    kv_at = pl.ds(pl.multiple_of(places()[1] // share * HEAD_DIM, HEAD_DIM), HEAD_DIM)
    return jnp.concatenate([key_gain_ref[:, kv_at], value_gain_ref[:, kv_at]], axis=1)


def collect_kernel(dims, key_gain_ref, value_gain_ref, *rest):
    count_chip, count_ka, share = dims
    parts, outs = rest[:count_chip], rest[count_chip:]
    gain = own_gain(key_gain_ref, value_gain_ref, share)
    total = add_parts(parts, pl.ds(count_ka * TILE, SPARE))
    packed = pack_gains(jnp.sum(total, axis=0, keepdims=True))
    for step, out_ref in enumerate(outs):
        total = add_parts(parts, pl.ds(step * TILE, TILE))
        if share == 1:
            total = total * gain
        out_ref[:TILE, :] = total.astype(out_ref.dtype)
        out_ref[TILE:, :] = packed.astype(out_ref.dtype)


def place_kernel(dims, *rest):
    count_ka, heads_dev, where = dims
    pieces, (dq_out, turned, sems) = rest[:len(where)], rest[len(where):]
    copies = []
    for number, ((step, first), piece) in enumerate(zip(where, pieces)):
        source = lax.rem(places()[1] - step + count_ka, count_ka)
        columns = pl.ds(pl.multiple_of((source * heads_dev + first) * HEAD_DIM, HEAD_DIM), piece.shape[1])
        here = pl.ds(first * HEAD_DIM, piece.shape[1])
        for head in range(piece.shape[1] // HEAD_DIM):
            part = pl.ds(head * HEAD_DIM, HEAD_DIM)
            turned[step, :, pl.ds((first + head) * HEAD_DIM, HEAD_DIM)] = piece[:, part].T
        copies.append(pltpu.make_async_copy(turned.at[step, :, here], dq_out.at[:, columns], sems.at[number]))
        copies[-1].start()
    for copy in copies:
        copy.wait()


def gains_kernel(gains_ref, other_ref, key_gain_out, value_gain_out):
    key_gain_out[...] = gains_ref[0:1, :] + other_ref[0:1, :]
    value_gain_out[...] = gains_ref[1:2, :] + other_ref[1:2, :]


def finish_kernel(dims, key_gain_ref, value_gain_ref, *rest):
    count_ka, share = dims
    pieces, rest = rest[:count_ka], rest[count_ka:]
    dk_out, dv_out, gains_out, sums = rest
    _, place_ka = places()
    sums[...] = jnp.zeros_like(sums)
    for step in range(count_ka):
        source = lax.rem(place_ka + step, count_ka)
        sums[source // share] += pieces[step][...].astype(F32)
    for head in range(count_ka // share):
        part = pl.ds(head * HEAD_DIM, HEAD_DIM)
        key_total = sums[head, :TILE, :HEAD_DIM]
        value_total = sums[head, :TILE, HEAD_DIM:]
        if share > 1:
            key_total = key_total * key_gain_ref[:, part]
            value_total = value_total * value_gain_ref[:, part]
        dk_out[:, part] = key_total.astype(BF16)
        dv_out[:, part] = value_total.astype(BF16)
        gains = jnp.sum(sums[head, TILE:, :], axis=0, keepdims=True)
        gains_out[0:1, part] = gains[:, :HEAD_DIM]
        gains_out[1:2, part] = gains[:, HEAD_DIM:]


def in_vmem(count):
    return [pl.BlockSpec(memory_space=VMEM)] * count


def in_smem(count):
    return [pl.BlockSpec(memory_space=SMEM)] * count


def anywhere(count):
    return [pl.BlockSpec(memory_space=pl.ANY)] * count


def params(mib):
    return pltpu.CompilerParams(vmem_limit_bytes=mib * 1024 * 1024)


def shards(
    queries,
    key_rows,
    values,
    attn_out,
    grad_out,
    log_sums,
    key_gain,
    value_gain,
    doc_ids,
    tile_mask,
    block_order,
):
    count_pb = lax.axis_size("pb")
    count_ka = lax.axis_size("ka")
    rows_dev = key_rows.shape[0]
    query_rows = queries.shape[0]
    heads = log_sums.shape[0]
    feat_width = queries.shape[1]
    kv_heads = key_rows.shape[1] // HEAD_DIM
    heads_dev = heads // count_ka
    share = count_ka // kv_heads
    assert rows_dev == TILE and share * kv_heads == count_ka and count_pb & (count_pb - 1) == 0
    width = heads_dev * HEAD_DIM
    key_gain = key_gain.reshape(1, -1)
    value_gain = value_gain.reshape(1, -1)

    spare = extra_rows(heads_dev)
    count_chip = count_pb // 2

    def swap(array, number):
        return lax.ppermute(array, "pb", [(at, at ^ number) for at in range(count_pb)])

    def turn(array, step):
        return lax.ppermute(array, "ka", [(at, (at + step) % count_ka) for at in range(count_ka)])

    sends = pl.pallas_call(
        functools.partial(prepare_kernel, (count_ka, heads, heads_dev, share)),
        in_specs=anywhere(5),
        out_specs=in_vmem(count_ka),
        out_shape=[jax.ShapeDtypeStruct((TILE + spare, 2 * HEAD_DIM), BF16)] * count_ka,
        scratch_shapes=[VMEM((PARTS, TILE, feat_width // PARTS), BF16)] * 2
        + [VMEM((2, *key_rows.shape), BF16)]
        + [VMEM((heads + 8, TILE), F32)] * 2
        + [pltpu.SemaphoreType.DMA((3, PARTS))],
        compiler_params=params(57),
        name="prepare",
    )(key_rows, values, attn_out, grad_out, log_sums)
    messages = [sends[0]] + [turn(sends[step], step) for step in range(1, count_ka)]

    later_queries, _ = lax.optimization_barrier((queries, sends[0]))
    own_queries = pl.pallas_call(
        own_heads_kernel,
        in_specs=anywhere(2),
        out_specs=in_vmem(1)[0],
        out_shape=jax.ShapeDtypeStruct((2, query_rows, width), BF16),
        scratch_shapes=[pltpu.SemaphoreType.DMA((2,))],
        compiler_params=params(48),
        cost_estimate=pl.CostEstimate(flops=0, bytes_accessed=8 * query_rows * width, transcendentals=0),
        name="own_heads",
    )(later_queries, grad_out)
    messages, own_queries = lax.optimization_barrier((messages, own_queries))
    own_block = jnp.concatenate([message[:TILE] for message in messages], axis=0)
    blocks = [own_block] + [swap(own_block, 2 * number) for number in range(1, count_chip)]
    other_blocks = [swap(block, 1) for block in blocks]
    own_stats = jnp.concatenate([message[TILE:] for message in messages], axis=0)
    later_order, _ = lax.optimization_barrier((block_order, own_block))

    key_tiles = count_chip * count_ka
    sum_shape = jax.ShapeDtypeStruct((key_tiles, TILE, HEAD_DIM), F32)
    key_shape = jax.ShapeDtypeStruct((key_tiles, TILE, HEAD_DIM), BF16)
    kv_shape = (query_rows + SPARE, 2 * HEAD_DIM)
    half = count_ka // 2
    late = tuple(step for step in range(count_ka) if step != half)
    order = (half,) + late
    entries = own_start(key_tiles, count_ka) + 1 + count_ka * key_tiles
    table = pl.pallas_call(
        functools.partial(plan_kernel, (count_chip, count_ka, order)),
        in_specs=in_smem(3),
        out_specs=in_smem(1)[0],
        out_shape=jax.ShapeDtypeStruct((ENTRY * entries,), jnp.int32),
        scratch_shapes=[SMEM((3 * count_ka,), jnp.int32)],
        cost_estimate=pl.CostEstimate(flops=0, bytes_accessed=1 << 22, transcendentals=0),
        name="plan",
    )(later_order, doc_ids, tile_mask)

    def attend(stage, outs, scratch, *operands):
        return pl.pallas_call(
            functools.partial(attention_kernel, (count_chip, count_ka, heads_dev, share, stage)),
            in_specs=in_smem(1) + in_vmem(len(operands)),
            out_specs=in_vmem(len(outs)),
            out_shape=outs,
            scratch_shapes=scratch + [
                VMEM((count_ka, head_rows(heads_dev), 2 * TILE), F32),
                VMEM((2 * TILE, width), BF16),
                VMEM((2 * TILE, width), BF16),
            ],
            compiler_params=params(14 + key_tiles * 11 // 16),
            cost_estimate=pl.CostEstimate(
                flops=5 * count_ka * key_tiles * TILE * TILE * width, bytes_accessed=1 << 20, transcendentals=0
            ),
            name=("attention_first", "attention_leaving", "attention_other", "attention_own")[stage],
        )(table, *operands)

    dq_sums = jax.ShapeDtypeStruct((count_ka, HEAD_DIM, width), F32)
    dq_tile = jax.ShapeDtypeStruct((HEAD_DIM, width), BF16)
    state = [key_shape] * 3 + [sum_shape] * 2
    dq_sum, *own = attend(0, [dq_sums] + state, [], key_gain, value_gain, own_queries, own_stats, *blocks)
    dq_sum, *other = attend(
        1, [dq_sums] + [jax.ShapeDtypeStruct((HEAD_DIM, width // 2), BF16)] * 2 + state, [],
        key_gain, value_gain, own_queries, own_stats, *other_blocks, dq_sum,
    )
    dq_parts = [None] * count_ka
    dq_halves, other = [turn(part, half) for part in other[:2]], other[2:]
    dq_sum, *own[3:], kv_other = attend(
        2,
        [dq_sums] + [sum_shape] * 2
        + [jax.ShapeDtypeStruct((key_tiles * TILE, 2 * HEAD_DIM), BF16)],
        [VMEM(sum_shape.shape, F32)] * 2,
        own_queries, own_stats, dq_sum, *own, *other,
    )
    kv_other, dq_halves[0] = lax.optimization_barrier((kv_other, dq_halves[0]))
    kv_back = swap(kv_other, 1)
    *dq_late, key_sum, value_sum = attend(
        3, [dq_tile] * len(late) + [sum_shape] * 2, [VMEM(dq_sums.shape, F32)],
        own_queries, own_stats, dq_sum, *own,
    )
    kv_own = pl.pallas_call(
        functools.partial(merge_kernel, (count_chip, count_ka)),
        in_specs=in_vmem(3 + count_chip),
        out_specs=in_vmem(count_chip),
        out_shape=[jax.ShapeDtypeStruct(kv_shape, BF16 if number else F32) for number in range(count_chip)],
        compiler_params=params(16 + key_tiles // 4),
        name="merge",
    )(key_sum, value_sum, kv_back, *blocks)
    kv_parts = [kv_own[0]] + [swap(kv_own[number], 2 * number) for number in range(1, count_chip)]
    dq_late, dq_halves[1] = lax.optimization_barrier((dq_late, dq_halves[1]))
    for step, tile in zip(late, dq_late):
        dq_parts[step] = turn(tile, step) if step else tile

    piece_type = BF16 if share == 1 else F32
    piece_shape = (TILE + SPARE, 2 * HEAD_DIM)
    pieces = list(pl.pallas_call(
        functools.partial(collect_kernel, (count_chip, count_ka, share)),
        in_specs=in_vmem(2 + count_chip),
        out_specs=in_vmem(count_ka),
        out_shape=[jax.ShapeDtypeStruct(piece_shape, piece_type if step else F32) for step in range(count_ka)],
        compiler_params=params(24),
        name="collect",
    )(key_gain, value_gain, *kv_parts))
    pieces = [pieces[0]] + [turn(piece, -step) for step, piece in enumerate(pieces[1:], 1)]
    where = ((half, 0), (half, heads_dev // 2)) + tuple((step, 0) for step in order[1:])
    grad_queries = pl.pallas_call(
        functools.partial(place_kernel, (count_ka, heads_dev, where)),
        in_specs=in_vmem(len(where)),
        out_specs=anywhere(1)[0],
        out_shape=jax.ShapeDtypeStruct((rows_dev, feat_width), BF16),
        scratch_shapes=[VMEM((count_ka, TILE, width), BF16), pltpu.SemaphoreType.DMA((len(where),))],
        compiler_params=params(16),
        cost_estimate=pl.CostEstimate(flops=0, bytes_accessed=4 * rows_dev * feat_width, transcendentals=0),
        name="place_queries",
    )(*dq_halves, *[dq_parts[step] for step in order[1:]])
    pieces, grad_queries = lax.optimization_barrier((pieces, grad_queries))
    grad_keys, grad_values, gains = pl.pallas_call(
        functools.partial(finish_kernel, (count_ka, share)),
        in_specs=in_vmem(2 + count_ka),
        out_specs=in_vmem(3),
        out_shape=[
            jax.ShapeDtypeStruct(key_rows.shape, BF16),
            jax.ShapeDtypeStruct(key_rows.shape, BF16),
            jax.ShapeDtypeStruct((2, key_rows.shape[1]), F32),
        ],
        scratch_shapes=[VMEM((kv_heads, TILE + SPARE, 2 * HEAD_DIM), F32)],
        compiler_params=params(16),
        name="finish",
    )(key_gain, value_gain, *pieces)
    grad_key_gain, grad_value_gain = pl.pallas_call(
        gains_kernel,
        in_specs=in_vmem(2),
        out_specs=in_vmem(2),
        out_shape=[jax.ShapeDtypeStruct(key_gain.shape, F32)] * 2,
        compiler_params=params(4),
        name="add_gains",
    )(gains, swap(gains, 1))
    return grad_queries, grad_keys, grad_values, grad_key_gain.reshape(-1), grad_value_gain.reshape(-1)


def solution(mesh):
    placed = (
        P("pb", None),
        P(("pb", "ka"), None),
        P(("pb", "ka"), None),
        P(("pb", "ka"), None),
        P("pb", None),
        P(None, ("pb", "ka")),
        P(),
        P(),
        P(),
        P(),
        P(),
    )
    return jax.shard_map(
        shards,
        mesh=mesh,
        in_specs=placed,
        out_specs=(P(("pb", "ka"), None), P(("pb", "ka"), None), P(("pb", "ka"), None), P(), P()),
        check_vma=False,
    )
```

```python
import functools

import jax
import jax.numpy as jnp
from jax import lax
from jax.experimental import pallas as pl
from jax.experimental.pallas import tpu as pltpu
from jax.sharding import PartitionSpec as P

HEAD_DIM = 128
TILE = 128
SPARE = 16
LOG2E = 1.4426950408889634
ENTRY = 4
PARTS = 4
STAT_TERMS = 2
LAST_DIMS = (((1,), (1,)), ((), ()))
VMEM = pltpu.VMEM
SMEM = pltpu.SMEM
F32 = jnp.float32
BF16 = jnp.bfloat16


def split_float(x, count):
    terms = []
    for _ in range(count):
        terms.append(x.astype(BF16).astype(F32))
        x = x - terms[-1]
    return terms


def head_rows(heads_dev):
    return -(-heads_dev // 8) * 8


def extra_rows(heads_dev):
    return STAT_TERMS * head_rows(heads_dev)


def prepare_kernel(dims, key_ref, value_ref, attn_ref, grads_ref, lse_ref, *rest):
    count_ka, heads, heads_dev, share = dims
    outs, (attn, grad, kv, lse_pad, delta_pad, sems) = rest[:count_ka], rest[count_ka:]
    _, place_ka = places()
    rows8 = head_rows(heads_dev)
    part_heads = heads // PARTS
    rows = pl.ds(pl.multiple_of(place_ka * TILE, TILE), TILE)
    copies = []
    for part in range(PARTS):
        columns = pl.ds(part * part_heads * HEAD_DIM, part_heads * HEAD_DIM)
        copies.append((
            pltpu.make_async_copy(attn_ref.at[:, columns], attn.at[part], sems.at[0, part]),
            pltpu.make_async_copy(grads_ref.at[rows, columns], grad.at[part], sems.at[1, part]),
        ))
    copies.append((
        pltpu.make_async_copy(key_ref, kv.at[0], sems.at[2, 0]),
        pltpu.make_async_copy(value_ref, kv.at[1], sems.at[2, 1]),
        pltpu.make_async_copy(lse_ref, lse_pad.at[pl.ds(0, heads), :], sems.at[2, 2]),
    ))
    for pair in copies:
        for copy in pair:
            copy.start()
    lanes = lax.broadcasted_iota(jnp.int32, (TILE, TILE), 1)
    columns = jnp.zeros((TILE, TILE), F32)
    for part in range(PARTS):
        for copy in copies[part]:
            copy.wait()
        for head in range(part_heads):
            at = pl.ds(head * HEAD_DIM, HEAD_DIM)
            products = grad[part, :, at].astype(F32) * attn[part, :, at].astype(F32)
            total = jnp.sum(products, axis=1, keepdims=True)
            columns = jnp.where(lanes == part * part_heads + head, total, columns)
    delta_pad[...] = jnp.zeros_like(delta_pad)
    lse_pad[pl.ds(heads, 8), :] = jnp.zeros((8, TILE), F32)
    delta_pad[:heads, :] = columns.T[:heads, :]
    for copy in copies[-1]:
        copy.wait()
    for step in range(count_ka):
        target = lax.rem(place_ka + step, count_ka)
        kv_at = pl.ds(pl.multiple_of(target // share * HEAD_DIM, HEAD_DIM), HEAD_DIM)
        outs[step][:TILE, :HEAD_DIM] = kv[0, :, kv_at]
        outs[step][:TILE, HEAD_DIM:] = kv[1, :, kv_at]
        head_at = pl.ds(target * heads_dev, rows8)
        both = jnp.concatenate([lse_pad[head_at, :], delta_pad[head_at, :]], axis=1)
        outs[step][TILE:, :] = jnp.concatenate(split_float(both, STAT_TERMS), axis=0).astype(BF16)


def own_heads_kernel(queries_ref, grads_ref, out_ref, sems):
    _, place_ka = places()
    width = out_ref.shape[2]
    columns = pl.ds(pl.multiple_of(place_ka * width, HEAD_DIM), width)
    copies = [
        pltpu.make_async_copy(ref.at[:, columns], out_ref.at[number], sems.at[number])
        for number, ref in enumerate((queries_ref, grads_ref))
    ]
    for copy in copies:
        copy.start()
    for copy in copies:
        copy.wait()


def places():
    return lax.axis_index("pb"), lax.axis_index("ka")


def own_start(key_tiles, count_ka):
    return 3 + count_ka * key_tiles


def plan_kernel(dims, order_ref, doc_ref, mask_ref, table, counts):
    count_chip, count_ka, order = dims
    place_pb, place_ka = places()
    own_at = own_start(count_chip * count_ka, count_ka)

    def walk(start, query_pb, key_pb, steps, units, count_at=None):
        def query_step(turn_q, units):
            before = units
            step_q = jnp.int32(order[0])
            for number, step in enumerate(order):
                step_q = jnp.where(turn_q == number, step, step_q)
            tile_at = lax.rem(place_ka + step_q, count_ka)
            seq_q = order_ref[query_pb * count_ka + tile_at]
            doc_q = doc_ref[seq_q]

            def collect(number, units):
                for step in range(count_ka):
                    stored = (key_pb ^ (2 * number)) * count_ka + lax.rem(
                        place_ka - step + count_ka, count_ka
                    )
                    seq_k = order_ref[stored]
                    live = (mask_ref[seq_q, seq_k] == 1) & (doc_ref[seq_k] == doc_q) & (seq_q >= seq_k)
                    if start is not None:
                        base = ENTRY * (start + units)
                        table[base] = turn_q
                        table[base + 1] = tile_at
                        table[base + 2] = number * count_ka + step
                        table[base + 3] = jnp.where(seq_q == seq_k, 0, -TILE)
                    units = units + live.astype(jnp.int32)
                return units

            units = lax.fori_loop(0, count_chip, collect, units)
            if start is not None:
                base = ENTRY * (start + units)
                table[base] = turn_q
                table[base + 1] = tile_at
                table[base + 2] = 0
                table[base + 3] = TILE
            units = 2 * ((units + 1) // 2)
            if count_at is not None:
                counts[count_at + tile_at] = units - before
            return units

        return lax.fori_loop(*steps, query_step, units)

    def steps_of(units):
        return units // 2

    none = jnp.int32(0)
    sibling = place_pb ^ 1
    every = (0, count_ka)
    other = steps_of(walk(2, place_pb, sibling, every, none, 2 * count_ka))
    own = steps_of(walk(own_at, place_pb, place_pb, every, none, 0))
    walk(None, sibling, sibling, every, none, count_ka)
    sibling_other = steps_of(walk(None, sibling, place_pb, every, none))

    def first_steps(place):
        tile = lax.rem(place + order[0], count_ka)
        return steps_of(counts[tile]), steps_of(counts[2 * count_ka + tile])

    first, second = none, none
    for place in range(count_ka):
        first = jnp.maximum(first, sum(first_steps(place)))
        for core, others in enumerate((other, sibling_other)):
            units = sum([counts[core * count_ka + (place + step) % count_ka] for step in order[:1]])
            second = jnp.maximum(second, others + steps_of(units))
    own_first, other_first = first_steps(place_ka)
    table[0] = own_first
    table[1] = jnp.minimum(second - other, own)
    table[2] = own
    table[ENTRY] = jnp.clip(first - own_first, other_first, other)
    table[ENTRY + 1] = other


def attention_kernel(dims, *rest):
    count_chip, count_ka, heads_dev, share, stage = dims
    table, rest = rest[0], rest[1:]
    if stage < 2:
        (key_gain_ref, value_gain_ref), rest = rest[:2], rest[2:]
    (heads_ref, stats_ref), rest = rest[:2], rest[2:]
    if stage < 2:
        blocks, rest = rest[:count_chip], rest[count_chip:]
    if stage == 0:
        (dq_sum, *own), rest = rest[:6], rest[6:]
    elif stage == 1:
        (dq_start, dq_sum, *dq_halves), other, rest = rest[:4], rest[4:9], rest[9:]
    elif stage == 2:
        (dq_start, *own_start_refs), rest = rest[:6], rest[6:]
        other_refs, rest = rest[:5], rest[5:]
        (dq_sum, *own_sums, kv_other, other_key_sum, other_value_sum), rest = rest[:6], rest[6:]
        own = own_start_refs[:3] + own_sums
        other = other_refs[:3] + (other_key_sum, other_value_sum)
    else:
        (dq_start, *own_start_refs), rest = rest[:6], rest[6:]
        dq_outs, rest = rest[:count_ka - 1], rest[count_ka - 1:]
        (*own_sums, dq_sum), rest = rest[:3], rest[3:]
        own = own_start_refs[:3] + own_sums
    lse_delta, weights_low, dscores_low = rest
    _, place_ka = places()
    rows8 = head_rows(heads_dev)
    spare = extra_rows(heads_dev)
    score_scale = HEAD_DIM ** -0.5

    if stage < 2:
        kv_at = pl.ds(pl.multiple_of(place_ka // share * HEAD_DIM, HEAD_DIM), HEAD_DIM)
        key_gain = key_gain_ref[:, kv_at]
        value_gain = value_gain_ref[:, kv_at]
        keys, values, keys_t, key_sum, value_sum = other if stage else own
        for number in range(count_chip):
            for step in range(count_ka):
                part = pl.ds(step * TILE, TILE)
                local = number * count_ka + step
                key_tile = (blocks[number][part, :HEAD_DIM].astype(F32) * key_gain).astype(BF16)
                value_tile = (blocks[number][part, HEAD_DIM:].astype(F32) * value_gain).astype(BF16)
                keys[local] = key_tile
                values[local] = value_tile
                keys_t[local] = key_tile.T
        key_sum[...] = jnp.zeros_like(key_sum)
        value_sum[...] = jnp.zeros_like(value_sum)
    else:
        for target, source in zip(own_sums, own_start_refs[3:]):
            target[...] = source[...]
    if stage == 0:
        dq_sum[...] = jnp.zeros_like(dq_sum)
    else:
        dq_sum[...] = dq_start[...]
    if stage == 2:
        other_key_sum[...] = other_refs[3][...]
        other_value_sum[...] = other_refs[4][...]

    for slot in range(count_ka):
        packed = stats_ref[pl.ds(slot * spare, spare), :].astype(F32)
        terms = [packed[term * rows8:(term + 1) * rows8] for term in range(STAT_TERMS)]
        total = sum(terms[1:], terms[0])
        lse_delta[slot, :, :TILE] = total[:, :TILE] * LOG2E
        lse_delta[slot, :, TILE:] = total[:, TILE:]

    reach = (lax.broadcasted_iota(jnp.int32, (TILE, TILE), 1)
             - lax.broadcasted_iota(jnp.int32, (TILE, TILE), 0))
    reach = jnp.concatenate([jnp.concatenate([reach, reach], axis=1)] * 2, axis=0)
    lower = lax.broadcasted_iota(jnp.int32, (2 * TILE, 2 * TILE), 0) < TILE

    def run(start, refs, first, last):
        keys, values, keys_t, key_sum, value_sum = refs

        def heads_of(kind, tile_at, heads):
            rows = pl.ds(pl.multiple_of(tile_at * TILE, TILE), TILE)
            return jnp.concatenate(
                [heads_ref[kind, rows, pl.ds(head * HEAD_DIM, HEAD_DIM)] for head in heads], axis=0
            )

        def pair_step(at, carry):
            base = ENTRY * (start + 2 * at)
            turn_q, tile_at, one = table[base], table[base + 1], table[base + 2]
            two = table[base + ENTRY + 2]
            slot = lax.rem(place_ka - tile_at + count_ka, count_ka)
            allowed = reach >= jnp.where(lower, table[base + 3], table[base + ENTRY + 3])
            key_pair = jnp.concatenate([keys[one], keys[two]], axis=0)
            value_pair = jnp.concatenate([values[one], values[two]], axis=0)
            key_turn = jnp.concatenate([keys_t[one], keys_t[two]], axis=1)
            for head in range(0, heads_dev, 2):
                part = pl.ds(head * HEAD_DIM, 2 * HEAD_DIM)
                both = (head, head + 1)
                scores = lax.dot_general(
                    key_pair, heads_of(0, tile_at, both), LAST_DIMS, preferred_element_type=F32
                )
                dweights = lax.dot_general(
                    value_pair, heads_of(1, tile_at, both), LAST_DIMS, preferred_element_type=F32
                )
                lse_row, delta_row = [
                    jnp.concatenate([lse_delta[slot, number:number + 1, lanes] for number in both], axis=1)
                    for lanes in (slice(0, TILE), slice(TILE, 2 * TILE))
                ]
                weights = jnp.exp2(scores * (score_scale * LOG2E) - lse_row)
                weights = jnp.where(allowed, weights, 0.0)
                weights_low[:, part] = weights.astype(BF16)
                dscores_low[:, part] = (weights * (dweights - delta_row)).astype(BF16)
            every = range(heads_dev)
            value_term = jnp.dot(weights_low[...], heads_of(1, tile_at, every), preferred_element_type=F32)
            key_term = jnp.dot(dscores_low[...], heads_of(0, tile_at, every), preferred_element_type=F32)
            dq_sum[turn_q] += jnp.dot(key_turn, dscores_low[...], preferred_element_type=F32)
            value_sum[one] += value_term[:TILE]
            key_sum[one] += key_term[:TILE]
            value_sum[two] += value_term[TILE:]
            key_sum[two] += key_term[TILE:]
            return carry

        lax.fori_loop(first, last, pair_step, 0)

    own_at = own_start(count_chip * count_ka, count_ka)
    if stage == 0:
        run(own_at, own, 0, table[0])
    elif stage == 1:
        run(2, other, 0, table[ENTRY])
        for number, dq_half in enumerate(dq_halves):
            part = pl.ds(number * dq_half.shape[1], dq_half.shape[1])
            dq_half[...] = (dq_sum[0, :, part] * score_scale).astype(BF16)
    elif stage == 2:
        run(2, other, table[ENTRY], table[ENTRY + 1])
        run(own_at, own, table[0], table[1])
        for local in range(count_chip * count_ka):
            part = pl.ds(local * TILE, TILE)
            kv_other[part, :HEAD_DIM] = (other_key_sum[local] * score_scale).astype(BF16)
            kv_other[part, HEAD_DIM:] = other_value_sum[local].astype(BF16)
    else:
        run(own_at, own, table[1], table[2])
        for number, dq_out in enumerate(dq_outs, 1):
            dq_out[...] = (dq_sum[number] * score_scale).astype(BF16)


def merge_kernel(dims, key_sum, value_sum, kv_back, *rest):
    count_chip, count_ka = dims
    blocks, kv_outs = rest[:count_chip], rest[count_chip:]
    key_gains = jnp.zeros((8, HEAD_DIM), F32)
    value_gains = jnp.zeros((8, HEAD_DIM), F32)
    for number in range(count_chip):
        for step in range(count_ka):
            local = number * count_ka + step
            there = pl.ds(local * TILE, TILE)
            key_total = key_sum[local] * HEAD_DIM ** -0.5 + kv_back[there, :HEAD_DIM].astype(F32)
            value_total = value_sum[local] + kv_back[there, HEAD_DIM:].astype(F32)
            out_ref = kv_outs[number]
            part = pl.ds(step * TILE, TILE)
            out_ref[part, :HEAD_DIM] = key_total.astype(out_ref.dtype)
            out_ref[part, HEAD_DIM:] = value_total.astype(out_ref.dtype)
            key_raw = blocks[number][part, :HEAD_DIM].astype(F32)
            value_raw = blocks[number][part, HEAD_DIM:].astype(F32)
            key_gains += jnp.sum((key_total * key_raw).reshape(TILE // 8, 8, HEAD_DIM), axis=0)
            value_gains += jnp.sum((value_total * value_raw).reshape(TILE // 8, 8, HEAD_DIM), axis=0)
    gains = jnp.concatenate([jnp.sum(key_gains, axis=0, keepdims=True),
                             jnp.sum(value_gains, axis=0, keepdims=True)], axis=1)
    packed = pack_gains(gains)
    for out_ref in kv_outs:
        out_ref[count_ka * TILE:, :] = packed.astype(out_ref.dtype)


def pack_gains(gains):
    rows = lax.broadcasted_iota(jnp.int32, (SPARE, gains.shape[1]), 0)
    high, middle, low = split_float(gains, 3)
    packed = jnp.where(rows == 0, high, jnp.where(rows == 1, middle, low))
    return jnp.where(rows < 3, packed, 0.0)


def add_parts(parts, rows):
    total = parts[0][rows, :]
    for part in parts[1:]:
        total = total + part[rows, :].astype(F32)
    return total


def own_gain(key_gain_ref, value_gain_ref, share):
    kv_at = pl.ds(pl.multiple_of(places()[1] // share * HEAD_DIM, HEAD_DIM), HEAD_DIM)
    return jnp.concatenate([key_gain_ref[:, kv_at], value_gain_ref[:, kv_at]], axis=1)


def collect_kernel(dims, key_gain_ref, value_gain_ref, *rest):
    count_chip, count_ka, share = dims
    parts, outs = rest[:count_chip], rest[count_chip:]
    gain = own_gain(key_gain_ref, value_gain_ref, share)
    total = add_parts(parts, pl.ds(count_ka * TILE, SPARE))
    packed = pack_gains(jnp.sum(total, axis=0, keepdims=True))
    for step, out_ref in enumerate(outs):
        total = add_parts(parts, pl.ds(step * TILE, TILE))
        if share == 1:
            total = total * gain
        out_ref[:TILE, :] = total.astype(out_ref.dtype)
        out_ref[TILE:, :] = packed.astype(out_ref.dtype)


def place_kernel(dims, *rest):
    count_ka, heads_dev, where = dims
    pieces, (dq_out, turned, sems) = rest[:len(where)], rest[len(where):]
    copies = []
    for number, ((step, first), piece) in enumerate(zip(where, pieces)):
        source = lax.rem(places()[1] - step + count_ka, count_ka)
        columns = pl.ds(pl.multiple_of((source * heads_dev + first) * HEAD_DIM, HEAD_DIM), piece.shape[1])
        here = pl.ds(first * HEAD_DIM, piece.shape[1])
        for head in range(piece.shape[1] // HEAD_DIM):
            part = pl.ds(head * HEAD_DIM, HEAD_DIM)
            turned[step, :, pl.ds((first + head) * HEAD_DIM, HEAD_DIM)] = piece[:, part].T
        copies.append(pltpu.make_async_copy(turned.at[step, :, here], dq_out.at[:, columns], sems.at[number]))
        copies[-1].start()
    for copy in copies:
        copy.wait()


def gains_kernel(gains_ref, other_ref, key_gain_out, value_gain_out):
    key_gain_out[...] = gains_ref[0:1, :] + other_ref[0:1, :]
    value_gain_out[...] = gains_ref[1:2, :] + other_ref[1:2, :]


def finish_kernel(dims, key_gain_ref, value_gain_ref, *rest):
    count_ka, share = dims
    pieces, rest = rest[:count_ka], rest[count_ka:]
    dk_out, dv_out, gains_out, sums = rest
    _, place_ka = places()
    sums[...] = jnp.zeros_like(sums)
    for step in range(count_ka):
        source = lax.rem(place_ka + step, count_ka)
        sums[source // share] += pieces[step][...].astype(F32)
    for head in range(count_ka // share):
        part = pl.ds(head * HEAD_DIM, HEAD_DIM)
        key_total = sums[head, :TILE, :HEAD_DIM]
        value_total = sums[head, :TILE, HEAD_DIM:]
        if share > 1:
            key_total = key_total * key_gain_ref[:, part]
            value_total = value_total * value_gain_ref[:, part]
        dk_out[:, part] = key_total.astype(BF16)
        dv_out[:, part] = value_total.astype(BF16)
        gains = jnp.sum(sums[head, TILE:, :], axis=0, keepdims=True)
        gains_out[0:1, part] = gains[:, :HEAD_DIM]
        gains_out[1:2, part] = gains[:, HEAD_DIM:]


def in_vmem(count):
    return [pl.BlockSpec(memory_space=VMEM)] * count


def in_smem(count):
    return [pl.BlockSpec(memory_space=SMEM)] * count


def anywhere(count):
    return [pl.BlockSpec(memory_space=pl.ANY)] * count


def params(mib):
    return pltpu.CompilerParams(vmem_limit_bytes=mib * 1024 * 1024)


def shards(
    queries,
    key_rows,
    values,
    attn_out,
    grad_out,
    log_sums,
    key_gain,
    value_gain,
    doc_ids,
    tile_mask,
    block_order,
):
    count_pb = lax.axis_size("pb")
    count_ka = lax.axis_size("ka")
    rows_dev = key_rows.shape[0]
    query_rows = queries.shape[0]
    heads = log_sums.shape[0]
    feat_width = queries.shape[1]
    kv_heads = key_rows.shape[1] // HEAD_DIM
    heads_dev = heads // count_ka
    share = count_ka // kv_heads
    assert rows_dev == TILE and share * kv_heads == count_ka and count_pb & (count_pb - 1) == 0
    width = heads_dev * HEAD_DIM
    key_gain = key_gain.reshape(1, -1)
    value_gain = value_gain.reshape(1, -1)

    spare = extra_rows(heads_dev)
    count_chip = count_pb // 2

    def swap(array, number):
        return lax.ppermute(array, "pb", [(at, at ^ number) for at in range(count_pb)])

    def turn(array, step):
        return lax.ppermute(array, "ka", [(at, (at + step) % count_ka) for at in range(count_ka)])

    sends = pl.pallas_call(
        functools.partial(prepare_kernel, (count_ka, heads, heads_dev, share)),
        in_specs=anywhere(5),
        out_specs=in_vmem(count_ka),
        out_shape=[jax.ShapeDtypeStruct((TILE + spare, 2 * HEAD_DIM), BF16)] * count_ka,
        scratch_shapes=[VMEM((PARTS, TILE, feat_width // PARTS), BF16)] * 2
        + [VMEM((2, *key_rows.shape), BF16)]
        + [VMEM((heads + 8, TILE), F32)] * 2
        + [pltpu.SemaphoreType.DMA((3, PARTS))],
        compiler_params=params(57),
        name="prepare",
    )(key_rows, values, attn_out, grad_out, log_sums)
    messages = [sends[0]] + [turn(sends[step], step) for step in range(1, count_ka)]

    later_queries, _ = lax.optimization_barrier((queries, sends[0]))
    own_queries = pl.pallas_call(
        own_heads_kernel,
        in_specs=anywhere(2),
        out_specs=in_vmem(1)[0],
        out_shape=jax.ShapeDtypeStruct((2, query_rows, width), BF16),
        scratch_shapes=[pltpu.SemaphoreType.DMA((2,))],
        compiler_params=params(48),
        cost_estimate=pl.CostEstimate(flops=0, bytes_accessed=8 * query_rows * width, transcendentals=0),
        name="own_heads",
    )(later_queries, grad_out)
    messages, own_queries = lax.optimization_barrier((messages, own_queries))
    own_block = jnp.concatenate([message[:TILE] for message in messages], axis=0)
    blocks = [own_block] + [swap(own_block, 2 * number) for number in range(1, count_chip)]
    other_blocks = [swap(block, 1) for block in blocks]
    own_stats = jnp.concatenate([message[TILE:] for message in messages], axis=0)
    later_order, _ = lax.optimization_barrier((block_order, own_block))

    key_tiles = count_chip * count_ka
    sum_shape = jax.ShapeDtypeStruct((key_tiles, TILE, HEAD_DIM), F32)
    key_shape = jax.ShapeDtypeStruct((key_tiles, TILE, HEAD_DIM), BF16)
    kv_shape = (query_rows + SPARE, 2 * HEAD_DIM)
    half = count_ka // 2
    late = tuple(step for step in range(count_ka) if step != half)
    order = (half,) + late
    entries = own_start(key_tiles, count_ka) + 1 + count_ka * key_tiles
    table = pl.pallas_call(
        functools.partial(plan_kernel, (count_chip, count_ka, order)),
        in_specs=in_smem(3),
        out_specs=in_smem(1)[0],
        out_shape=jax.ShapeDtypeStruct((ENTRY * entries,), jnp.int32),
        scratch_shapes=[SMEM((3 * count_ka,), jnp.int32)],
        cost_estimate=pl.CostEstimate(flops=0, bytes_accessed=1 << 22, transcendentals=0),
        name="plan",
    )(later_order, doc_ids, tile_mask)
    table = jnp.maximum(table, -TILE)

    def attend(stage, outs, scratch, *operands):
        return pl.pallas_call(
            functools.partial(attention_kernel, (count_chip, count_ka, heads_dev, share, stage)),
            in_specs=in_smem(1) + in_vmem(len(operands)),
            out_specs=in_vmem(len(outs)),
            out_shape=outs,
            scratch_shapes=scratch + [
                VMEM((count_ka, head_rows(heads_dev), 2 * TILE), F32),
                VMEM((2 * TILE, width), BF16),
                VMEM((2 * TILE, width), BF16),
            ],
            compiler_params=params(14 + key_tiles * 11 // 16),
            cost_estimate=pl.CostEstimate(
                flops=5 * count_ka * key_tiles * TILE * TILE * width, bytes_accessed=1 << 20, transcendentals=0
            ),
            name=("attention_first", "attention_leaving", "attention_other", "attention_own")[stage],
        )(table, *operands)

    dq_sums = jax.ShapeDtypeStruct((count_ka, HEAD_DIM, width), F32)
    dq_tile = jax.ShapeDtypeStruct((HEAD_DIM, width), BF16)
    state = [key_shape] * 3 + [sum_shape] * 2
    dq_sum, *own = attend(0, [dq_sums] + state, [], key_gain, value_gain, own_queries, own_stats, *blocks)
    dq_sum, *other = attend(
        1, [dq_sums] + [jax.ShapeDtypeStruct((HEAD_DIM, width // 2), BF16)] * 2 + state, [],
        key_gain, value_gain, own_queries, own_stats, *other_blocks, dq_sum,
    )
    dq_parts = [None] * count_ka
    dq_halves, other = [turn(part, half) for part in other[:2]], other[2:]
    dq_sum, *own[3:], kv_other = attend(
        2,
        [dq_sums] + [sum_shape] * 2
        + [jax.ShapeDtypeStruct((key_tiles * TILE, 2 * HEAD_DIM), BF16)],
        [VMEM(sum_shape.shape, F32)] * 2,
        own_queries, own_stats, dq_sum, *own, *other,
    )
    kv_other, dq_halves[0] = lax.optimization_barrier((kv_other, dq_halves[0]))
    kv_back = swap(kv_other, 1)
    *dq_late, key_sum, value_sum = attend(
        3, [dq_tile] * len(late) + [sum_shape] * 2, [VMEM(dq_sums.shape, F32)],
        own_queries, own_stats, dq_sum, *own,
    )
    kv_own = pl.pallas_call(
        functools.partial(merge_kernel, (count_chip, count_ka)),
        in_specs=in_vmem(3 + count_chip),
        out_specs=in_vmem(count_chip),
        out_shape=[jax.ShapeDtypeStruct(kv_shape, BF16 if number else F32) for number in range(count_chip)],
        compiler_params=params(16 + key_tiles // 4),
        name="merge",
    )(key_sum, value_sum, kv_back, *blocks)
    kv_parts = [kv_own[0]] + [swap(kv_own[number], 2 * number) for number in range(1, count_chip)]
    dq_late, dq_halves[1] = lax.optimization_barrier((dq_late, dq_halves[1]))
    for step, tile in zip(late, dq_late):
        dq_parts[step] = turn(tile, step) if step else tile

    piece_type = BF16 if share == 1 else F32
    piece_shape = (TILE + SPARE, 2 * HEAD_DIM)
    pieces = list(pl.pallas_call(
        functools.partial(collect_kernel, (count_chip, count_ka, share)),
        in_specs=in_vmem(2 + count_chip),
        out_specs=in_vmem(count_ka),
        out_shape=[jax.ShapeDtypeStruct(piece_shape, piece_type if step else F32) for step in range(count_ka)],
        compiler_params=params(24),
        name="collect",
    )(key_gain, value_gain, *kv_parts))
    pieces = [pieces[0]] + [turn(piece, -step) for step, piece in enumerate(pieces[1:], 1)]
    where = ((half, 0), (half, heads_dev // 2)) + tuple((step, 0) for step in order[1:])
    grad_queries = pl.pallas_call(
        functools.partial(place_kernel, (count_ka, heads_dev, where)),
        in_specs=in_vmem(len(where)),
        out_specs=anywhere(1)[0],
        out_shape=jax.ShapeDtypeStruct((rows_dev, feat_width), BF16),
        scratch_shapes=[VMEM((count_ka, TILE, width), BF16), pltpu.SemaphoreType.DMA((len(where),))],
        compiler_params=params(16),
        cost_estimate=pl.CostEstimate(flops=0, bytes_accessed=4 * rows_dev * feat_width, transcendentals=0),
        name="place_queries",
    )(*dq_halves, *[dq_parts[step] for step in order[1:]])
    pieces, grad_queries = lax.optimization_barrier((pieces, grad_queries))
    grad_keys, grad_values, gains = pl.pallas_call(
        functools.partial(finish_kernel, (count_ka, share)),
        in_specs=in_vmem(2 + count_ka),
        out_specs=in_vmem(3),
        out_shape=[
            jax.ShapeDtypeStruct(key_rows.shape, BF16),
            jax.ShapeDtypeStruct(key_rows.shape, BF16),
            jax.ShapeDtypeStruct((2, key_rows.shape[1]), F32),
        ],
        scratch_shapes=[VMEM((kv_heads, TILE + SPARE, 2 * HEAD_DIM), F32)],
        compiler_params=params(16),
        name="finish",
    )(key_gain, value_gain, *pieces)
    grad_key_gain, grad_value_gain = pl.pallas_call(
        gains_kernel,
        in_specs=in_vmem(2),
        out_specs=in_vmem(2),
        out_shape=[jax.ShapeDtypeStruct(key_gain.shape, F32)] * 2,
        compiler_params=params(4),
        name="add_gains",
    )(gains, swap(gains, 1))
    return grad_queries, grad_keys, grad_values, grad_key_gain.reshape(-1), grad_value_gain.reshape(-1)


def solution(mesh):
    placed = (
        P("pb", None),
        P(("pb", "ka"), None),
        P(("pb", "ka"), None),
        P(("pb", "ka"), None),
        P("pb", None),
        P(None, ("pb", "ka")),
        P(),
        P(),
        P(),
        P(),
        P(),
    )
    return jax.shard_map(
        shards,
        mesh=mesh,
        in_specs=placed,
        out_specs=(P(("pb", "ka"), None), P(("pb", "ka"), None), P(("pb", "ka"), None), P(), P()),
        check_vma=False,
    )
```
